32 devices in a mesh: dp: 16 (over z, y, x), tensor: 2 (over core).
Axes of the slice: x: 2, y: 2, z: 4, core: 2. Of those that a mesh axis runs over, the one named last changes fastest.
Arguments:
- inputs: bfloat16 [32768, 768], P('dp'), may hold values from -6 to 6
- segments: int32 [32, 1024], P('dp'), may hold values from 0 to 7, never falling along the last dimension, each value on 1 to 512 neighbouring positions
- cotangent: bfloat16 [32768, 768], P('dp'), may hold values from -6 to 6
- weight_qkv: float32 [3, 768, 768], P(None, 'dp', 'tensor'), may hold values from -0.21875 to 0.21875
- first_qkv: float32 [3, 768, 768], P(None, 'dp', 'tensor'), may hold values from -64 to 64
- second_qkv: float32 [3, 768, 768], P(None, 'dp', 'tensor'), may hold values from 4.096 to 65.536
- weight_out: float32 [768, 768], P(('tensor', 'dp')), may hold values from -0.625 to 0.625
- first_out: float32 [768, 768], P(('tensor', 'dp')), may hold values from -24 to 24
- second_out: float32 [768, 768], P(('tensor', 'dp')), may hold values from 0.65536 to 10.48576
- weight_gate_up: float32 [2, 768, 3072], P(None, 'dp', 'tensor'), may hold values from -0.21875 to 0.21875
- first_gate_up: float32 [2, 768, 3072], P(None, 'dp', 'tensor'), may hold values from -24 to 24
- second_gate_up: float32 [2, 768, 3072], P(None, 'dp', 'tensor'), may hold values from 0.65536 to 10.48576
- weight_down: float32 [3072, 768], P(('tensor', 'dp')), may hold values from -0.109375 to 0.109375
- first_down: float32 [3072, 768], P(('tensor', 'dp')), may hold values from -56 to 56
- second_down: float32 [3072, 768], P(('tensor', 'dp')), may hold values from 3.2768 to 52.4288
- head_bias: float32 [2, 768], P(None, ('tensor', 'dp')), may hold values from -4 to 4
- first_head_bias: float32 [2, 768], P(None, ('tensor', 'dp')), may hold values from -64 to 64
- second_head_bias: float32 [2, 768], P(None, ('tensor', 'dp')), may hold values from 4.096 to 65.536
- norm_vectors: float32 [6, 768], P(None, 'dp'), may hold values from -1.5 to 1.75, as said below
- first_norm_vectors: float32 [6, 768], P(None, 'dp'), may hold values from -80 to 80
- second_norm_vectors: float32 [6, 768], P(None, 'dp'), may hold values from 8.192 to 131.072
Outputs:
- layer_out: bfloat16 [32768, 768], P('dp')
- input_grad: bfloat16 [32768, 768], P('dp')
- grad_qkv: float32 [3, 768, 768], P(None, 'dp', 'tensor')
- new_second_qkv: float32 [3, 768, 768], P(None, 'dp', 'tensor')
- new_weight_qkv: float32 [3, 768, 768], P(None, 'dp', 'tensor')
- grad_out: float32 [768, 768], P(('tensor', 'dp'))
- new_second_out: float32 [768, 768], P(('tensor', 'dp'))
- new_weight_out: float32 [768, 768], P(('tensor', 'dp'))
- grad_gate_up: float32 [2, 768, 3072], P(None, 'dp', 'tensor')
- new_second_gate_up: float32 [2, 768, 3072], P(None, 'dp', 'tensor')
- new_weight_gate_up: float32 [2, 768, 3072], P(None, 'dp', 'tensor')
- grad_down: float32 [3072, 768], P(('tensor', 'dp'))
- new_second_down: float32 [3072, 768], P(('tensor', 'dp'))
- new_weight_down: float32 [3072, 768], P(('tensor', 'dp'))
- grad_head_bias: float32 [2, 768], P(None, ('tensor', 'dp'))
- new_second_head_bias: float32 [2, 768], P(None, ('tensor', 'dp'))
- new_weight_head_bias: float32 [2, 768], P(None, ('tensor', 'dp'))
- grad_norm_vectors: float32 [6, 768], P(None, 'dp')
- new_second_norm_vectors: float32 [6, 768], P(None, 'dp')
- new_weight_norm_vectors: float32 [6, 768], P(None, 'dp')
The draws below stay inside these ranges and needn't reach their ends.
Inputs may be any that keep to these rules, and one draw needn't show every extreme that they name: `segments`: each row numbers the documents packed into one sequence from 0 upward, never falling; a document has 1 to 512 tokens. `norm_vectors`: rows 2 and 4 lie in 0.25 to 1.75, the other rows in -1.5 to 1.5.
All inputs are finite; a program needn't handle non-finite values.
Results may differ from the reference program's by a relative error of at most 0.025.
Values may be sent and summed in bfloat16 or wider, within the bound.
A program may use at most 192 MiB of HBM per device.

```python
import math
import jax
import jax.numpy as jnp
import numpy as np
from jax import lax

D = 768
HEADS = 12
HEAD_DIM = 64
FF = 3072
SEQ = 1024
SEG_COUNT = 8
STEP = 10
SEQS = 32
TOKENS = 32768
SEG_MOST = 512
N_TENSOR = 2


def draw_norm_vectors(key, part):
    key = jax.random.fold_in(key, 5)
    deviation = jnp.clip(jax.random.normal(key, (6, D), jnp.float32), -5.0, 5.0)
    row_index = jnp.arange(6)[:, None]
    gain_rows = (row_index == 2) | (row_index == 4)
    return jnp.where(gain_rows, 1.0 + 0.15 * deviation, 0.3 * deviation)


def block_scale(own_key, extent, cuts, smallest, largest):
    level = 1.0
    for axis_at, shards_of in cuts:
        draws = jax.random.uniform(jax.random.fold_in(jax.random.fold_in(own_key, 6), axis_at), (shards_of,), jnp.float32, smallest / len(cuts), largest / len(cuts))
        level = level * jnp.repeat(jnp.exp(draws), extent[axis_at] // shards_of).reshape((-1,) + (1,) * (len(extent) - 1 - axis_at))
    return level


def profile(amount, total, most, lean):
    portions = [(1 << 20) // math.isqrt(grade ** lean) + 1 for grade in range(2, amount + 1)]
    surplus, counts = total - most - (amount - 1), [1] * (amount - 1)
    while surplus > 0:
        movable = [i for i in range(amount - 1) if counts[i] < most]
        mass, budget = sum([portions[i] for i in movable]), surplus
        for i in movable:
            more = min(most - counts[i], max(1, budget * portions[i] // mass), surplus)
            counts[i] = counts[i] + more
            surplus = surplus - more
    return np.array([most] + counts)


def ragged_sizes(own_key, number_of, total, most, lean):
    if number_of == 2:
        one = jax.random.randint(own_key, (), max(1, total - most), min(most, total - 1) + 1)
        return jnp.stack([one, total - one])
    lengths = jnp.asarray(profile(number_of, total, most, lean), jnp.int32)
    couples = (number_of - 1) // 2
    source_of, taker = lengths[1:1 + 2 * couples:2], lengths[2:2 + 2 * couples:2]
    margin = jnp.minimum(source_of - 1, most - taker)
    shifted = jax.random.randint(jax.random.fold_in(own_key, 1), (couples,), 0, 1 << 20) % (margin + 1)
    lengths = lengths.at[1:1 + 2 * couples:2].set(source_of - shifted).at[2:2 + 2 * couples:2].set(taker + shifted)
    return lengths[jax.random.permutation(jax.random.fold_in(own_key, 2), number_of)]


def scatter_about(rng, dims, spread, limit, cuts=(), held_as=jnp.bfloat16):
    level = block_scale(rng, dims, cuts, -0.22, 0.18) if cuts else 1.0
    values = jax.random.normal(rng, dims, jnp.float32) * spread * level
    return jnp.minimum(jnp.maximum(values, -limit), limit).astype(held_as)


def setup_inputs(seed: int = 0) -> dict:
    arg_keys = jax.random.split(jax.random.key(seed), 22)
    inputs = scatter_about(arg_keys[0], (TOKENS, D), 1.0, 6.0, ((0, 16),))
    segments = jax.vmap(lambda own: jnp.searchsorted(jnp.cumsum(ragged_sizes(own, SEG_COUNT, SEQ, SEG_MOST, 2)), jnp.arange(SEQ), side="right"))(jax.random.split(arg_keys[1], SEQS)).reshape((SEQS, SEQ)).astype(jnp.int32)
    cotangent = scatter_about(arg_keys[2], (TOKENS, D), 1.0, 6.0, ((0, 16),))
    weight_qkv = scatter_about(arg_keys[3], (3, D, D), D ** -0.5, 0.21875, ((1, 16), (2, 2)), jnp.float32)
    first_qkv = scatter_about(arg_keys[4], (3, D, D), (0.055 * TOKENS ** 0.5), 64.0, ((1, 16), (2, 2)), jnp.float32)
    second_qkv = jnp.clip(jnp.exp(math.log(65.536) - 2.7725887 * jax.random.uniform(arg_keys[5], (3, D, D), jnp.float32) ** block_scale(arg_keys[5], (3, D, D), ((1, 16), (2, 2)), -0.2, 0.2)), 4.096, 65.536)
    weight_out = scatter_about(arg_keys[6], (D, D), (D // 8) ** -0.5, 0.625, ((0, 32),), jnp.float32)
    first_out = scatter_about(arg_keys[7], (D, D), (0.022 * TOKENS ** 0.5), 24.0, ((0, 32),), jnp.float32)
    second_out = jnp.clip(jnp.exp(math.log(10.48576) - 2.7725887 * jax.random.uniform(arg_keys[8], (D, D), jnp.float32) ** block_scale(arg_keys[8], (D, D), ((0, 32),), -0.2, 0.2)), 0.65536, 10.48576)
    weight_gate_up = scatter_about(arg_keys[9], (2, D, FF), D ** -0.5, 0.21875, ((1, 16), (2, 2)), jnp.float32)
    first_gate_up = scatter_about(arg_keys[10], (2, D, FF), (0.022 * TOKENS ** 0.5), 24.0, ((1, 16), (2, 2)), jnp.float32)
    second_gate_up = jnp.clip(jnp.exp(math.log(10.48576) - 2.7725887 * jax.random.uniform(arg_keys[11], (2, D, FF), jnp.float32) ** block_scale(arg_keys[11], (2, D, FF), ((1, 16), (2, 2)), -0.2, 0.2)), 0.65536, 10.48576)
    weight_down = scatter_about(arg_keys[12], (FF, D), FF ** -0.5, 0.109375, ((0, 32),), jnp.float32)
    first_down = scatter_about(arg_keys[13], (FF, D), (0.05 * TOKENS ** 0.5), 56.0, ((0, 32),), jnp.float32)
    second_down = jnp.clip(jnp.exp(math.log(52.4288) - 2.7725887 * jax.random.uniform(arg_keys[14], (FF, D), jnp.float32) ** block_scale(arg_keys[14], (FF, D), ((0, 32),), -0.2, 0.2)), 3.2768, 52.4288)
    head_bias = scatter_about(arg_keys[15], (2, D), 0.3, 4.0, ((1, 32),), jnp.float32)
    first_head_bias = scatter_about(arg_keys[16], (2, D), (0.055 * TOKENS ** 0.5), 64.0, ((1, 32),), jnp.float32)
    second_head_bias = jnp.clip(jnp.exp(math.log(65.536) - 2.7725887 * jax.random.uniform(arg_keys[17], (2, D), jnp.float32) ** block_scale(arg_keys[17], (2, D), ((1, 32),), -0.2, 0.2)), 4.096, 65.536)
    norm_vectors = draw_norm_vectors(jax.random.fold_in(arg_keys[21], 71), 0)
    first_norm_vectors = scatter_about(arg_keys[19], (6, D), (0.077 * TOKENS ** 0.5), 80.0, ((1, 16),), jnp.float32)
    second_norm_vectors = jnp.clip(jnp.exp(math.log(131.072) - 2.7725887 * jax.random.uniform(arg_keys[20], (6, D), jnp.float32) ** block_scale(arg_keys[20], (6, D), ((1, 16),), -0.2, 0.2)), 8.192, 131.072)
    return dict(inputs=inputs, segments=segments, cotangent=cotangent, weight_qkv=weight_qkv, first_qkv=first_qkv, second_qkv=second_qkv, weight_out=weight_out, first_out=first_out, second_out=second_out, weight_gate_up=weight_gate_up, first_gate_up=first_gate_up, second_gate_up=second_gate_up, weight_down=weight_down, first_down=first_down, second_down=second_down, head_bias=head_bias, first_head_bias=first_head_bias, second_head_bias=second_head_bias, norm_vectors=norm_vectors, first_norm_vectors=first_norm_vectors, second_norm_vectors=second_norm_vectors)


highest = lax.Precision.HIGHEST
norm_epsilon = 1e-12
beta_first = 0.9
beta_second = 0.999
adam_epsilon = 1e-08
decay_rate = 0.1
matrix_rate = 0.05
vector_rate = 0.5

@jax.custom_vjp
def low(v):
    return lax.optimization_barrier(v.astype(jnp.bfloat16)).astype(jnp.float32)

@jax.custom_vjp
def low_back(v):
    return v

def low_keep(v):
    return (low(v), None)

def low_pass(kept, grad):
    return (grad,)

def back_keep(v):
    return (v, None)

def back_low(kept, grad):
    return (low(grad),)
low.defvjp(low_keep, low_pass)
low_back.defvjp(back_keep, back_low)

def alibi_slopes(head_total):
    power_two = 2 ** int(math.floor(math.log2(head_total)))
    leading = [2.0 ** (-8.0 * (h + 1) / power_two) for h in range(power_two)]
    trailing = [2.0 ** (-8.0 * (2 * h + 1) / (2 * power_two)) for h in range(head_total - power_two)]
    return np.array(leading + trailing, dtype=np.float32)

def product(left, right):
    return jnp.dot(left, right, precision=highest, preferred_element_type=jnp.float32)

def layer_norm(values, gain, shift):
    centred = values - lax.optimization_barrier(jnp.mean(values, axis=-1, keepdims=True))
    variance = lax.optimization_barrier(jnp.mean(centred * centred, axis=-1, keepdims=True))
    return centred * lax.rsqrt(variance + norm_epsilon) * gain + shift

def geglu(gate, upper):
    return jax.nn.gelu(gate, approximate=False) * upper

def attention(query, keys, values_in, segments, slopes, head_count):
    block_rows = min(SEQ, 512)
    block_count = SEQ // block_rows
    score_scale = HEAD_DIM ** (-0.5)
    query_seq = query.reshape(SEQS, SEQ, head_count, HEAD_DIM)
    keys_seq = keys.reshape(SEQS, SEQ, head_count, HEAD_DIM)
    values_seq = values_in.reshape(SEQS, SEQ, head_count, HEAD_DIM)

    def one_sequence(packed):
        q_seq, k_seq, v_seq, seg_seq = packed

        def one_block(row_start):
            q_rows = lax.dynamic_slice_in_dim(q_seq, row_start, block_rows, 0)
            seg_rows = lax.dynamic_slice_in_dim(seg_seq, row_start, block_rows, 0)
            raw = jnp.einsum('qhd,khd->hqk', q_rows, k_seq, precision=highest)
            row_pos = row_start + jnp.arange(block_rows, dtype=jnp.int32)
            key_pos = jnp.arange(SEQ, dtype=jnp.int32)
            distance = jnp.abs(row_pos[:, None] - key_pos[None, :]).astype(jnp.float32)
            scores = low_back(raw * score_scale - slopes[:, None, None] * distance[None])
            allowed = seg_rows[:, None] == seg_seq[None, :]
            masked = jnp.where(allowed[None], scores, -1000000000.0)
            row_max = lax.optimization_barrier(jnp.max(masked, axis=-1, keepdims=True))
            exp_scores = jnp.exp(masked - row_max)
            row_total = lax.optimization_barrier(jnp.sum(exp_scores, axis=-1, keepdims=True))
            probs = low(exp_scores / row_total)
            return jnp.einsum('hqk,khd->qhd', probs, v_seq, precision=highest)
        starts = jnp.arange(block_count, dtype=jnp.int32) * block_rows
        context = lax.map(jax.checkpoint(one_block), starts)
        return context.reshape(SEQ, head_count * HEAD_DIM)
    context = lax.map(one_sequence, (query_seq, keys_seq, values_seq, segments))
    return context.reshape(TOKENS, head_count * HEAD_DIM)

def forward(inputs, weight_qkv, weight_out, weight_gate_up, weight_down, head_bias, norm_vectors, segments):
    proj_qkv = low(weight_qkv)
    proj_out = low(weight_out)
    proj_gate_up = low(weight_gate_up)
    proj_down = low(weight_down)
    bias_heads = low(head_bias)
    vectors = low(norm_vectors)
    group_width = D // N_TENSOR
    hidden_width = FF // N_TENSOR
    head_count = HEADS // N_TENSOR
    all_slopes = jnp.asarray(alibi_slopes(HEADS), dtype=jnp.float32)
    input_low = low(inputs)
    attn_parts = jnp.zeros((TOKENS, D), jnp.float32)
    for group_index in range(N_TENSOR):
        col_start = group_index * group_width
        col_end = col_start + group_width
        x_group = low_back(input_low)
        query = product(x_group, proj_qkv[0][:, col_start:col_end]) + bias_heads[0][col_start:col_end]
        keys = product(x_group, proj_qkv[1][:, col_start:col_end])
        values_in = product(x_group, proj_qkv[2][:, col_start:col_end]) + bias_heads[1][col_start:col_end]
        query = low_back(low(query))
        keys = low_back(low(keys))
        values_in = low_back(low(values_in))
        slopes = all_slopes[group_index * head_count:(group_index + 1) * head_count]
        context = attention(query, keys, values_in, segments, slopes, head_count)
        context = low_back(low(context))
        attn_parts = attn_parts + low(product(context, proj_out[col_start:col_end, :]))
    attention_out = low_back(attn_parts) + vectors[0]
    normed = layer_norm(inputs + attention_out, vectors[2], vectors[3])
    normed_low = low(normed)
    ffn_parts = jnp.zeros((TOKENS, D), jnp.float32)
    for group_index in range(N_TENSOR):
        col_start = group_index * hidden_width
        col_end = col_start + hidden_width
        x_group = low_back(normed_low)
        gate = low_back(product(x_group, proj_gate_up[0][:, col_start:col_end]))
        upper = low_back(product(x_group, proj_gate_up[1][:, col_start:col_end]))
        hidden = low(geglu(gate, upper))
        ffn_parts = ffn_parts + low(product(hidden, proj_down[col_start:col_end, :]))
    ffn_out = low_back(ffn_parts) + vectors[1]
    return layer_norm(normed + ffn_out, vectors[4], vectors[5])

def adam_update(weight_old, first_old, second_old, gradient, step_rate):
    first_new = beta_first * first_old + (1.0 - beta_first) * gradient
    second_new = beta_second * second_old + (1.0 - beta_second) * gradient * gradient
    first_hat = first_new / (1.0 - beta_first ** STEP)
    second_hat = second_new / (1.0 - beta_second ** STEP)
    weight_new = weight_old - step_rate * (first_hat / (jnp.sqrt(second_hat) + adam_epsilon) + decay_rate * weight_old)
    return (second_new, weight_new)

def reference(inputs, segments, cotangent, weight_qkv, first_qkv, second_qkv, weight_out, first_out, second_out, weight_gate_up, first_gate_up, second_gate_up, weight_down, first_down, second_down, head_bias, first_head_bias, second_head_bias, norm_vectors, first_norm_vectors, second_norm_vectors):

    def run(inputs_f, p_qkv, p_out, p_gate_up, p_down, p_heads, p_vectors):
        return forward(inputs_f, p_qkv, p_out, p_gate_up, p_down, p_heads, p_vectors, segments)
    result, pullback = jax.vjp(run, inputs.astype(jnp.float32), weight_qkv, weight_out, weight_gate_up, weight_down, head_bias, norm_vectors)
    d_inputs, grad_qkv, grad_out, grad_gate_up, grad_down, grad_heads, grad_vectors = pullback(cotangent.astype(jnp.float32))
    second_qkv_new, weight_qkv_new = adam_update(weight_qkv, first_qkv, second_qkv, grad_qkv, matrix_rate)
    second_out_new, weight_out_new = adam_update(weight_out, first_out, second_out, grad_out, matrix_rate)
    second_gu_new, weight_gu_new = adam_update(weight_gate_up, first_gate_up, second_gate_up, grad_gate_up, matrix_rate)
    second_down_new, weight_down_new = adam_update(weight_down, first_down, second_down, grad_down, matrix_rate)
    second_heads_new, weight_heads_new = adam_update(head_bias, first_head_bias, second_head_bias, grad_heads, vector_rate)
    second_vectors_new, weight_vectors_new = adam_update(norm_vectors, first_norm_vectors, second_norm_vectors, grad_vectors, vector_rate)
    return (result.astype(jnp.bfloat16), d_inputs.astype(jnp.bfloat16), grad_qkv, second_qkv_new, weight_qkv_new, grad_out, second_out_new, weight_out_new, grad_gate_up, second_gu_new, weight_gu_new, grad_down, second_down_new, weight_down_new, grad_heads, second_heads_new, weight_heads_new, grad_vectors, second_vectors_new, weight_vectors_new)
```

```python
import math

import jax
import jax.numpy as jnp
import numpy as np
from jax import lax
from jax.experimental import pallas as pl
from jax.experimental.pallas import tpu as pltpu
from jax.sharding import PartitionSpec as P

MESH = pl.DeviceIdType.MESH
TORUS = (4, 2, 2)

HEADS = 12
HEAD_DIM = 64
SEQ = 1024
STEP = 10


norm_epsilon = 1e-12
beta_first = 0.9
beta_second = 0.999
adam_epsilon = 1e-08
decay_rate = 0.1
matrix_rate = 0.05
vector_rate = 0.5


def alibi_slopes(head_total):
    power_two = 2 ** int(math.floor(math.log2(head_total)))
    leading = [2.0 ** (-8.0 * (h + 1) / power_two) for h in range(power_two)]
    trailing = [
        2.0 ** (-8.0 * (2 * h + 1) / (2 * power_two)) for h in range(head_total - power_two)
    ]
    return np.array(leading + trailing, dtype=np.float32)


def layer_norm(values, gain, shift):
    centred = values - jnp.mean(values, axis=-1, keepdims=True)
    variance = jnp.mean(centred * centred, axis=-1, keepdims=True)
    return centred * lax.rsqrt(variance + norm_epsilon) * gain + shift


def geglu(gate_up):
    return jax.nn.gelu(gate_up[0], approximate=False) * gate_up[1]


def block_scores(q_rows, k_seq, seg_rows, seg_seq, row_start, slopes):
    block_rows = q_rows.shape[0]
    raw = jnp.einsum("qhd,khd->hqk", q_rows, k_seq, preferred_element_type=jnp.float32)
    row_pos = row_start + jnp.arange(block_rows, dtype=jnp.int32)
    key_pos = jnp.arange(SEQ, dtype=jnp.int32)
    distance = jnp.abs(row_pos[:, None] - key_pos[None, :]).astype(jnp.float32)
    scores = raw * HEAD_DIM ** (-0.5) - slopes[:, None, None] * distance[None]
    allowed = seg_rows[:, None] == seg_seq[None, :]
    return (jnp.where(allowed[None], scores, -1000000000.0), allowed)


def attend_forward(query, keys, values_in, segments, slopes):
    block_rows = min(SEQ, 512)
    block_count = SEQ // block_rows
    head_count = query.shape[2]

    def one_sequence(packed):
        q_seq, k_seq, v_seq, seg_seq = packed

        def one_block(row_start):
            q_rows = lax.dynamic_slice_in_dim(q_seq, row_start, block_rows, 0)
            seg_rows = lax.dynamic_slice_in_dim(seg_seq, row_start, block_rows, 0)
            masked, allowed = block_scores(q_rows, k_seq, seg_rows, seg_seq, row_start, slopes)
            row_max = jnp.max(masked, axis=-1, keepdims=True)
            exp_scores = jnp.exp(masked - row_max)
            row_total = jnp.sum(exp_scores, axis=-1, keepdims=True)
            weights_low = (exp_scores / row_total).astype(jnp.bfloat16)
            context = jnp.einsum(
                "hqk,khd->qhd", weights_low, v_seq, preferred_element_type=jnp.float32
            )
            return (context.astype(jnp.bfloat16), (row_max + jnp.log(row_total))[..., 0])

        starts = jnp.arange(block_count, dtype=jnp.int32) * block_rows
        context, log_total = lax.map(one_block, starts)
        return (context.reshape(SEQ, head_count, HEAD_DIM), log_total)

    return lax.map(one_sequence, (query, keys, values_in, segments))


def attend_backward(query, keys, values_in, segments, d_context, log_total, slopes):
    block_rows = min(SEQ, 512)
    block_count = SEQ // block_rows
    head_count = query.shape[2]
    score_scale = HEAD_DIM ** (-0.5)

    def one_sequence(packed):
        q_seq, k_seq, v_seq, seg_seq, dctx_seq, total_seq = packed
        q_blocks = q_seq.reshape(block_count, block_rows, head_count, HEAD_DIM)
        dctx_blocks = dctx_seq.reshape(block_count, block_rows, head_count, HEAD_DIM)

        def one_block(carry, items):
            d_keys, d_values = carry
            q_rows, dctx_rows, total_rows, block_index = items
            row_start = block_index * block_rows
            seg_rows = lax.dynamic_slice_in_dim(seg_seq, row_start, block_rows, 0)
            masked, allowed = block_scores(q_rows, k_seq, seg_rows, seg_seq, row_start, slopes)
            probs = jnp.where(allowed[None], jnp.exp(masked - total_rows[..., None]), 0.0)
            d_values = d_values + jnp.einsum(
                "hqk,qhd->khd",
                probs.astype(jnp.bfloat16),
                dctx_rows,
                preferred_element_type=jnp.float32,
            )
            d_probs = jnp.einsum(
                "qhd,khd->hqk", dctx_rows, v_seq, preferred_element_type=jnp.float32
            )
            delta = jnp.sum(probs * d_probs, axis=-1, keepdims=True)
            d_scores = (probs * (d_probs - delta)).astype(jnp.bfloat16)
            d_query = (
                jnp.einsum("hqk,khd->qhd", d_scores, k_seq, preferred_element_type=jnp.float32)
                * score_scale
            )
            d_keys = (
                d_keys
                + jnp.einsum("hqk,qhd->khd", d_scores, q_rows, preferred_element_type=jnp.float32)
                * score_scale
            )
            return ((d_keys, d_values), d_query)

        zeros_seq = jnp.zeros((SEQ, head_count, HEAD_DIM), jnp.float32)
        block_ids = jnp.arange(block_count, dtype=jnp.int32)
        (d_keys, d_values), d_query = lax.scan(
            one_block, (zeros_seq, zeros_seq), (q_blocks, dctx_blocks, total_seq, block_ids)
        )
        return (d_query.reshape(SEQ, head_count, HEAD_DIM), d_keys, d_values)

    return lax.map(one_sequence, (query, keys, values_in, segments, d_context, log_total))


def adam_update(weight_old, first_old, second_old, gradient, step_rate):
    first_new = beta_first * first_old + (1.0 - beta_first) * gradient
    second_new = beta_second * second_old + (1.0 - beta_second) * gradient * gradient
    first_hat = first_new / (1.0 - beta_first**STEP)
    second_hat = second_new / (1.0 - beta_second**STEP)
    weight_new = weight_old - step_rate * (
        first_hat / (jnp.sqrt(second_hat) + adam_epsilon) + decay_rate * weight_old
    )
    return (second_new, weight_new)


def place():
    me = lax.axis_index("dp")
    return lax.div(me, 4), lax.rem(lax.div(me, 2), 2), lax.rem(me, 2)

def rdma(src, dst, ssem, rsem, dev):
    return pltpu.make_async_remote_copy(src_ref=src, dst_ref=dst, send_sem=ssem, recv_sem=rsem, device_id={"dp": dev}, device_id_type=MESH)

class Gather:
    def s0(self): self.start_z()
    def s1(self): self.wait_z(); self.start_p(0)
    def s2(self): self.wait_p(0); self.start_p(1)
    def s3(self): self.wait_p(1)

    def __init__(self, src, dst, first, ssem, rsem, lsem):
        self.src, self.dst, self.first, self.ssem, self.rsem, self.lsem = src, dst, first, ssem, rsem, lsem
        self.z, self.y, self.x = place()
    def zcopy(self, d):
        z, y, x = self.z, self.y, self.x
        zt = lax.rem(z + d, 4); zs = lax.rem(z + 4 - d, 4)
        c = rdma(self.src, self.dst(z, y, x), self.ssem.at[d - 1], self.rsem.at[d - 1], zt * 4 + y * 2 + x)
        r = rdma(self.src, self.dst(zs, y, x), self.ssem.at[d - 1], self.rsem.at[d - 1], zs * 4 + y * 2 + x)
        return c, r
    def start_z(self):
        pltpu.make_async_copy(self.src, self.dst(self.z, self.y, self.x), self.lsem).start()
        for d in (1, 3, 2):
            self.zcopy(d)[0].start()
    def wait_z(self):
        pltpu.make_async_copy(self.src, self.dst(self.z, self.y, self.x), self.lsem).wait()
        for d in (1, 3, 2):
            c, r = self.zcopy(d); c.wait_send(); r.wait_recv()
    def plane(self, k):
        z, y, x = self.z, self.y, self.x
        al = slice(None)
        if self.first == 'x':
            if k == 0:
                mine, theirs, dev = self.dst(al, y, x), self.dst(al, y, 1 - x), z * 4 + y * 2 + 1 - x
            else:
                mine, theirs, dev = self.dst(al, y, al), self.dst(al, 1 - y, al), z * 4 + (1 - y) * 2 + x
        else:
            if k == 0:
                mine, theirs, dev = self.dst(al, y, x), self.dst(al, 1 - y, x), z * 4 + (1 - y) * 2 + x
            else:
                mine, theirs, dev = self.dst(al, al, x), self.dst(al, al, 1 - x), z * 4 + y * 2 + 1 - x
        c = rdma(mine, mine, self.ssem.at[3 + k], self.rsem.at[3 + k], dev)
        r = rdma(theirs, theirs, self.ssem.at[3 + k], self.rsem.at[3 + k], dev)
        return c, r
    def start_p(self, k):
        self.plane(k)[0].start()
    def wait_p(self, k):
        c, r = self.plane(k); c.wait_send(); r.wait_recv()

def enter():
    z, y, x = place()
    peers = [lax.rem(z + d, 4) * 4 + y * 2 + x for d in (1, 2, 3)] + [z * 4 + (1 - y) * 2 + x, z * 4 + y * 2 + 1 - x]
    b = pltpu.get_barrier_semaphore()
    for p in peers:
        pl.semaphore_signal(b, inc=1, device_id={"dp": p}, device_id_type=MESH)
    pl.semaphore_wait(b, 5)

class Scatter:
    def __init__(self, g, r1, r2, r3, out, first, ssem, rsem):
        self.g, self.r1, self.r2, self.r3, self.out, self.first, self.ssem, self.rsem = g, r1, r2, r3, out, first, ssem, rsem
        z, y, x = self.z, self.y, self.x = place()
        if first == 'y':
            self.sel = lambda zz, a, b: g(zz, a, b)
            self.a, self.b = y, x
            self.d1, self.d2 = z * 4 + (1 - y) * 2 + x, z * 4 + y * 2 + 1 - x
        else:
            self.sel = lambda zz, a, b: g(zz, b, a)
            self.a, self.b = x, y
            self.d1, self.d2 = z * 4 + y * 2 + 1 - x, z * 4 + (1 - y) * 2 + x
    def c1(self):
        al = slice(None)
        return rdma(self.sel(al, 1 - self.a, al), self.r1, self.ssem.at[0], self.rsem.at[0], self.d1)
    def c2(self):
        return rdma(self.r1.at[:, 1 - self.b], self.r2, self.ssem.at[1], self.rsem.at[1], self.d2)
    def c3(self, d):
        zt = lax.rem(self.z + d, 4)
        return rdma(self.r2.at[zt], self.r3.at[d - 1], self.ssem.at[1 + d], self.rsem.at[1 + d], zt * 4 + self.y * 2 + self.x)
    def s0(self):
        self.c1().start()
    def s1(self):
        self.c1().wait()
        o = 1 - self.b
        def add(zz, _):
            t = self.r1.at[zz, o]
            t[...] = (t[...].astype(jnp.float32) + self.sel(zz, self.a, o)[...].astype(jnp.float32)).astype(t.dtype)
            return 0
        lax.fori_loop(0, 4, add, 0)
        self.c2().start()
    def s2(self):
        self.c2().wait()
        def add(d, _):
            zz = lax.rem(self.z + d, 4)
            t = self.r2.at[zz]
            t[...] = (t[...].astype(jnp.float32) + self.r1[zz, self.b].astype(jnp.float32) + self.sel(zz, self.a, self.b)[...].astype(jnp.float32)).astype(t.dtype)
            return 0
        lax.fori_loop(1, 4, add, 0)
        for d in (2, 1, 3): self.c3(d).start()
    def s3(self):
        for d in (2, 1, 3): self.c3(d).wait()
        f = lambda v: v.astype(jnp.float32)
        z = self.z
        self.out[...] = f(self.sel(z, self.a, self.b)[...]) + f(self.r1[z, self.b]) + f(self.r2[z]) + f(self.r3[0]) + f(self.r3[1]) + f(self.r3[2])


def pipeline(groups, stages):
    n = len(groups)
    for s in range(n + stages - 1):
        for k in range(stages):
            if 0 <= s - k < n:
                for flow in groups[s - k]:
                    getattr(flow, f"s{k}")()


def cuts_of(i, rows):
    if i in (1, 5):
        return [(0, rows, "x")]
    if i == 2:
        return [(0, rows, "y")]
    return [(0, rows // 32 * 16, "x"), (rows // 32 * 16, rows, "y")]


def gather_kernel(*refs):
    n = 6
    src, dst = refs[:n], refs[n : 2 * n]
    ssem, rsem, lsem = refs[2 * n :]
    enter()
    fl = []
    for i, (s, d) in enumerate(zip(src, dst)):
        for a, b, first in cuts_of(i, s.shape[0]):
            j = len(fl)
            fl.append(
                Gather(
                    s.at[a:b],
                    lambda z, y, x, d=d, a=a, b=b: d.at[z, y, x, a:b],
                    first,
                    ssem.at[j],
                    rsem.at[j],
                    lsem.at[j],
                )
            )
    pipeline([[fl[0], fl[1], fl[8]], [fl[6], fl[7]], [fl[2], fl[3]], [fl[4], fl[5]]], 4)


def gather_call(shards_low):
    n = len(shards_low)
    return pl.pallas_call(
        gather_kernel,
        out_shape=[jax.ShapeDtypeStruct(TORUS + s.shape, s.dtype) for s in shards_low],
        in_specs=[pl.BlockSpec(memory_space=pltpu.VMEM)] * n,
        out_specs=[pl.BlockSpec(memory_space=pl.ANY)] * n,
        scratch_shapes=[
            pltpu.SemaphoreType.DMA((9, 5)),
            pltpu.SemaphoreType.DMA((9, 5)),
            pltpu.SemaphoreType.DMA((9,)),
        ],
        compiler_params=pltpu.CompilerParams(
            collective_id=0, has_side_effects=True, vmem_limit_bytes=60 << 20
        ),
    )(*shards_low)


def scatter_kernel(*refs):
    n = 6
    g, out, r1, r2, r3 = (refs[k * n : (k + 1) * n] for k in range(5))
    ssem, rsem = refs[5 * n :]
    enter()
    fl = []
    for i in range(n):
        for a, b, first in cuts_of(i, out[i].shape[0]):
            j = len(fl)
            fl.append(
                Scatter(
                    lambda z, y, x, i=i, a=a, b=b: g[i].at[z, y, x, a:b],
                    r1[i].at[:, :, a:b],
                    r2[i].at[:, a:b],
                    r3[i].at[:, a:b],
                    out[i].at[a:b],
                    first,
                    ssem.at[j],
                    rsem.at[j],
                )
            )
    pipeline([[fl[2], fl[3]], [fl[4], fl[5]], [fl[0], fl[1]], [fl[6], fl[7], fl[8]]], 4)


def scatter_call(parts):
    n = len(parts)
    vmem = pl.BlockSpec(memory_space=pltpu.VMEM)
    return pl.pallas_call(
        scatter_kernel,
        out_shape=[jax.ShapeDtypeStruct(v.shape[3:], jnp.float32) for v in parts],
        in_specs=[vmem] * n,
        out_specs=[vmem] * n,
        scratch_shapes=[pltpu.VMEM((4, 2) + v.shape[3:], v.dtype) for v in parts]
        + [pltpu.VMEM((4,) + v.shape[3:], v.dtype) for v in parts]
        + [pltpu.VMEM((3,) + v.shape[3:], v.dtype) for v in parts]
        + [pltpu.SemaphoreType.DMA((9, 5)), pltpu.SemaphoreType.DMA((9, 5))],
        compiler_params=pltpu.CompilerParams(
            collective_id=1, has_side_effects=True, vmem_limit_bytes=60 << 20
        ),
    )(*parts)


def gather_weights(weight_qkv, weight_out, weight_gate_up, weight_down, head_bias, norm_vectors):
    n = lax.axis_size("dp")
    low = lambda v: v.astype(jnp.bfloat16)
    if n != TORUS[0] * TORUS[1] * TORUS[2]:
        return (
            lax.all_gather(low(weight_qkv), "dp", axis=1, tiled=True),
            lax.all_gather(low(weight_out), "dp", axis=0, tiled=True),
            lax.all_gather(low(weight_gate_up), "dp", axis=1, tiled=True),
            lax.all_gather(low(weight_down), "dp", axis=0, tiled=True),
            lax.all_gather(low(head_bias), "dp", axis=1, tiled=True),
            lax.all_gather(low(norm_vectors), "dp", axis=1, tiled=True),
        )
    me = lax.axis_index("dp")
    width = weight_qkv.shape[2]
    model = weight_out.shape[1]
    rows_out = weight_out.shape[0]
    qkv = low(weight_qkv).reshape(-1, width)
    out = jnp.pad(low(weight_out), ((0, -rows_out % 32), (0, 0)))
    small = jnp.zeros((16, model), jnp.bfloat16)
    small = lax.dynamic_update_slice(small, low(norm_vectors), (0, me * norm_vectors.shape[1]))
    small = lax.dynamic_update_slice(small, low(head_bias), (8, me * head_bias.shape[1]))
    qkv, gate, up, down, out, small = gather_call(
        [qkv, low(weight_gate_up[0]), low(weight_gate_up[1]), low(weight_down), out, small]
    )
    small = jnp.sum(small.reshape(n, 16, model).astype(jnp.float32), axis=0)
    qkv = qkv.reshape(n, 3, -1, width).transpose(1, 0, 2, 3).reshape(3, model, width)
    return (
        qkv,
        out.reshape(n, -1, model)[:, :rows_out].reshape(-1, model),
        jnp.stack([gate.reshape(model, -1), up.reshape(model, -1)]),
        down.reshape(-1, model),
        small[8:10, :width],
        small[:6],
    )


def reduce_grads(grad_qkv, grad_out, grad_gate_up, grad_down, grad_heads, grad_vectors):
    n = lax.axis_size("dp")
    low = lambda v: v.astype(jnp.bfloat16)
    if n != TORUS[0] * TORUS[1] * TORUS[2]:
        return (
            lax.psum_scatter(grad_qkv, "dp", scatter_dimension=1, tiled=True),
            lax.psum_scatter(grad_out, "dp", scatter_dimension=0, tiled=True),
            lax.psum_scatter(grad_gate_up, "dp", scatter_dimension=1, tiled=True),
            lax.psum_scatter(grad_down, "dp", scatter_dimension=0, tiled=True),
            lax.psum_scatter(grad_heads, "dp", scatter_dimension=1, tiled=True),
            lax.psum_scatter(grad_vectors, "dp", scatter_dimension=1, tiled=True),
        )
    model, width = grad_qkv.shape[1:]
    rows = model // n
    rows_out, rows_heads = grad_out.shape[0] // n, grad_heads.shape[1] // n
    blocks = lambda v: v.reshape(TORUS + (-1, v.shape[-1]))
    qkv = blocks(low(grad_qkv).reshape(3, n, rows, width).transpose(1, 0, 2, 3))
    out = low(grad_out).reshape(n, rows_out, model)
    out = blocks(jnp.pad(out, ((0, 0), (0, -rows_out % 32), (0, 0))))
    vec = grad_vectors.reshape(6, n, rows).transpose(1, 0, 2)
    heads = grad_heads.reshape(2, n, rows_heads).transpose(1, 0, 2)
    vec = jnp.pad(vec, ((0, 0), (0, 2), (0, 128 - rows)))
    heads = jnp.pad(heads, ((0, 0), (6, 0), (0, 128 - rows_heads)))
    qkv, gate, up, down, out, small = scatter_call(
        [
            qkv,
            blocks(low(grad_gate_up[0])),
            blocks(low(grad_gate_up[1])),
            blocks(low(grad_down)),
            out,
            blocks(vec + heads),
        ]
    )
    return (
        qkv.reshape(3, rows, width),
        out[:rows_out],
        jnp.stack([gate, up]),
        down,
        small[6:8, :rows_heads],
        small[:6, :rows],
    )


def shards(
    inputs,
    segments,
    cotangent,
    weight_qkv,
    first_qkv,
    second_qkv,
    weight_out,
    first_out,
    second_out,
    weight_gate_up,
    first_gate_up,
    second_gate_up,
    weight_down,
    first_down,
    second_down,
    head_bias,
    first_head_bias,
    second_head_bias,
    norm_vectors,
    first_norm_vectors,
    second_norm_vectors,
):
    head_count = HEADS // lax.axis_size("tensor")
    all_slopes = jnp.asarray(alibi_slopes(HEADS))
    slopes = lax.dynamic_slice_in_dim(all_slopes, lax.axis_index("tensor") * head_count, head_count)
    proj_qkv, proj_out, proj_gate_up, proj_down, bias_heads, vectors = gather_weights(
        weight_qkv, weight_out, weight_gate_up, weight_down, head_bias, norm_vectors
    )
    bias_heads = bias_heads.astype(jnp.float32)
    vectors = vectors.astype(jnp.float32)
    token_rows = inputs.shape[0]
    seq_count = segments.shape[0]
    group_width = proj_out.shape[0]
    qkv_sum = jnp.einsum("td,cdw->ctw", inputs, proj_qkv, preferred_element_type=jnp.float32)
    qkv_bias = jnp.stack([bias_heads[0], jnp.zeros_like(bias_heads[0]), bias_heads[1]])
    qkv_low = (qkv_sum + qkv_bias[:, None, :]).astype(jnp.bfloat16)
    shaped = qkv_low.reshape(3, seq_count, SEQ, head_count, HEAD_DIM)
    context, log_total = attend_forward(shaped[0], shaped[1], shaped[2], segments, slopes)
    context_low = context.reshape(token_rows, group_width)
    attn_part = jnp.dot(context_low, proj_out, preferred_element_type=jnp.float32)
    attention_out = (
        lax.psum(attn_part.astype(jnp.bfloat16), "tensor").astype(jnp.float32) + vectors[0]
    )
    normed, norm_back_one = jax.vjp(
        layer_norm, inputs.astype(jnp.float32) + attention_out, vectors[2], vectors[3]
    )
    normed_low = normed.astype(jnp.bfloat16)
    gate_up = jnp.einsum(
        "td,cdf->ctf", normed_low, proj_gate_up, preferred_element_type=jnp.float32
    )
    hidden, geglu_back = jax.vjp(geglu, gate_up)
    hidden_low = hidden.astype(jnp.bfloat16)
    ffn_part = jnp.dot(hidden_low, proj_down, preferred_element_type=jnp.float32)
    ffn_out = lax.psum(ffn_part.astype(jnp.bfloat16), "tensor").astype(jnp.float32) + vectors[1]
    result, norm_back_two = jax.vjp(layer_norm, normed + ffn_out, vectors[4], vectors[5])
    layer_out = result.astype(jnp.bfloat16)
    d_second, d_gain_two, d_shift_two = norm_back_two(cotangent.astype(jnp.float32))
    d_ffn_low = d_second.astype(jnp.bfloat16)
    grad_down = jnp.einsum("tf,td->fd", hidden_low, d_ffn_low, preferred_element_type=jnp.float32)
    d_hidden = jnp.einsum("td,fd->tf", d_ffn_low, proj_down, preferred_element_type=jnp.float32)
    (d_gate_up,) = geglu_back(d_hidden)
    d_gate_up_low = d_gate_up.astype(jnp.bfloat16)
    grad_gate_up = jnp.einsum(
        "td,ctf->cdf", normed_low, d_gate_up_low, preferred_element_type=jnp.float32
    )
    back_part = jnp.einsum(
        "ctf,cdf->td", d_gate_up_low, proj_gate_up, preferred_element_type=jnp.float32
    )
    d_normed = d_second + lax.psum(back_part.astype(jnp.bfloat16), "tensor").astype(jnp.float32)
    d_first, d_gain_one, d_shift_one = norm_back_one(d_normed)
    d_attn_low = d_first.astype(jnp.bfloat16)
    grad_out = jnp.einsum("tw,td->wd", context_low, d_attn_low, preferred_element_type=jnp.float32)
    d_context = jnp.einsum(
        "td,wd->tw", d_attn_low, proj_out, preferred_element_type=jnp.float32
    ).astype(jnp.bfloat16)
    d_query, d_keys, d_values = attend_backward(
        shaped[0],
        shaped[1],
        shaped[2],
        segments,
        d_context.reshape(seq_count, SEQ, head_count, HEAD_DIM),
        log_total,
        slopes,
    )
    d_qkv_low = (
        jnp.stack([d_query, d_keys, d_values])
        .reshape(3, token_rows, group_width)
        .astype(jnp.bfloat16)
    )
    grad_qkv = jnp.einsum("td,ctw->cdw", inputs, d_qkv_low, preferred_element_type=jnp.float32)
    grad_heads = jnp.stack(
        [
            jnp.sum(d_qkv_low[0], axis=0, dtype=jnp.float32),
            jnp.sum(d_qkv_low[2], axis=0, dtype=jnp.float32),
        ]
    )
    input_part = jnp.einsum("ctw,cdw->td", d_qkv_low, proj_qkv, preferred_element_type=jnp.float32)
    input_grad = (
        d_first + lax.psum(input_part.astype(jnp.bfloat16), "tensor").astype(jnp.float32)
    ).astype(jnp.bfloat16)
    grad_vectors = jnp.stack(
        [
            jnp.sum(d_first, axis=0),
            jnp.sum(d_second, axis=0),
            d_gain_one,
            d_shift_one,
            d_gain_two,
            d_shift_two,
        ]
    )
    grad_qkv, grad_out, grad_gate_up, grad_down, grad_heads, grad_vectors = reduce_grads(
        grad_qkv, grad_out, grad_gate_up, grad_down, grad_heads, grad_vectors
    )
    second_qkv_new, weight_qkv_new = adam_update(
        weight_qkv, first_qkv, second_qkv, grad_qkv, matrix_rate
    )
    second_out_new, weight_out_new = adam_update(
        weight_out, first_out, second_out, grad_out, matrix_rate
    )
    second_gu_new, weight_gu_new = adam_update(
        weight_gate_up, first_gate_up, second_gate_up, grad_gate_up, matrix_rate
    )
    second_down_new, weight_down_new = adam_update(
        weight_down, first_down, second_down, grad_down, matrix_rate
    )
    second_heads_new, weight_heads_new = adam_update(
        head_bias, first_head_bias, second_head_bias, grad_heads, vector_rate
    )
    second_vectors_new, weight_vectors_new = adam_update(
        norm_vectors, first_norm_vectors, second_norm_vectors, grad_vectors, vector_rate
    )
    return (
        layer_out,
        input_grad,
        grad_qkv,
        second_qkv_new,
        weight_qkv_new,
        grad_out,
        second_out_new,
        weight_out_new,
        grad_gate_up,
        second_gu_new,
        weight_gu_new,
        grad_down,
        second_down_new,
        weight_down_new,
        grad_heads,
        second_heads_new,
        weight_heads_new,
        grad_vectors,
        second_vectors_new,
        weight_vectors_new,
    )


def solution(mesh):
    in_specs = (
        P("dp", None),
        P("dp", None),
        P("dp", None),
        P(None, "dp", "tensor"),
        P(None, "dp", "tensor"),
        P(None, "dp", "tensor"),
        P(("tensor", "dp"), None),
        P(("tensor", "dp"), None),
        P(("tensor", "dp"), None),
        P(None, "dp", "tensor"),
        P(None, "dp", "tensor"),
        P(None, "dp", "tensor"),
        P(("tensor", "dp"), None),
        P(("tensor", "dp"), None),
        P(("tensor", "dp"), None),
        P(None, ("tensor", "dp")),
        P(None, ("tensor", "dp")),
        P(None, ("tensor", "dp")),
        P(None, "dp"),
        P(None, "dp"),
        P(None, "dp"),
    )
    out_specs = (
        P("dp", None),
        P("dp", None),
        P(None, "dp", "tensor"),
        P(None, "dp", "tensor"),
        P(None, "dp", "tensor"),
        P(("tensor", "dp"), None),
        P(("tensor", "dp"), None),
        P(("tensor", "dp"), None),
        P(None, "dp", "tensor"),
        P(None, "dp", "tensor"),
        P(None, "dp", "tensor"),
        P(("tensor", "dp"), None),
        P(("tensor", "dp"), None),
        P(("tensor", "dp"), None),
        P(None, ("tensor", "dp")),
        P(None, ("tensor", "dp")),
        P(None, ("tensor", "dp")),
        P(None, "dp"),
        P(None, "dp"),
        P(None, "dp"),
    )
    return jax.shard_map(shards, mesh=mesh, in_specs=in_specs, out_specs=out_specs, check_vma=False)
```

```python
import functools
import math

import jax
import jax.numpy as jnp
import numpy as np
from jax import lax
from jax.experimental import pallas as pl
from jax.experimental.pallas import tpu as pltpu
from jax.sharding import PartitionSpec as P

HEADS = 12
HEAD_DIM = 64
SEQ = 1024
STEP = 10

norm_epsilon = 1e-12
beta_first = 0.9
beta_second = 0.999
adam_epsilon = 1e-08
decay_rate = 0.1
matrix_rate = 0.05
vector_rate = 0.5

MESH = pl.DeviceIdType.MESH
TORUS = (4, 2, 2)
f32, bf16 = jnp.float32, jnp.bfloat16
LOG2E = 1.4426950408889634
FAR = 3e12
REACH = 512
BQ = 256
TM = 256
HC = 512
VMEM = pl.BlockSpec(memory_space=pltpu.VMEM)
SMEM = pl.BlockSpec(memory_space=pltpu.SMEM)
ANY = pl.BlockSpec(memory_space=pl.ANY)


def alibi_slopes(head_total):
    power_two = 2 ** int(math.floor(math.log2(head_total)))
    leading = [2.0 ** (-8.0 * (h + 1) / power_two) for h in range(power_two)]
    trailing = [
        2.0 ** (-8.0 * (2 * h + 1) / (2 * power_two)) for h in range(head_total - power_two)
    ]
    return np.array(leading + trailing, dtype=np.float32)


def place():
    me = lax.axis_index("dp")
    return lax.div(me, 4), lax.rem(lax.div(me, 2), 2), lax.rem(me, 2)


def chip(z, y, x):
    return z * 4 + y * 2 + x


def remote(src, dst, ssem, rsem, dp):
    return pltpu.make_async_remote_copy(
        src_ref=src,
        dst_ref=dst,
        send_sem=ssem,
        recv_sem=rsem,
        device_id={"dp": dp},
        device_id_type=MESH,
    )


def swap(src, dst, ssem, rsem):
    return pltpu.make_async_remote_copy(
        src_ref=src,
        dst_ref=dst,
        send_sem=ssem,
        recv_sem=rsem,
        device_id={"tensor": 1 - lax.axis_index("tensor")},
        device_id_type=MESH,
    )


def greet(chips, core):
    barrier = pltpu.get_barrier_semaphore()
    count = 0
    if chips:
        z, y, x = place()
        peers = [chip(lax.rem(z + d, 4), y, x) for d in (1, 2, 3)]
        for dp in peers + [chip(z, 1 - y, x), chip(z, y, 1 - x)]:
            pl.semaphore_signal(barrier, inc=1, device_id={"dp": dp}, device_id_type=MESH)
            count += 1
    if core:
        other = {"tensor": 1 - lax.axis_index("tensor")}
        pl.semaphore_signal(barrier, inc=1, device_id=other, device_id_type=MESH)
        count += 1
    pl.semaphore_wait(barrier, count)


class Gather:
    def __init__(self, src, dst, first, ssem, rsem, lsem):
        self.src, self.dst, self.first = src, dst, first
        self.ssem, self.rsem, self.lsem = ssem, rsem, lsem
        self.z, self.y, self.x = place()

    def own(self):
        return pltpu.make_async_copy(self.src, self.dst(self.z, self.y, self.x), self.lsem)

    def along_z(self, d, arriving):
        z, y, x = self.z, self.y, self.x
        other = lax.rem(z + (4 - d if arriving else d), 4)
        slot = self.dst(other if arriving else z, y, x)
        return remote(self.src, slot, self.ssem.at[d - 1], self.rsem.at[d - 1], chip(other, y, x))

    def plane(self, k, arriving):
        z, y, x = self.z, self.y, self.x
        whole = slice(None)
        on_x = (self.first == "x") == (k == 0)
        dp = chip(z, y, 1 - x) if on_x else chip(z, 1 - y, x)
        yy, xx = y, x
        if arriving:
            yy, xx = (y, 1 - x) if on_x else (1 - y, x)
        if k == 1:
            yy, xx = (whole, xx) if on_x else (yy, whole)
        part = self.dst(whole, yy, xx)
        return remote(part, part, self.ssem.at[3 + k], self.rsem.at[3 + k], dp)

    def s0(self):
        self.own().start()
        for d in (1, 3, 2):
            self.along_z(d, False).start()

    def s1(self):
        self.own().wait()
        for d in (1, 3, 2):
            self.along_z(d, False).wait_send()
            self.along_z(d, True).wait_recv()
        self.plane(0, False).start()

    def s2(self):
        self.plane(0, False).wait_send()
        self.plane(0, True).wait_recv()
        self.plane(1, False).start()

    def s3(self):
        self.plane(1, False).wait_send()
        self.plane(1, True).wait_recv()


class Scatter:
    def __init__(self, g, r1, r2, r3, out, first, ssem, rsem):
        self.r1, self.r2, self.r3, self.out, self.ssem, self.rsem = r1, r2, r3, out, ssem, rsem
        z, y, x = self.z, self.y, self.x = place()
        on_y, on_x = chip(z, 1 - y, x), chip(z, y, 1 - x)
        if first == "y":
            self.block = lambda zz, a, b: g(zz, a, b)
            self.a, self.b, self.to1, self.to2 = y, x, on_y, on_x
        else:
            self.block = lambda zz, a, b: g(zz, b, a)
            self.a, self.b, self.to1, self.to2 = x, y, on_x, on_y

    def c1(self):
        whole = slice(None)
        src = self.block(whole, 1 - self.a, whole)
        return remote(src, self.r1, self.ssem.at[0], self.rsem.at[0], self.to1)

    def c2(self):
        src = self.r1.at[:, 1 - self.b]
        return remote(src, self.r2, self.ssem.at[1], self.rsem.at[1], self.to2)

    def c3(self, d):
        to = lax.rem(self.z + d, 4)
        dp = chip(to, self.y, self.x)
        return remote(
            self.r2.at[to], self.r3.at[d - 1], self.ssem.at[1 + d], self.rsem.at[1 + d], dp
        )

    def s0(self):
        self.c1().start()

    def s1(self):
        self.c1().wait()
        o = 1 - self.b

        def add(zz, carry):
            t = self.r1.at[zz, o]
            t[...] = (t[...].astype(f32) + self.block(zz, self.a, o)[...].astype(f32)).astype(t.dtype)
            return carry

        lax.fori_loop(0, 4, add, 0)
        self.c2().start()

    def s2(self):
        self.c2().wait()

        def add(d, carry):
            zz = lax.rem(self.z + d, 4)
            t = self.r2.at[zz]
            here = self.r1[zz, self.b].astype(f32) + self.block(zz, self.a, self.b)[...].astype(f32)
            t[...] = (t[...].astype(f32) + here).astype(t.dtype)
            return carry

        lax.fori_loop(1, 4, add, 0)
        for d in (2, 1, 3):
            self.c3(d).start()

    def s3(self):
        for d in (2, 1, 3):
            self.c3(d).wait()
        z = self.z
        total = self.block(z, self.a, self.b)[...].astype(f32) + self.r1[z, self.b].astype(f32)
        total = total + self.r2[z].astype(f32)
        for d in range(3):
            total = total + self.r3[d].astype(f32)
        self.out[...] = total


def run(flows, stage):
    for flow in flows:
        getattr(flow, f"s{stage}")()


def halves(rows):
    return ((0, rows // 32 * 16, "x"), (rows // 32 * 16, rows, "y"))


def routed():
    return lax.axis_size("dp") == TORUS[0] * TORUS[1] * TORUS[2]


def nt(a, b):
    return lax.dot_general(a, b, (((1,), (1,)), ((), ())), preferred_element_type=f32)


def nn(a, b):
    return jnp.dot(a, b, preferred_element_type=f32)


def span(b, seq):
    lo = max(0, (b * BQ - REACH + 1) // BQ * BQ)
    hi = min(seq, -(-(b * BQ + BQ - 1 + REACH) // BQ) * BQ)
    return lo, hi


def fill_far(far_ref, seg_col, seg_row, seq):
    def rows(c, carry):
        o = pl.multiple_of(c * 128, 128)
        r = lax.broadcasted_iota(jnp.int32, (128, seq), 0) + o
        k = lax.broadcasted_iota(jnp.int32, (128, seq), 1)
        d = jnp.abs(r - k).astype(f32)
        far_ref[pl.ds(o, 128), :] = jnp.where(seg_col[pl.ds(o, 128), :] == seg_row, d, FAR)
        return carry

    lax.fori_loop(0, seq // 128, rows, 0)


def half(value, which):
    lane = lax.broadcasted_iota(jnp.int32, value.shape, 1)
    keep = (lane < 64) if which == 0 else (lane >= 64)
    return jnp.where(keep, value, jnp.zeros_like(value))


def attend_pair(s, pair, q_ref, k_ref, v_ref, vt_ref, far_ref, slope_ref, ctx_ref, lse_ref, seq, pairs):
    cols = pl.ds(pl.multiple_of(pair * 128, 128), 128)
    base = s * seq
    at = lambda lo, n: pl.ds(pl.multiple_of(base + lo, 128), n)
    vt_ref[...] = v_ref[at(0, seq), cols].T
    slopes = [slope_ref[2 * pair + h] for h in range(2)]
    for b in range(seq // BQ):
        lo, hi = span(b, seq)
        qb = q_ref[at(b * BQ, BQ), cols] * jnp.asarray(HEAD_DIM**-0.5, bf16)
        kb = k_ref[at(lo, hi - lo), cols]
        far = lambda: far_ref[lo:hi, b * BQ : (b + 1) * BQ]
        score = [nt(kb, half(qb, h)) * LOG2E - slopes[h] * far() for h in range(2)]
        top = [jnp.max(t, axis=0, keepdims=True) for t in score]
        weight = [jnp.exp2(t - m) for t, m in zip(score, top)]
        total = [jnp.sum(e, axis=0, keepdims=True) for e in weight]
        out = [
            nn(vt_ref[64 * h : 64 * h + 64, lo:hi], weight[h].astype(bf16)) * (1.0 / total[h])
            for h in range(2)
        ]
        for h in range(2):
            lse_ref[s * pairs + pair, h : h + 1, b * BQ : (b + 1) * BQ] = top[h] + jnp.log2(total[h])
        ctx_ref[at(b * BQ, BQ), cols] = jnp.concatenate(out, axis=0).T.astype(bf16)


def attend_pair_back(
    s, pair, q_ref, k_ref, v_ref, ctx_ref, dctx_ref, lse_ref, far_ref, slope_ref,
    kt_ref, dk_acc, dv_acc, dq_ref, dk_ref, dv_ref, seq, pairs,
):
    cols = pl.ds(pl.multiple_of(pair * 128, 128), 128)
    base = s * seq
    at = lambda lo, n: pl.ds(pl.multiple_of(base + lo, 128), n)
    kt_ref[...] = k_ref[at(0, seq), cols].T
    slopes = [slope_ref[2 * pair + h] for h in range(2)]
    dk_acc[...] = jnp.zeros_like(dk_acc)
    dv_acc[...] = jnp.zeros_like(dv_acc)
    for b in range(seq // BQ):
        lo, hi = span(b, seq)
        qb = q_ref[at(b * BQ, BQ), cols] * jnp.asarray(HEAD_DIM**-0.5, bf16)
        db = dctx_ref[at(b * BQ, BQ), cols]
        prod = (db.astype(f32) * ctx_ref[at(b * BQ, BQ), cols].astype(f32)).T
        out = []
        for h in range(2):
            qh, dh = half(qb, h), half(db, h)
            delta = jnp.sum(prod[64 * h : 64 * h + 64], axis=0, keepdims=True)
            lse = lse_ref[s * pairs + pair, h : h + 1, b * BQ : (b + 1) * BQ]
            score = nt(k_ref[at(lo, hi - lo), cols], qh) * LOG2E
            p = jnp.exp2(score - slopes[h] * far_ref[lo:hi, b * BQ : (b + 1) * BQ] - lse)
            ds = (p * (nt(v_ref[at(lo, hi - lo), cols], dh) - delta)).astype(bf16)
            dv_acc[lo:hi, :] += nn(p.astype(bf16), dh)
            dk_acc[lo:hi, :] += nn(ds, qh)
            out.append(nn(kt_ref[64 * h : 64 * h + 64, lo:hi], ds))
        dq = jnp.concatenate(out, axis=0).T * HEAD_DIM**-0.5
        dq_ref[at(b * BQ, BQ), cols] = dq.astype(bf16)
    dk_ref[at(0, seq), cols] = dk_acc[...].astype(bf16)
    dv_ref[at(0, seq), cols] = dv_acc[...].astype(bf16)


def front_kernel(*refs, seq, pairs, routes):
    n = 4 if routes else 0
    x_ref, segc_ref, segr_ref, slope_ref, qkv_in, small_in = refs[:6]
    sources, refs = refs[6 : 6 + n], refs[6 + n :]
    q_ref, k_ref, v_ref, ctx_ref, lse_ref, small_ref = refs[:6]
    outs, refs = refs[6 : 6 + n], refs[6 + n :]
    if routes:
        w_out, refs = refs[0], refs[1:]
    far_ref, vt_ref = refs[:2]
    rows, width = x_ref.shape[0], q_ref.shape[1]
    model = x_ref.shape[1]
    if routes:
        w_ref, sm_ref, ssem, rsem, lsem, w_sem = refs[2:]
        greet(True, False)
        flows = []

        def flow(src, dst, cuts):
            made = []
            for a, b, first in cuts:
                j = len(flows)
                slot = lambda z, y, x, a=a, b=b: dst.at[z, y, x, a:b]
                made.append(Gather(src.at[a:b], slot, first, ssem.at[j], rsem.at[j], lsem.at[j]))
                flows.append(made[-1])
            return made

        whole = lambda s, first: ((0, s.shape[0], first),)
        gate, up, down, out = sources
        lead = flow(qkv_in, w_ref, halves(qkv_in.shape[0])) + flow(small_in, sm_ref, whole(small_in, "x"))
        second = flow(down, outs[2], halves(down.shape[0])) + flow(out, outs[3], halves(out.shape[0]))
        third = flow(gate, outs[0], whole(gate, "x")) + flow(up, outs[1], whole(up, "y"))
        run(lead, 0)
        run(lead, 1)
        run(second, 0)
        run(lead, 2)
        run(lead, 3)
        run(second, 1)
        run(third, 0)
        keep = pltpu.make_async_copy(w_ref, w_out, w_sem)
        keep.start()
        blocks = TORUS[0] * TORUS[1] * TORUS[2]
        load_w = lambda a, b: w_ref[:, :, :, a:b, :]
        small = sum(
            sm_ref[z, y, x].astype(f32)
            for z in range(TORUS[0])
            for y in range(TORUS[1])
            for x in range(TORUS[2])
        )
    else:
        blocks = 1
        load_w = lambda a, b: qkv_in[:, a:b, :]
        small = small_in[0].astype(f32)
    small_ref[...] = small
    each = model // blocks

    def project(i, carry):
        at = pl.ds(pl.multiple_of(i * TM, TM), TM)
        xb = x_ref[at, :]
        for j, (ref, bias) in enumerate(((q_ref, 8), (k_ref, None), (v_ref, 9))):
            val = nn(xb, load_w(j * each, (j + 1) * each).reshape(model, width))
            if bias is not None:
                val = val + small[bias : bias + 1, :width]
            ref[at, :] = val.astype(bf16)
        return carry

    lax.fori_loop(0, rows // TM, project, 0)
    total = segr_ref.shape[0] * pairs

    def step(it, carry):
        s, pair = lax.div(it, pairs), lax.rem(it, pairs)

        @pl.when(pair == 0)
        def _():
            fill_far(far_ref, segc_ref.at[s], segr_ref[s], seq)

        attend_pair(
            s, pair, q_ref, k_ref, v_ref, vt_ref, far_ref, slope_ref, ctx_ref, lse_ref, seq, pairs
        )
        if routes:

            @pl.when(it == 0)
            def _():
                run(second, 2)

            @pl.when(it == total - 2)
            def _():
                run(third, 1)

        return carry

    lax.fori_loop(0, total, step, 0)
    if routes:
        run(second, 3)
        run(third, 2)
        run(third, 3)
        keep.wait()


def front(x, segments, slopes, qkv, small, sources):
    routes = routed()
    rows, width = x.shape[0], qkv.shape[-1]
    count, seq = segments.shape
    pairs = width // 128
    low = lambda *s: jax.ShapeDtypeStruct(s, bf16)
    full = lambda *s: jax.ShapeDtypeStruct(s, f32)
    outs = [low(rows, width)] * 4 + [full(count * pairs, 8, seq), full(*small.shape[-2:])]
    scratch = [pltpu.VMEM((seq, seq), f32), pltpu.VMEM((128, seq), bf16)]
    params = pltpu.CompilerParams(vmem_limit_bytes=56 << 20)
    if routes:
        outs += [low(*TORUS, *s.shape) for s in [*sources, qkv]]
        scratch += [pltpu.VMEM(TORUS + qkv.shape, bf16), pltpu.VMEM(TORUS + small.shape, bf16)]
        dma = pltpu.SemaphoreType.DMA
        scratch += [dma((9, 5)), dma((9, 5)), dma((9,)), dma]
        params = pltpu.CompilerParams(
            vmem_limit_bytes=56 << 20, collective_id=0, has_side_effects=True
        )
    return pl.pallas_call(
        functools.partial(front_kernel, seq=seq, pairs=pairs, routes=routes),
        out_shape=outs,
        in_specs=[VMEM, VMEM, VMEM, SMEM, VMEM, VMEM] + [VMEM] * len(sources),
        out_specs=[VMEM] * 6 + [ANY] * (len(outs) - 6),
        scratch_shapes=scratch,
        compiler_params=params,
        name="front",
    )(x, segments[..., None], segments[:, None, :], slopes * LOG2E, qkv, small, *sources)


def stats(h):
    mean = jnp.mean(h, axis=-1, keepdims=True)
    c = h - mean
    r = lax.rsqrt(jnp.mean(c * c, axis=-1, keepdims=True) + norm_epsilon)
    return c * r, r

def norm_back(e, n, r):
    return r * (e - jnp.mean(e, axis=-1, keepdims=True) - n * jnp.mean(e * n, axis=-1, keepdims=True))

def mid_kernel(ctx_ref, wo_in, wg_ref, wu_ref, wd_ref, vec_ref, x_hbm, cot_hbm,
               out_hbm, dattn_hbm, dctx_ref, dwg_hbm, dwu_hbm, dwd_hbm, dwo_ref, dvec_ref,
               wo_ref, io, s1, q1, s2, q2, n1, rr, xt, ht, av, bv, wide, tall,
               io_sem, out_sem, dat_sem, ssem, rsem, wsem, *, tiles, ff):
    n_blk, wide_rows, model = wo_in.shape
    each = ctx_ref.shape[1] // n_blk
    wo_ref[...] = wo_in[:, :each].astype(f32).reshape(n_blk * each, model).astype(bf16)
    bo, bd, g1, c1, g2, c2 = (vec_ref[k:k + 1, :] for k in range(6))
    at = lambda i: pl.ds(pl.multiple_of(i * TM, TM), TM)
    load = lambda hbm, i: pltpu.make_async_copy(hbm.at[at(i)], io.at[at(i)], io_sem.at[i])
    exch = lambda k, i: swap((s1, s2, s1)[k].at[at(i)], (q1, q2, q1)[k].at[at(i)], ssem.at[k, i], rsem.at[k, i])

    def pre(i, _):
        load(x_hbm, i).start()
        return 0
    lax.fori_loop(0, tiles, pre, 0)
    dvec_ref[...] = jnp.zeros_like(dvec_ref)
    greet(False, True)

    def phase_a(i, _):
        s1[at(i), :] = nn(ctx_ref[at(i), :], wo_ref[...]).astype(bf16)
        exch(0, i).start()
        return 0
    lax.fori_loop(0, tiles, phase_a, 0)

    def phase_b(i, _):
        exch(0, i).wait()
        load(x_hbm, i).wait()
        attn = s1[at(i), :].astype(f32) + q1[at(i), :].astype(f32) + bo
        n, r = stats(io[at(i), :].astype(f32) + attn)
        load(cot_hbm, i).start()
        n1[at(i), :] = n
        rr[at(i), :] = r
        xb = (n * g1 + c1).astype(bf16)
        xt[:, at(i)] = xb.T
        part = None
        for c in range(0, ff, HC):
            gate = nn(xb, wg_ref[:, c:c + HC])
            up = nn(xb, wu_ref[:, c:c + HC])
            cdf = 0.5 * (1.0 + lax.erf(gate * 0.7071067811865476))
            gel = gate * cdf
            slope = cdf + gate * (jnp.exp(gate * gate * -0.5) * 0.3989422804014327)
            hid = (gel * up).astype(bf16)
            ht[c:c + HC, at(i)] = hid.T
            av[at(i), c:c + HC] = (up * slope).astype(bf16)
            bv[at(i), c:c + HC] = gel.astype(bf16)
            p = nn(hid, wd_ref[c:c + HC, :])
            part = p if part is None else part + p
        s2[at(i), :] = part.astype(bf16)
        exch(1, i).start()
        return 0
    lax.fori_loop(0, tiles, phase_b, 0)

    def phase_c(i, _):
        exch(1, i).wait()
        load(cot_hbm, i).wait()
        ffn = s2[at(i), :].astype(f32) + q2[at(i), :].astype(f32) + bd
        n2, r2 = stats(n1[at(i), :] * g1 + c1 + ffn)
        dy = io[at(i), :].astype(f32)
        io[at(i), :] = (n2 * g2 + c2).astype(bf16)
        pltpu.make_async_copy(io.at[at(i)], out_hbm.at[at(i)], out_sem.at[i]).start()
        dvec_ref[4:5, :] += jnp.sum(dy * n2, axis=0, keepdims=True)
        dvec_ref[5:6, :] += jnp.sum(dy, axis=0, keepdims=True)
        dh2 = norm_back(dy * g2, n2, r2)
        dvec_ref[1:2, :] += jnp.sum(dh2, axis=0, keepdims=True)
        df = dh2.astype(bf16)
        s2[at(i), :] = df
        part = None
        for c in range(0, ff, HC):
            dh = nt(df, wd_ref[c:c + HC, :])
            dg = (dh * av[at(i), c:c + HC].astype(f32)).astype(bf16)
            du = (dh * bv[at(i), c:c + HC].astype(f32)).astype(bf16)
            av[at(i), c:c + HC] = dg
            bv[at(i), c:c + HC] = du
            p = nt(dg, wg_ref[:, c:c + HC]) + nt(du, wu_ref[:, c:c + HC])
            part = p if part is None else part + p
        s1[at(i), :] = part.astype(bf16)
        exch(2, i).start()
        return 0
    lax.fori_loop(0, tiles, phase_c, 0)

    def grad_block(left, right, buf, hbm, sem, c, slot, before):
        cols = pl.ds(pl.multiple_of(c * 256, 256), 256)
        val = nn(left[...], right[:, cols]).astype(bf16)
        cp = pltpu.make_async_copy(buf.at[slot], hbm.at[:, cols], sem.at[slot])
        @pl.when(before)
        def _():
            cp.wait()
        buf[slot] = val
        cp.start()
    def e_down(c, _):
        grad_block(ht, s2, tall, dwd_hbm, wsem.at[0], c, lax.rem(c, 2), c >= 2)
        return 0
    nd = s2.shape[1] // 256
    lax.fori_loop(0, nd, e_down, 0)
    def e_gate(c, _):
        grad_block(xt, av, wide, dwg_hbm, wsem.at[1], c, 0, c >= 1)
        grad_block(xt, bv, wide, dwu_hbm, wsem.at[1], c, 1, c >= 1)
        return 0
    nf = ff // 256
    lax.fori_loop(0, nf, e_gate, 0)

    def phase_d(i, _):
        exch(2, i).wait()
        n, r = n1[at(i), :], rr[at(i), :]
        dx1 = s2[at(i), :].astype(f32) + s1[at(i), :].astype(f32) + q1[at(i), :].astype(f32)
        dvec_ref[2:3, :] += jnp.sum(dx1 * n, axis=0, keepdims=True)
        dvec_ref[3:4, :] += jnp.sum(dx1, axis=0, keepdims=True)
        dh1 = norm_back(dx1 * g1, n, r)
        dvec_ref[0:1, :] += jnp.sum(dh1, axis=0, keepdims=True)
        da = dh1.astype(bf16)
        pltpu.make_async_copy(io.at[at(i)], out_hbm.at[at(i)], out_sem.at[i]).wait()
        io[at(i), :] = da
        pltpu.make_async_copy(io.at[at(i)], dattn_hbm.at[at(i)], dat_sem.at[i]).start()
        dctx_ref[at(i), :] = nt(da, wo_ref[...]).astype(bf16)
        return 0
    lax.fori_loop(0, tiles, phase_d, 0)
    dwo = nn(ctx_ref[...].T, io[...])
    dwo_ref[...] = jnp.zeros_like(dwo_ref)
    for b in range(n_blk):
        dwo_ref[b, :each, :] = dwo[b * each : (b + 1) * each].astype(bf16)
    def fin(i, _):
        pltpu.make_async_copy(io.at[at(i)], dattn_hbm.at[at(i)], dat_sem.at[i]).wait()
        return 0
    lax.fori_loop(0, tiles, fin, 0)
    for slot in range(min(2, nd)):
        pltpu.make_async_copy(tall.at[slot], dwd_hbm.at[:, 0:256], wsem.at[0, slot]).wait()
    pltpu.make_async_copy(wide.at[0], dwg_hbm.at[:, 0:256], wsem.at[1, 0]).wait()
    pltpu.make_async_copy(wide.at[1], dwu_hbm.at[:, 0:256], wsem.at[1, 1]).wait()

def middle(ctx, wo, wg, wu, wd, vec, x, cot):
    T, W = ctx.shape
    D, ff, tiles = x.shape[1], wg.shape[1], T // TM
    n_blk, pad = wo.shape[:2]
    sd = lambda *s: jax.ShapeDtypeStruct(s, bf16)
    return pl.pallas_call(functools.partial(mid_kernel, tiles=tiles, ff=ff),
        out_shape=[sd(T, D), sd(T, D), sd(T, W), sd(D, ff), sd(D, ff), sd(ff, D), sd(n_blk, pad, D), jax.ShapeDtypeStruct((8, D), f32)],
        in_specs=[VMEM, VMEM, VMEM, VMEM, VMEM, VMEM, ANY, ANY],
        out_specs=[ANY, ANY, VMEM, ANY, ANY, ANY, VMEM, VMEM],
        scratch_shapes=[pltpu.VMEM((W, D), bf16)] + [pltpu.VMEM((T, D), bf16)] * 5 + [pltpu.VMEM((T, D), f32), pltpu.VMEM((T, 1), f32), pltpu.VMEM((D, T), bf16), pltpu.VMEM((ff, T), bf16), pltpu.VMEM((T, ff), bf16), pltpu.VMEM((T, ff), bf16),
            pltpu.VMEM((2, D, 256), bf16), pltpu.VMEM((2, ff, 256), bf16)]
            + [pltpu.SemaphoreType.DMA((tiles,))] * 3 + [pltpu.SemaphoreType.DMA((3, tiles))] * 2 + [pltpu.SemaphoreType.DMA((2, 2))],
        compiler_params=pltpu.CompilerParams(collective_id=2, has_side_effects=True, vmem_limit_bytes=64 << 20), name="middle")(ctx, wo, wg, wu, wd, vec, x, cot)


def back_kernel(*refs, seq, pairs, routes):
    q_ref, k_ref, v_ref, ctx_ref, dctx_ref, lse_ref, segc_ref, segr_ref, slope_ref = refs[:9]
    x_ref, dh1_ref, w_ref, vec_ref = refs[9:13]
    refs = refs[13:]
    n = 4 if routes else 0
    grads, refs = refs[:n], refs[n:]
    dx_ref = refs[0]
    outs, refs = refs[1 : 1 + n + 2], refs[1 + n + 2 :]
    far_ref, kt_ref, dk_acc, dv_acc, dq_ref, dk_ref, dv_ref, xt, s, r, dx_sem, core_s, core_r = refs[:13]
    refs = refs[13:]
    rows, model = x_ref.shape
    width = q_ref.shape[1]
    tiles = rows // TM
    at = lambda i: pl.ds(pl.multiple_of(i * TM, TM), TM)
    if routes:
        gq, gs, ssem, rsem = refs[:4]
        bufs = refs[4:]
        blocks = TORUS[0] * TORUS[1] * TORUS[2]
        flows = []

        def flow(i, g, cuts):
            r1, r2, r3 = bufs[3 * i : 3 * i + 3]
            made = []
            for a, b, first in cuts:
                j = len(flows)
                flows.append(
                    Scatter(
                        lambda z, y, x, a=a, b=b: g.at[z, y, x, a:b],
                        r1.at[:, :, a:b],
                        r2.at[:, a:b],
                        r3.at[:, a:b],
                        outs[i].at[a:b],
                        first,
                        ssem.at[j],
                        rsem.at[j],
                    )
                )
                made.append(flows[-1])
            return made

        whole = lambda g, first: ((0, g.shape[3], first),)
        split = lambda g: halves(g.shape[3])
        first = flow(0, grads[0], whole(grads[0], "x")) + flow(1, grads[1], whole(grads[1], "y"))
        second = flow(2, grads[2], split(grads[2])) + flow(3, grads[3], split(grads[3]))
        third = flow(4, gq, split(gq)) + flow(5, gs, whole(gs, "x"))
    else:
        blocks = 1
    greet(routes, True)
    if routes:
        run(first, 0)
    total = segr_ref.shape[0] * pairs

    def step(it, carry):
        seq_at, pair = lax.div(it, pairs), lax.rem(it, pairs)

        @pl.when(pair == 0)
        def _():
            fill_far(far_ref, segc_ref.at[seq_at], segr_ref[seq_at], seq)

        attend_pair_back(
            seq_at, pair, q_ref, k_ref, v_ref, ctx_ref, dctx_ref, lse_ref, far_ref, slope_ref,
            kt_ref, dk_acc, dv_acc, dq_ref, dk_ref, dv_ref, seq, pairs,
        )
        if routes:

            @pl.when(it == 2)
            def _():
                run(second, 0)

            @pl.when(it == total - 2)
            def _():
                run(first, 1)

        return carry

    lax.fori_loop(0, total, step, 0)
    each = model // blocks
    if routes:
        load_w = lambda j: w_ref[:, :, :, j * each : (j + 1) * each, :].reshape(model, width)
    else:
        load_w = lambda j: w_ref[:, j * each : (j + 1) * each, :].reshape(model, width)
    d_refs = (dq_ref, dk_ref, dv_ref)
    exch = lambda i: swap(s.at[at(i)], r.at[at(i)], core_s.at[i], core_r.at[i])

    def part(i, carry):
        val = sum(nt(d[at(i), :], load_w(j)) for j, d in enumerate(d_refs))
        s[at(i), :] = val.astype(bf16)
        exch(i).start()
        xt[:, at(i)] = x_ref[at(i), :].T
        return carry

    lax.fori_loop(0, tiles, part, 0)
    heads = [jnp.sum(d[...].astype(f32), axis=0, keepdims=True) for d in (dq_ref, dv_ref)]
    heads = jnp.concatenate([jnp.zeros((6, width), f32)] + heads, axis=0)
    for j, d in enumerate(d_refs):
        val = nn(xt[...], d[...]).astype(bf16)
        for b in range(blocks):
            piece = val[b * each : (b + 1) * each]
            if routes:
                gq[b // 4, (b // 2) % 2, b % 2, j * each : (j + 1) * each, :] = piece
            else:
                outs[0][b, j * each : (j + 1) * each, :] = piece
    if routes:
        share = width // blocks
        row = lax.broadcasted_iota(jnp.int32, (8, 128), 0)
        for b in range(blocks):
            upper = pltpu.roll(vec_ref[...], (model - b * each) % model, 1)[:, :128]
            lower = pltpu.roll(heads, (width - b * share) % width, 1)[:, :128]
            gs[b // 4, (b // 2) % 2, b % 2] = jnp.where(row < 6, upper, lower)
        run(third, 0)
        run(second, 1)
    else:
        outs[1][...] = heads

    def finish(i, carry):
        exch(i).wait()
        val = dh1_ref[at(i), :].astype(f32) + (s[at(i), :].astype(f32) + r[at(i), :].astype(f32))
        s[at(i), :] = val.astype(bf16)
        pltpu.make_async_copy(s.at[at(i)], dx_ref.at[at(i)], dx_sem.at[i]).start()
        return carry

    lax.fori_loop(0, tiles, finish, 0)
    if routes:
        run(first, 2)
        run(third, 1)
        run(second, 2)
        run(first, 3)
        run(third, 2)
        run(second, 3)
        run(third, 3)

    def done(i, carry):
        pltpu.make_async_copy(s.at[at(i)], dx_ref.at[at(i)], dx_sem.at[i]).wait()
        return carry

    lax.fori_loop(0, tiles, done, 0)


def back(q, k, v, ctx, dctx, lse, segments, slopes, x, dh1, w, vec, grads):
    routes = routed()
    rows, width = q.shape
    model = x.shape[1]
    count, seq = segments.shape
    pairs = width // 128
    tiles = rows // TM
    dma = pltpu.SemaphoreType.DMA
    outs = [jax.ShapeDtypeStruct((rows, model), bf16)]
    scratch = [
        pltpu.VMEM((seq, seq), f32),
        pltpu.VMEM((128, seq), bf16),
        pltpu.VMEM((seq, 128), f32),
        pltpu.VMEM((seq, 128), f32),
        pltpu.VMEM((rows, width), bf16),
        pltpu.VMEM((rows, width), bf16),
        pltpu.VMEM((rows, width), bf16),
        pltpu.VMEM((model, rows), bf16),
        pltpu.VMEM((rows, model), bf16),
        pltpu.VMEM((rows, model), bf16),
        dma((tiles,)),
        dma((tiles,)),
        dma((tiles,)),
    ]
    if routes:
        small = (8, 128)
        shapes = [(g.shape[3:], bf16) for g in grads] + [(w.shape[3:], bf16), (small, f32)]
        outs += [jax.ShapeDtypeStruct(sh, f32) for sh, _ in shapes]
        scratch += [pltpu.VMEM(w.shape, bf16), pltpu.VMEM(TORUS + small, f32), dma((9, 5)), dma((9, 5))]
        for sh, dtype in shapes:
            scratch += [
                pltpu.VMEM((4, 2) + sh, dtype),
                pltpu.VMEM((4,) + sh, dtype),
                pltpu.VMEM((3,) + sh, dtype),
            ]
    else:
        outs += [jax.ShapeDtypeStruct(w.shape, bf16), jax.ShapeDtypeStruct((8, width), f32)]
    return pl.pallas_call(
        functools.partial(back_kernel, seq=seq, pairs=pairs, routes=routes),
        out_shape=outs,
        in_specs=[VMEM] * 8 + [SMEM] + [VMEM] * (4 + len(grads)),
        out_specs=[ANY] + [VMEM] * (len(outs) - 1),
        scratch_shapes=scratch,
        compiler_params=pltpu.CompilerParams(
            vmem_limit_bytes=64 << 20, collective_id=1, has_side_effects=True
        ),
        name="back",
    )(q, k, v, ctx, dctx, lse, segments[..., None], segments[:, None, :], slopes * LOG2E, x, dh1, w, vec, *grads)


def adam_update(weight_old, first_old, second_old, gradient, step_rate):
    first_new = beta_first * first_old + (1.0 - beta_first) * gradient
    second_new = beta_second * second_old + (1.0 - beta_second) * gradient * gradient
    first_hat = first_new / (1.0 - beta_first**STEP)
    second_hat = second_new / (1.0 - beta_second**STEP)
    weight_new = weight_old - step_rate * (
        first_hat / (jnp.sqrt(second_hat) + adam_epsilon) + decay_rate * weight_old
    )
    return (second_new, weight_new)


def shards(
    inputs,
    segments,
    cotangent,
    weight_qkv,
    first_qkv,
    second_qkv,
    weight_out,
    first_out,
    second_out,
    weight_gate_up,
    first_gate_up,
    second_gate_up,
    weight_down,
    first_down,
    second_down,
    head_bias,
    first_head_bias,
    second_head_bias,
    norm_vectors,
    first_norm_vectors,
    second_norm_vectors,
):
    head_count = HEADS // lax.axis_size("tensor")
    all_slopes = jnp.asarray(alibi_slopes(HEADS))
    slopes = lax.dynamic_slice_in_dim(all_slopes, lax.axis_index("tensor") * head_count, head_count)
    low = lambda v: v.astype(bf16)
    model, width = weight_out.shape[1], weight_qkv.shape[2]
    rows_out = weight_out.shape[0]
    small = jnp.zeros((16, model), bf16)
    if routed():
        me = lax.axis_index("dp")
        small = lax.dynamic_update_slice(
            small, low(norm_vectors), (0, me * norm_vectors.shape[1])
        )
        small = lax.dynamic_update_slice(small, low(head_bias), (8, me * head_bias.shape[1]))
        qkv = low(weight_qkv).reshape(-1, width)
        sources = [
            low(weight_gate_up[0]),
            low(weight_gate_up[1]),
            low(weight_down),
            jnp.pad(low(weight_out), ((0, -rows_out % 32), (0, 0))),
        ]
        q, k, v, ctx, lse, vec, gate, up, down, out, qkv = front(
            inputs, segments, slopes, qkv, small, sources
        )
        gate, up = gate.reshape(model, -1), up.reshape(model, -1)
        down = down.reshape(-1, model)
        out = out.reshape((-1,) + out.shape[3:])
    else:
        whole = lambda v, axis: lax.all_gather(low(v), "dp", axis=axis, tiled=True)
        qkv = whole(weight_qkv, 1).reshape(1, -1, width)
        out, down = whole(weight_out, 0)[None], whole(weight_down, 0)
        gate, up = whole(weight_gate_up, 1)
        small = small.at[:6].set(whole(norm_vectors, 1)).at[8:10, :width].set(whole(head_bias, 1))
        q, k, v, ctx, lse, vec = front(inputs, segments, slopes, qkv, small[None], [])
    layer_out, dh1, dctx, d_gate, d_up, d_down, d_out, d_vec = middle(
        ctx, out, gate, up, down, vec, inputs, cotangent
    )
    if routed():
        blocks = lambda v: v.reshape(TORUS + (-1, v.shape[-1]))
        grads = [blocks(d_gate), blocks(d_up), blocks(d_down), blocks(d_out)]
        input_grad, d_gate, d_up, grad_down, d_out, d_qkv, d_small = back(
            q, k, v, ctx, dctx, lse, segments, slopes, inputs, dh1, qkv, d_vec, grads
        )
        grad_qkv = d_qkv.reshape(weight_qkv.shape)
        grad_out = d_out[:rows_out]
        grad_gate_up = jnp.stack([d_gate, d_up])
        grad_heads = d_small[6:8, : head_bias.shape[1]]
        grad_vectors = d_small[:6, : norm_vectors.shape[1]]
    else:
        input_grad, d_qkv, d_heads = back(
            q, k, v, ctx, dctx, lse, segments, slopes, inputs, dh1, qkv, d_vec, []
        )
        owned = lambda v, axis: lax.psum_scatter(
            v.astype(f32), "dp", scatter_dimension=axis, tiled=True
        )
        grad_qkv = owned(d_qkv.reshape(3, model, width), 1)
        grad_out = owned(d_out[0], 0)
        grad_gate_up = owned(jnp.stack([d_gate, d_up]), 1)
        grad_down = owned(d_down, 0)
        grad_heads = owned(d_heads[6:8], 1)
        grad_vectors = owned(d_vec[:6], 1)
    second_qkv_new, weight_qkv_new = adam_update(
        weight_qkv, first_qkv, second_qkv, grad_qkv, matrix_rate
    )
    second_out_new, weight_out_new = adam_update(
        weight_out, first_out, second_out, grad_out, matrix_rate
    )
    second_gu_new, weight_gu_new = adam_update(
        weight_gate_up, first_gate_up, second_gate_up, grad_gate_up, matrix_rate
    )
    second_down_new, weight_down_new = adam_update(
        weight_down, first_down, second_down, grad_down, matrix_rate
    )
    second_heads_new, weight_heads_new = adam_update(
        head_bias, first_head_bias, second_head_bias, grad_heads, vector_rate
    )
    second_vectors_new, weight_vectors_new = adam_update(
        norm_vectors, first_norm_vectors, second_norm_vectors, grad_vectors, vector_rate
    )
    return (
        layer_out,
        input_grad,
        grad_qkv,
        second_qkv_new,
        weight_qkv_new,
        grad_out,
        second_out_new,
        weight_out_new,
        grad_gate_up,
        second_gu_new,
        weight_gu_new,
        grad_down,
        second_down_new,
        weight_down_new,
        grad_heads,
        second_heads_new,
        weight_heads_new,
        grad_vectors,
        second_vectors_new,
        weight_vectors_new,
    )


def solution(mesh):
    in_specs = (
        P("dp", None),
        P("dp", None),
        P("dp", None),
        P(None, "dp", "tensor"),
        P(None, "dp", "tensor"),
        P(None, "dp", "tensor"),
        P(("tensor", "dp"), None),
        P(("tensor", "dp"), None),
        P(("tensor", "dp"), None),
        P(None, "dp", "tensor"),
        P(None, "dp", "tensor"),
        P(None, "dp", "tensor"),
        P(("tensor", "dp"), None),
        P(("tensor", "dp"), None),
        P(("tensor", "dp"), None),
        P(None, ("tensor", "dp")),
        P(None, ("tensor", "dp")),
        P(None, ("tensor", "dp")),
        P(None, "dp"),
        P(None, "dp"),
        P(None, "dp"),
    )
    out_specs = (
        P("dp", None),
        P("dp", None),
        P(None, "dp", "tensor"),
        P(None, "dp", "tensor"),
        P(None, "dp", "tensor"),
        P(("tensor", "dp"), None),
        P(("tensor", "dp"), None),
        P(("tensor", "dp"), None),
        P(None, "dp", "tensor"),
        P(None, "dp", "tensor"),
        P(None, "dp", "tensor"),
        P(("tensor", "dp"), None),
        P(("tensor", "dp"), None),
        P(("tensor", "dp"), None),
        P(None, ("tensor", "dp")),
        P(None, ("tensor", "dp")),
        P(None, ("tensor", "dp")),
        P(None, "dp"),
        P(None, "dp"),
        P(None, "dp"),
    )
    return jax.shard_map(shards, mesh=mesh, in_specs=in_specs, out_specs=out_specs, check_vma=False)
```

```python
import functools
import math
import types

import jax
import jax.numpy as jnp
import numpy as np
from jax import lax
from jax.experimental import pallas as pl
from jax.experimental.pallas import tpu as pltpu
from jax.sharding import PartitionSpec as P

HEADS = 12
HEAD_DIM = 64
SEQ = 1024
STEP = 10

norm_epsilon = 1e-12
beta_first = 0.9
beta_second = 0.999
adam_epsilon = 1e-08
decay_rate = 0.1
matrix_rate = 0.05
vector_rate = 0.5

MESH = pl.DeviceIdType.MESH
TORUS = (4, 2, 2)
f32, bf16 = jnp.float32, jnp.bfloat16
LOG2E = 1.4426950408889634
FAR = 3e12
REACH = 512
BQ = 256
TM = 256
HC = 512
VMEM = pl.BlockSpec(memory_space=pltpu.VMEM)
SMEM = pl.BlockSpec(memory_space=pltpu.SMEM)
ANY = pl.BlockSpec(memory_space=pl.ANY)


def alibi_slopes(head_total):
    power_two = 2 ** int(math.floor(math.log2(head_total)))
    leading = [2.0 ** (-8.0 * (h + 1) / power_two) for h in range(power_two)]
    trailing = [
        2.0 ** (-8.0 * (2 * h + 1) / (2 * power_two)) for h in range(head_total - power_two)
    ]
    return np.array(leading + trailing, dtype=np.float32)


def place():
    me = lax.axis_index("dp")
    return lax.div(me, 4), lax.rem(lax.div(me, 2), 2), lax.rem(me, 2)


def chip(z, y, x):
    return z * 4 + y * 2 + x


def remote(src, dst, ssem, rsem, dp):
    return pltpu.make_async_remote_copy(
        src_ref=src,
        dst_ref=dst,
        send_sem=ssem,
        recv_sem=rsem,
        device_id={"dp": dp},
        device_id_type=MESH,
    )


def swap(src, dst, ssem, rsem):
    return pltpu.make_async_remote_copy(
        src_ref=src,
        dst_ref=dst,
        send_sem=ssem,
        recv_sem=rsem,
        device_id={"tensor": 1 - lax.axis_index("tensor")},
        device_id_type=MESH,
    )


def greet(chips, core):
    barrier = pltpu.get_barrier_semaphore()
    count = 0
    if chips:
        z, y, x = place()
        peers = [chip(lax.rem(z + d, 4), y, x) for d in (1, 2, 3)]
        for dp in peers + [chip(z, 1 - y, x), chip(z, y, 1 - x)]:
            pl.semaphore_signal(barrier, inc=1, device_id={"dp": dp}, device_id_type=MESH)
            count += 1
    if core:
        other = {"tensor": 1 - lax.axis_index("tensor")}
        pl.semaphore_signal(barrier, inc=1, device_id=other, device_id_type=MESH)
        count += 1
    pl.semaphore_wait(barrier, count)


class Gather:
    def __init__(self, src, dst, first, ssem, rsem, lsem):
        self.src, self.dst, self.first = src, dst, first
        self.ssem, self.rsem, self.lsem = ssem, rsem, lsem
        self.z, self.y, self.x = place()

    def own(self):
        return pltpu.make_async_copy(self.src, self.dst(self.z, self.y, self.x), self.lsem)

    def along_z(self, d, arriving):
        z, y, x = self.z, self.y, self.x
        other = lax.rem(z + (4 - d if arriving else d), 4)
        slot = self.dst(other if arriving else z, y, x)
        return remote(self.src, slot, self.ssem.at[d - 1], self.rsem.at[d - 1], chip(other, y, x))

    def plane(self, k, arriving):
        z, y, x = self.z, self.y, self.x
        whole = slice(None)
        on_x = (self.first == "x") == (k == 0)
        dp = chip(z, y, 1 - x) if on_x else chip(z, 1 - y, x)
        yy, xx = y, x
        if arriving:
            yy, xx = (y, 1 - x) if on_x else (1 - y, x)
        if k == 1:
            yy, xx = (whole, xx) if on_x else (yy, whole)
        part = self.dst(whole, yy, xx)
        return remote(part, part, self.ssem.at[3 + k], self.rsem.at[3 + k], dp)

    def s0(self):
        self.own().start()
        for d in (1, 3, 2):
            self.along_z(d, False).start()

    def s1(self):
        self.own().wait()
        for d in (1, 3, 2):
            self.along_z(d, False).wait_send()
            self.along_z(d, True).wait_recv()
        self.plane(0, False).start()

    def s2(self):
        self.plane(0, False).wait_send()
        self.plane(0, True).wait_recv()
        self.plane(1, False).start()

    def s3(self):
        self.plane(1, False).wait_send()
        self.plane(1, True).wait_recv()


class GatherLate(Gather):
    def hop(self, k, arriving):
        z, y, x = self.z, self.y, self.x
        whole = slice(None)
        on_x = (self.first == "x") == (k == 0)
        dp = chip(z, y, 1 - x) if on_x else chip(z, 1 - y, x)
        yy, xx = y, x
        if arriving:
            yy, xx = (y, 1 - x) if on_x else (1 - y, x)
        if k == 1:
            yy, xx = (whole, xx) if on_x else (yy, whole)
        part = self.dst(z, yy, xx)
        src = self.src if k == 0 and not arriving else part
        return remote(src, part, self.ssem.at[3 + k], self.rsem.at[3 + k], dp)

    def along_z(self, d, arriving):
        whole = slice(None)
        other = lax.rem(self.z + (4 - d if arriving else d), 4)
        part = self.dst(other if arriving else self.z, whole, whole)
        dp = chip(other, self.y, self.x)
        return remote(part, part, self.ssem.at[d - 1], self.rsem.at[d - 1], dp)

    def s0(self):
        self.own().start()
        self.hop(0, False).start()

    def s1(self):
        self.own().wait()
        self.hop(0, False).wait_send()
        self.hop(0, True).wait_recv()
        self.hop(1, False).start()

    def s2(self):
        self.hop(1, False).wait_send()
        self.hop(1, True).wait_recv()
        for d in (1, 3, 2):
            self.along_z(d, False).start()

    def s3(self):
        for d in (1, 3, 2):
            self.along_z(d, False).wait_send()
            self.along_z(d, True).wait_recv()


class Scatter:
    def __init__(self, g, r1, r2, r3, out, first, ssem, rsem):
        self.r1, self.r2, self.r3, self.out, self.ssem, self.rsem = r1, r2, r3, out, ssem, rsem
        z, y, x = self.z, self.y, self.x = place()
        on_y, on_x = chip(z, 1 - y, x), chip(z, y, 1 - x)
        if first == "y":
            self.block = lambda zz, a, b: g(zz, a, b)
            self.a, self.b, self.to1, self.to2 = y, x, on_y, on_x
        else:
            self.block = lambda zz, a, b: g(zz, b, a)
            self.a, self.b, self.to1, self.to2 = x, y, on_x, on_y

    def c1(self):
        whole = slice(None)
        src = self.block(whole, 1 - self.a, whole)
        return remote(src, self.r1, self.ssem.at[0], self.rsem.at[0], self.to1)

    def c2(self):
        src = self.r1.at[:, 1 - self.b]
        return remote(src, self.r2, self.ssem.at[1], self.rsem.at[1], self.to2)

    def c3(self, d):
        to = lax.rem(self.z + d, 4)
        dp = chip(to, self.y, self.x)
        return remote(
            self.r2.at[to], self.r3.at[d - 1], self.ssem.at[1 + d], self.rsem.at[1 + d], dp
        )

    def s0(self):
        self.c1().start()

    def s1(self):
        self.c1().wait()
        o = 1 - self.b

        def add(zz, carry):
            t = self.r1.at[zz, o]
            t[...] = (t[...].astype(f32) + self.block(zz, self.a, o)[...].astype(f32)).astype(t.dtype)
            return carry

        lax.fori_loop(0, 4, add, 0)
        self.c2().start()

    def s2(self):
        self.c2().wait()

        def add(d, carry):
            zz = lax.rem(self.z + d, 4)
            t = self.r2.at[zz]
            here = self.r1[zz, self.b].astype(f32) + self.block(zz, self.a, self.b)[...].astype(f32)
            t[...] = (t[...].astype(f32) + here).astype(t.dtype)
            return carry

        lax.fori_loop(1, 4, add, 0)
        for d in (2, 1, 3):
            self.c3(d).start()

    def s3(self):
        for d in (2, 1, 3):
            self.c3(d).wait()
        z = self.z
        total = self.block(z, self.a, self.b)[...].astype(f32) + self.r1[z, self.b].astype(f32)
        total = total + self.r2[z].astype(f32)
        for d in range(3):
            total = total + self.r3[d].astype(f32)
        self.out[...] = total


def run(flows, stage):
    for flow in flows:
        getattr(flow, f"s{stage}")()


def routed():
    return lax.axis_size("dp") == TORUS[0] * TORUS[1] * TORUS[2]


def nt(a, b):
    return lax.dot_general(a, b, (((1,), (1,)), ((), ())), preferred_element_type=f32)


def tn(a, b):
    return lax.dot_general(a, b, (((0,), (0,)), ((), ())), preferred_element_type=f32)


def nn(a, b):
    return jnp.dot(a, b, preferred_element_type=f32)


def span(b, seq):
    lo = max(0, (b * BQ - REACH + 1) // BQ * BQ)
    hi = min(seq, -(-(b * BQ + BQ - 1 + REACH) // BQ) * BQ)
    return lo, hi


def half(value, which):
    lane = lax.broadcasted_iota(jnp.int32, value.shape, 1)
    keep = (lane < 64) if which == 0 else (lane >= 64)
    return jnp.where(keep, value, jnp.zeros_like(value))


def stats(h):
    c = h - jnp.mean(h, axis=-1, keepdims=True)
    return c, spread(c)


def spread(c):
    return lax.rsqrt(jnp.mean(c * c, axis=-1, keepdims=True) + norm_epsilon)


def norm_back(e, n, r):
    return r * (e - jnp.mean(e, axis=-1, keepdims=True) - n * jnp.mean(e * n, axis=-1, keepdims=True))


class Rows:
    def __init__(self, ref, lane, lanes):
        self.ref, self.lane, self.lanes = ref, lane, lanes

    def cols(self, pair):
        return pl.ds(pl.multiple_of(self.lane + pair * 128, 128), 128)

    def tile(self, i):
        return self.ref.at[lax.div(i, 2), lax.rem(i, 2), :, self.lane : self.lane + self.lanes]

    def block(self, s, b, pair):
        return self.ref.at[2 * s + b // 2, b % 2, :, self.cols(pair)]

    def span(self, s, lo, hi, pair):
        parts = [self.block(s, b, pair)[...] for b in range(lo // TM, hi // TM)]
        return jnp.concatenate(parts, axis=0)

    def all(self):
        v = self.ref[:, :, :, self.lane : self.lane + self.lanes]
        return v.reshape(-1, self.lanes)


class Far:
    def __init__(self, ref, seq):
        self.ref, self.seq = ref, seq
        self.across = ref.shape[1] // BQ

    def at(self, lo, hi, b):
        row, col = b // self.across * self.seq, b % self.across * BQ
        return self.ref.at[row + lo : row + hi, col : col + BQ]

    def fill(self, seg_ref, s):
        seq = self.seq
        segs = seg_ref[pl.ds(s, 1), :].astype(f32)
        for c in range(seq // 128):
            mine = jnp.broadcast_to(segs[:, c * 128 : (c + 1) * 128], (128, 128)).T
            for b in range(seq // BQ):
                r = lax.broadcasted_iota(jnp.int32, (128, BQ), 0) + c * 128
                k = lax.broadcasted_iota(jnp.int32, (128, BQ), 1) + b * BQ
                d = jnp.abs(r - k).astype(f32)
                same = jnp.concatenate([mine] * (BQ // 128), axis=1) == segs[:, b * BQ : (b + 1) * BQ]
                self.at(c * 128, (c + 1) * 128, b)[...] = jnp.where(same, d, FAR)


def attend(s, pair, q, k, v, vt_ref, far, slopes, ctx_ref, lse_ref, seq, pairs):
    cols = pl.ds(pl.multiple_of(pair * 128, 128), 128)
    vt_ref[...] = v.span(s, 0, seq, pair).T
    for b in range(seq // BQ):
        lo, hi = span(b, seq)
        qb = q.block(s, b, pair)[...] * jnp.asarray(HEAD_DIM**-0.5, bf16)
        kb = k.span(s, lo, hi, pair)
        score = [nt(kb, half(qb, h)) * LOG2E - slopes[h] * far.at(lo, hi, b)[...] for h in range(2)]
        top = [jnp.max(t, axis=0, keepdims=True) for t in score]
        weight = [jnp.exp2(t - m) for t, m in zip(score, top)]
        total = [jnp.sum(e, axis=0, keepdims=True) for e in weight]
        out = [
            nn(vt_ref[64 * h : 64 * h + 64, lo:hi], weight[h].astype(bf16)) * (1.0 / total[h])
            for h in range(2)
        ]
        for h in range(2):
            lse_ref[s * pairs + pair, h : h + 1, b * BQ : (b + 1) * BQ] = top[h] + jnp.log2(total[h])
        at = pl.ds(pl.multiple_of(s * seq + b * BQ, BQ), BQ)
        ctx_ref[at, cols] = jnp.concatenate(out, axis=0).T.astype(bf16)


def attend_back(
    s, pair, q, k, v, ctx_ref, dctx_ref, lse_ref, far, slopes, kt_ref, dk_acc, dv_acc, dq, dk, dv, seq, pairs
):
    cols = pl.ds(pl.multiple_of(pair * 128, 128), 128)
    kt_ref[...] = k.span(s, 0, seq, pair).T
    dk_acc[...] = jnp.zeros(dk_acc.shape, f32)
    dv_acc[...] = jnp.zeros(dv_acc.shape, f32)
    for b in range(seq // BQ):
        lo, hi = span(b, seq)
        at = pl.ds(pl.multiple_of(s * seq + b * BQ, BQ), BQ)
        qb = q.block(s, b, pair)[...] * jnp.asarray(HEAD_DIM**-0.5, bf16)
        kb, vb = k.span(s, lo, hi, pair), v.span(s, lo, hi, pair)
        db = dctx_ref[at, cols]
        prod = (db.astype(f32) * ctx_ref[at, cols].astype(f32)).T
        out = []
        for h in range(2):
            qh, dh = half(qb, h), half(db, h)
            delta = jnp.sum(prod[64 * h : 64 * h + 64], axis=0, keepdims=True)
            lse = lse_ref[s * pairs + pair, h : h + 1, b * BQ : (b + 1) * BQ]
            p = jnp.exp2(nt(kb, qh) * LOG2E - slopes[h] * far.at(lo, hi, b)[...] - lse)
            ds = (p * (nt(vb, dh) - delta)).astype(bf16)
            dv_acc[lo:hi, :] += nn(p.astype(bf16), dh)
            dk_acc[lo:hi, :] += nn(ds, qh)
            out.append(nn(kt_ref[64 * h : 64 * h + 64, lo:hi], ds))
        dq_val = jnp.concatenate(out, axis=0).T * HEAD_DIM**-0.5
        dq.block(s, b, pair)[...] = dq_val.astype(bf16)
    for b in range(seq // BQ):
        dk.block(s, b, pair)[...] = dk_acc[b * BQ : (b + 1) * BQ, :].astype(bf16)
        dv.block(s, b, pair)[...] = dv_acc[b * BQ : (b + 1) * BQ, :].astype(bf16)


def layer_kernel(names, seq, pairs, routes, lead, *refs):
    R = types.SimpleNamespace(**dict(zip(names, refs)))
    seg_ref, slope_ref, x_hbm, cot_hbm = R.seg, R.slope, R.x, R.cot
    out_hbm, dx_hbm, keep_hbm = R.out, R.dx, R.keep
    wq, wg, wu, wd, wo5 = R.wq, R.wg, R.wu, R.wd, R.wo5
    wo, sm, vec, dvec, gd = R.wo, R.sm, R.vec, R.dvec, R.gd
    io, s1, q1, s2, q2, n1 = R.io, R.s1, R.q1, R.s2, R.q2, R.n1
    hv, av, bv, ctx, lse, vt = R.hv, R.av, R.bv, R.ctx, R.lse, R.vt
    io_sem, out_sem, dx_sem = R.io_sem, R.out_sem, R.dx_sem
    xs, xr, misc = R.xs, R.xr, R.misc
    rows, model = io.shape
    width, ff = ctx.shape[1], av.shape[3]
    tiles, nb = rows // TM, lead[0] * lead[1] * lead[2]
    each, each_out, each_ff = model // nb, width // nb, ff // nb
    pad_out = wo5.shape[3]
    count = seg_ref.shape[0]
    HC = ff // 2
    at = lambda i: pl.ds(pl.multiple_of(i * TM, TM), TM)
    tile = lambda ref, i: ref.at[lax.div(i, 2), lax.rem(i, 2)]
    load = lambda hbm, i: pltpu.make_async_copy(hbm.at[at(i)], io.at[at(i)], io_sem.at[i])
    emit = lambda i: pltpu.make_async_copy(io.at[at(i)], out_hbm.at[at(i)], out_sem.at[i])
    exch = lambda k, i: swap((s1, s2, s1, s1)[k].at[at(i)], (q1, q2, q1, q1)[k].at[at(i)], xs.at[k, i], xr.at[k, i])
    me = lax.axis_index("dp")
    core = lax.axis_index("tensor")
    head0 = core * (2 * pairs)
    slopes_of = lambda pair: [slope_ref[head0 + 2 * pair + h] for h in range(2)]
    gate_w = lambda ref, c: ref[:, :, :, :, c : c + HC].reshape(model, HC)
    lh = lead[0] // 2

    def down_w(c):
        if routes:
            return wd[c // HC * lh : (c // HC + 1) * lh].reshape(HC, model)
        return wd[0, 0, 0, c : c + HC, :]

    def each_tile(f, lo, hi):
        def body(i, carry):
            f(i)
            return carry

        lax.fori_loop(lo, hi, body, 0)

    each_tile(lambda i: load(x_hbm, i).start(), 0, tiles)

    if routes:
        lanes = n1.shape[1]
        place_of, moves, row = {}, [], 0

        def stage_in(name, src):
            nonlocal row
            r, c = src.shape
            place_of[name] = []
            for a in range(0, c, lanes):
                w = min(lanes, c - a)
                spot_in = n1.at[row : row + r, 0:w]
                cp = pltpu.make_async_copy(src.at[:, a : a + w], spot_in, misc.at[len(moves)])
                cp.start()
                moves.append(cp)
                place_of[name].append(spot_in)
                row += -(-r // 8) * 8

        for j in range(3):
            stage_in(j, R.weight_qkv.at[j])
        for j in range(2):
            stage_in(3 + j, R.weight_gate_up.at[j])
        stage_in(5, R.weight_down)
        stage_in(6, R.weight_out)
        for cp in moves:
            cp.wait()
        fetch = lambda name: jnp.concatenate([p[...] for p in place_of[name]], axis=1)
        for j in range(3):
            R.qkv_src[j * each : (j + 1) * each, :] = fetch(j).astype(bf16)
        R.gate_src[...] = fetch(3).astype(bf16)
        R.up_src[...] = fetch(4).astype(bf16)
        R.down_src[...] = fetch(5).astype(bf16)
        pad = R.out_src.shape[0] - each_out
        R.out_src[...] = jnp.concatenate(
            [fetch(6), jnp.zeros((pad, model), f32)], axis=0
        ).astype(bf16)
        spot = R.spot
        spot[...] = jnp.zeros(spot.shape, f32)
        spot[0:6, 0:each] = R.norm_vectors[...]
        spot[6:8, 0:each_out] = R.head_bias[...]
        R.small_src[...] = spot[...].astype(bf16)
        gs, gr, gl = R.gs, R.gr, R.gl
        flows = []

        def flow(src, dst, cuts, kind=Gather):
            made = []
            for a, b, first in cuts:
                j = len(flows)
                slot = lambda z, y, x, a=a, b=b: dst.at[z, y, x, a:b]
                made.append(kind(src.at[a:b], slot, first, gs.at[j], gr.at[j], gl.at[j]))
                flows.append(made[-1])
            return made

        both = lambda a, m, b: ((a, m, "x"), (m, b, "y"))
        gate_up = lambda a, b: flow(R.gate_src, wg, ((a, b, "x"),)) + flow(R.up_src, wu, ((a, b, "y"),))
        qkv_src, down_src = R.qkv_src, R.down_src
        cut = each // 3
        pieces = [
            flow(qkv_src, wq, both(0, 32, 64)) + flow(R.small_src, sm, ((0, 16, "x"),)),
            flow(qkv_src, wq, both(64, 96, 3 * each)),
            flow(R.out_src, wo5, both(0, 16, pad_out)),
            gate_up(0, cut),
            gate_up(cut, 2 * cut),
            gate_up(2 * cut, each),
            flow(down_src, wd, both(0, 32, 64)),
            flow(down_src, wd, both(64, 80, each_ff), GatherLate),
        ]

        def bring(*steps):
            for step in steps:
                run(pieces[step // 10], step % 10)

        greet(True, True)
        bring(20, 21, 10, 0, 22, 23, 50, 70, 1, 71, 11, 40, 2, 12, 51, 3, 13, 30, 41)
    else:
        pairs_in = [
            (R.weight_qkv, wq), (R.weight_gate, wg), (R.weight_up, wu),
            (R.weight_down, wd), (R.weight_out, wo5), (R.small, sm),
        ]
        copies = [pltpu.make_async_copy(a, b.at[0, 0, 0], misc.at[2 + j]) for j, (a, b) in enumerate(pairs_in)]
        for cp in copies:
            cp.start()
        greet(False, True)
        for cp in copies:
            cp.wait()
    if routes:
        wide_zero = jnp.zeros((8, model - 128), f32)
        lane = lax.broadcasted_iota(jnp.int32, (8, 128), 1)
        row = lax.broadcasted_iota(jnp.int32, (8, 128), 0)
        width_of = jnp.where(row < 6, each, each_out)
        upper, lower = 0.0, 0.0
        for b in range(nb):
            piece = sm[b // 4, (b // 2) % 2, b % 2].astype(f32)[0:8]
            piece = jnp.concatenate([jnp.where(lane < width_of, piece, 0.0), wide_zero], axis=1)
            upper = upper + pltpu.roll(piece, b * each, 1)
            lower = lower + pltpu.roll(piece, b * each_out, 1)
        vec[0:8, :], vec[8:16, :] = upper, lower
    else:
        vec[0:8, :] = sm[0, 0, 0, 0:16, :].astype(f32)[0:8]
        vec[8:16, :] = vec[0:8, :]
    bo, bd, g1, c1, g2, c2 = (vec[k : k + 1, :] for k in range(6))

    q, k, v = (Rows(bv, j * width, width) for j in range(3))
    keep = lambda out: pltpu.make_async_copy(
        *((bv.at[:, :, :, 0 : 3 * width], keep_hbm) if out else (keep_hbm, bv.at[:, :, :, 0 : 3 * width])),
        misc.at[0],
    )
    qkv_w = lambda j: wq[:, :, :, j * each : (j + 1) * each, :].reshape(model, width)

    def project(i):
        load(x_hbm, i).wait()
        xb = io[at(i), :]
        for j, (dst, bias) in enumerate(((q, 14), (k, None), (v, 15))):
            val = nn(xb, qkv_w(j))
            if bias is not None:
                val = val + vec[bias : bias + 1, :width]
            dst.tile(i)[...] = val.astype(bf16)

    each_tile(project, 0, tiles)
    if routes:
        bring(52, 31, 72)
    keep(True).start()
    far = Far(n1, seq)

    def forward(it):
        s, pair = lax.div(it, pairs), lax.rem(it, pairs)

        @pl.when(pair == 0)
        def _():
            far.fill(seg_ref, s)

        attend(s, pair, q, k, v, vt, far, slopes_of(pair), ctx, lse, seq, pairs)
        if routes:
            for when, what in ((0, (42,)), (1, (60,)), (2, (32,)), (3, (53,)), (5, (61,))):
                pl.when(it == when)(functools.partial(bring, *what))

    each_tile(forward, 0, count * pairs)
    wo[...] = wo5[:, :, :, :each_out, :].astype(f32).reshape(width, model).astype(bf16)

    def phase_a(i):
        s1[at(i), :] = nn(ctx[at(i), :], wo[...]).astype(bf16)
        exch(0, i).start()

    each_tile(phase_a, 0, tiles)
    keep(True).wait()

    if routes:
        lo_hi = (slice(0, lh), slice(lh, lead[0]))
        stage = [gd.at[part, :, :, 0 : TM * 2 // nb, :] for part in lo_hi]
    else:
        stage = [gd.at[:, :, :, j * TM : (j + 1) * TM, :] for j in range(2)]

    def meet_one(i):
        exch(0, i).wait()

    def norm_one(i, parity):
        attn = s1[at(i), :].astype(f32) + q1[at(i), :].astype(f32) + bo
        c, r = stats(io[at(i), :].astype(f32) + attn)
        load(cot_hbm, i).start()
        n1[at(i), :] = c
        stage[parity][...] = (c * r * g1 + c1).astype(bf16).reshape(stage[parity].shape)

    def geglu(i, parity):
        xb = stage[parity][...].reshape(TM, model)
        for c in range(0, ff, HC):
            gate, up = nn(xb, gate_w(wg, c)), nn(xb, gate_w(wu, c))
            cdf = 0.5 * (1.0 + lax.erf(gate * 0.7071067811865476))
            gel = gate * cdf
            slope = cdf + gate * (jnp.exp(gate * gate * -0.5) * 0.3989422804014327)
            tile(hv, i)[:, c : c + HC] = (gel * up).astype(bf16)
            tile(av, i)[:, c : c + HC] = (up * slope).astype(bf16)
            tile(bv, i)[:, c : c + HC] = gel.astype(bf16)

    def phase_b(j):
        meet_one(2 * j + 1)
        norm_one(2 * j + 1, 1)
        geglu(2 * j, 0)
        meet_one(2 * j + 2)
        norm_one(2 * j + 2, 0)
        geglu(2 * j + 1, 1)

    meet_one(0)
    norm_one(0, 0)
    if routes:
        bring(43, 33)
    each_tile(phase_b, 0, 1)
    if routes:
        bring(62)
    each_tile(phase_b, 1, tiles // 2 - 1)
    meet_one(tiles - 1)
    norm_one(tiles - 1, 1)
    geglu(tiles - 2, 0)
    geglu(tiles - 1, 1)
    if routes:
        bring(63, 73)

    dvec[...] = jnp.zeros(dvec.shape, f32)

    def norm_two(i):
        exch(1, i).wait()
        load(cot_hbm, i).wait()
        c = n1[at(i), :]
        x1 = c * spread(c) * g1 + c1
        ffn = s2[at(i), :].astype(f32) + q2[at(i), :].astype(f32) + bd
        h, r2 = stats(x1 + ffn)
        n2 = h * r2
        dy = io[at(i), :].astype(f32)
        io[at(i), :] = (n2 * g2 + c2).astype(bf16)
        emit(i).start()
        dvec[4:5, :] += jnp.sum(dy * n2, axis=0, keepdims=True)
        dvec[5:6, :] += jnp.sum(dy, axis=0, keepdims=True)
        dh2 = norm_back(dy * g2, n2, r2)
        dvec[1:2, :] += jnp.sum(dh2, axis=0, keepdims=True)
        s2[at(i), :] = dh2.astype(bf16)
        q2[at(i), :] = x1.astype(bf16)

    def phase_down(i):
        s2[at(i), :] = nn(tile(hv, i)[...], wd[...].reshape(ff, model)).astype(bf16)
        exch(1, i).start()

    lag = 3

    def phase_c(i):
        norm_two(i - lag)
        phase_down(i)

    each_tile(phase_down, 0, lag)
    each_tile(phase_c, lag, tiles)
    each_tile(norm_two, tiles - lag, tiles)

    def grad_down(c):
        cols = pl.ds(pl.multiple_of(c * 256, 256), 256)
        val = tn(hv[...].reshape(rows, ff), s2[:, cols]).astype(bf16)
        gd[:, :, :, :, cols] = val.reshape(wd.shape[:4] + (256,))

    each_tile(grad_down, 0, model // 256)
    if routes:
        z, y, x = place()
        peers = [chip(lax.rem(z + d, 4), y, x) for d in (1, 2, 3)]
        peers += [chip(z, 1 - y, x), chip(z, y, 1 - x)]
        other = {"tensor": 1 - core}

        def ready(sem, devices):
            for dev in devices:
                pl.semaphore_signal(sem, inc=1, device_id=dev, device_id_type=MESH)
            pl.semaphore_wait(sem, len(devices))

        ss, sr = R.ss, R.sr
        sent = []

        def back_flow(g, r1, r2, r3, out, cuts, lo=0, lanes=None, shift=(0, 0)):
            made = []
            hi = lo + (lanes or out.shape[1])
            down, along = shift
            for a, b, first in cuts:
                j = len(sent)
                made.append(
                    Scatter(
                        lambda z, y, x, a=a, b=b: g.at[z, y, x, a - down : b - down, lo + along : hi + along],
                        r1(a, b), r2(a, b), r3(a, b), out.at[a:b, lo:hi], first, ss.at[j], sr.at[j],
                    )
                )
                sent.append(made[-1])
            return made

        own = lambda r1, r2, r3: (
            lambda a, b: r1.at[:, :, a:b],
            lambda a, b: r2.at[:, a:b],
            lambda a, b: r3.at[:, a:b],
        )
        eff = wd.shape[3]
        downs = back_flow(
            gd,
            lambda a, b: hv.at[:, :, a:b, 0:model],
            lambda a, b: hv.at[:, 0, eff + a : eff + b, 0:model],
            lambda a, b: hv.at[0:3, 1, eff + a : eff + b, 0:model],
            R.g_down,
            both(0, 48, eff),
        )
        def wide(g, j, out, first, lo, top, end):
            lanes = slice(lo, lo + HC)
            return back_flow(
                g,
                lambda a, b: av.at[:, :, j * each + a : j * each + b, lanes],
                lambda a, b: av.at[:, j, 2 * each + a : 2 * each + b, lanes],
                lambda a, b: av.at[0:3, j, 3 * each + a : 3 * each + b, lanes],
                out,
                ((top, end, first),),
                lo,
                HC,
            )

        gates = [
            wide(wg, 0, R.g_gate, "x", lo, 0, each) + wide(wu, 1, R.g_up, "y", lo, 0, each)
            for lo in (0, HC)
        ]
        outs_flow = back_flow(wo5, *own(R.ro1, R.ro2, R.ro3), R.g_out, both(0, 16, pad_out))
        heads_flow = [
            back_flow(wd, *own(R.rq1, R.rq2, R.rq3), R.g_qkv, both(0, 32, 64)),
            back_flow(wd, *own(R.rq1, R.rq2, R.rq3), R.g_qkv, both(64, 96, 3 * each), shift=(64, width)),
        ]
        heads_flow[1] += back_flow(R.gsm, *own(R.rs1, R.rs2, R.rs3), R.g_small, ((0, 8, "x"),))
        parts = [downs, gates[0], gates[1], outs_flow, heads_flow[0], heads_flow[1]]

        def push(*steps):
            for step in steps:
                run(parts[step // 10], step % 10)

        chips = [{"dp": p} for p in peers]

    def ffn_back(c, i):
        df = s2[at(i), :]
        dh = nt(df, down_w(c))
        a, b = tile(av, i), tile(bv, i)
        dg = (dh * a[:, c : c + HC].astype(f32)).astype(bf16)
        du = (dh * b[:, c : c + HC].astype(f32)).astype(bf16)
        a[:, c : c + HC] = dg
        b[:, c : c + HC] = du
        part = nt(dg, gate_w(wg, c)) + nt(du, gate_w(wu, c))
        if c > 0:
            part = part + s1[at(i), :].astype(f32)
        s1[at(i), :] = part.astype(bf16)
        if c + HC == ff:
            exch(2, i).start()

    def norm_one_back(i):
        exch(2, i).wait()
        emit(i).wait()
        c = n1[at(i), :]
        r = spread(c)
        n = c * r
        dx1 = s2[at(i), :].astype(f32) + (s1[at(i), :].astype(f32) + q1[at(i), :].astype(f32))
        dvec[2:3, :] += jnp.sum(dx1 * n, axis=0, keepdims=True)
        dvec[3:4, :] += jnp.sum(dx1, axis=0, keepdims=True)
        dh1 = norm_back(dx1 * g1, n, r)
        dvec[0:1, :] += jnp.sum(dh1, axis=0, keepdims=True)
        da = dh1.astype(bf16)
        io[at(i), :] = da
        s2[at(i), 0:width] = nt(da, wo[...]).astype(bf16)

    def grad_wide(c):
        cols = pl.ds(pl.multiple_of(c * 256, 256), 256)
        for src, dst in ((av, wg), (bv, wu)):
            val = tn(q2[...], src[:, :, :, cols].reshape(rows, 256)).astype(bf16)
            dst[:, :, :, :, cols] = val.reshape(dst.shape[:4] + (256,))

    per = HC // 256
    if routes:
        ready(R.ready.at[0], chips)
        push(0)
    mid = tiles // 2
    each_tile(lambda i: ffn_back(0, i), 0, tiles)
    each_tile(grad_wide, 0, per)
    if routes:
        ready(R.ready.at[1], chips)
        push(10)
    each_tile(lambda i: ffn_back(HC, i), 0, tiles)
    if routes:
        push(1)

    def phase_e(j):
        norm_one_back(2 * j)
        norm_one_back(2 * j + 1)
        grad_wide(per + j)

    each_tile(phase_e, 0, per)
    each_tile(norm_one_back, 2 * per, tiles)
    keep(False).start()
    reload = pltpu.make_async_copy(x_hbm, q2, misc.at[1])
    reload.start()
    dwo = tn(ctx[...], io[...])
    wo5[:, :, :, :each_out, :] = dwo.reshape(lead + (each_out, model)).astype(bf16)
    if routes:
        ready(R.ready.at[2], chips + [other])
        push(20)
    else:
        pl.semaphore_signal(R.ready.at[2], inc=1, device_id={"tensor": 1 - core}, device_id_type=MESH)
        pl.semaphore_wait(R.ready.at[2], 1)
        grads_out = [(wg, R.g_gate), (wu, R.g_up), (gd, R.g_down), (wo5, R.g_out)]
        copies = [pltpu.make_async_copy(a.at[0, 0, 0], b, misc.at[2 + j]) for j, (a, b) in enumerate(grads_out)]
        for cp in copies:
            cp.start()
    keep(False).wait()

    dq, dk, dv = Rows(hv, model, width), Rows(hv, model + width, width), Rows(bv, 3 * width, width)
    dk_acc, dv_acc = (n1.at[seq : 2 * seq, j : j + 128] for j in (BQ, BQ + 128))

    def backward(it):
        s, pair = lax.div(it, pairs), lax.rem(it, pairs)

        @pl.when(pair == 0)
        def _():
            far.fill(seg_ref, s)

        attend_back(
            s, pair, q, k, v, ctx, s2, lse, far, slopes_of(pair), vt, dk_acc, dv_acc, dq, dk, dv, seq, pairs
        )
        if routes:

            for when, what in ((0, (11, 2)), (3, (30, 12)), (4, (31, 21)), (5, (32,))):
                pl.when(it == when)(functools.partial(push, *what))

    each_tile(backward, 0, count * pairs)
    reload.wait()

    for j, d in enumerate((dq, dk, dv)):
        val = tn(q2[...], d.all()).astype(bf16).reshape(lead + (each, width))
        if routes:
            for top in range(j * each, (j + 1) * each, 16):
                row, lane = (top, 0) if top < 64 else (top - 64, width)
                wd[:, :, :, row : row + 16, lane : lane + width] = val[:, :, :, top - j * each : top - j * each + 16]
        else:
            wd[:, :, :, j // 2 * each : (j // 2 + 1) * each, j % 2 * width : (j % 2 + 1) * width] = val
    heads = [jnp.sum(d.all().astype(f32), axis=0, keepdims=True) for d in (dq, dv)]
    heads = jnp.concatenate([jnp.zeros((6, width), f32)] + heads, axis=0)
    if routes:
        row = lax.broadcasted_iota(jnp.int32, (8, 128), 0)
        for b in range(nb):
            upper = pltpu.roll(dvec[...], (model - b * each) % model, 1)[:, :128]
            lower = pltpu.roll(heads, (width - b * each_out) % width, 1)[:, :128]
            R.gsm[b // 4, (b // 2) % 2, b % 2] = jnp.where(row < 6, upper, lower)
        push(22, 3, 40)
    else:
        R.g_heads[...] = heads
        R.g_vec[...] = dvec[...]
        for j in range(3):
            src = wd.at[0, 0, 0, j // 2 * each : (j // 2 + 1) * each, j % 2 * width : (j % 2 + 1) * width]
            copies.append(pltpu.make_async_copy(src, R.g_qkv.at[j * each : (j + 1) * each], misc.at[6 + j]))
            copies[-1].start()

    def input_part(i):
        val = sum(nt(d.tile(i)[...], qkv_w(j)) for j, d in enumerate((dq, dk, dv)))
        s1[at(i), :] = val.astype(bf16)
        exch(3, i).start()

    each_tile(input_part, 0, mid)
    if routes:
        push(50, 33, 41)
    each_tile(input_part, mid, tiles)
    if routes:
        push(42, 51, 52)

    def finish(i):
        exch(3, i).wait()
        val = io[at(i), :].astype(f32) + (s1[at(i), :].astype(f32) + q1[at(i), :].astype(f32))
        s1[at(i), :] = val.astype(bf16)
        pltpu.make_async_copy(s1.at[at(i)], dx_hbm.at[at(i)], dx_sem.at[i]).start()

    each_tile(finish, 0, tiles)
    if routes:
        push(23, 53, 43, 13)
    else:
        for cp in copies:
            cp.wait()
    each_tile(lambda i: pltpu.make_async_copy(s1.at[at(i)], dx_hbm.at[at(i)], dx_sem.at[i]).wait(), 0, tiles)


def layer(x, cot, segments, slopes, weights):
    routes = routed()
    lead = TORUS if routes else (1, 1, 1)
    rows, model = x.shape
    count, seq = segments.shape
    width, ff = weights.qkv.shape[-1], weights.gate_up.shape[-1]
    pairs, tiles = width // 128, rows // TM
    nb = lead[0] * lead[1] * lead[2]
    each, each_out, each_ff = model // nb, width // nb, ff // nb
    pad_out = -(-each_out // 32) * 32
    dma = pltpu.SemaphoreType.DMA
    low = lambda *s: (s, bf16)
    full = lambda *s: (s, f32)
    ins = [("seg", segments, VMEM), ("slope", slopes, SMEM), ("x", x, ANY), ("cot", cot, ANY)]
    outs = [("out", low(rows, model), ANY), ("dx", low(rows, model), ANY)]
    outs += [("keep", low(tiles // 2, 2, TM, 3 * width), ANY)]
    if routes:
        ins += [("weight_qkv", weights.qkv, ANY), ("weight_gate_up", weights.gate_up, ANY)]
        ins += [("weight_down", weights.down, ANY), ("weight_out", weights.out, ANY)]
        ins += [("head_bias", weights.heads, VMEM), ("norm_vectors", weights.vectors, VMEM)]
        outs += [
            ("g_qkv", full(3 * each, width), VMEM),
            ("g_gate", full(each, ff), VMEM),
            ("g_up", full(each, ff), VMEM),
            ("g_down", full(each_ff, model), VMEM),
            ("g_out", full(pad_out, model), VMEM),
            ("g_small", full(8, 128), VMEM),
        ]
    else:
        ins += [("weight_qkv", weights.qkv.reshape(-1, width), ANY)]
        ins += [("weight_gate", weights.gate_up[0], ANY)]
        ins += [("weight_up", weights.gate_up[1], ANY)]
        ins += [("weight_down", weights.down, ANY), ("weight_out", weights.out, ANY)]
        ins += [("small", weights.small, ANY)]
        outs += [
            ("g_qkv", low(3 * model, width), ANY),
            ("g_gate", low(model, ff), ANY),
            ("g_up", low(model, ff), ANY),
            ("g_down", low(ff, model), ANY),
            ("g_out", low(width, model), ANY),
            ("g_heads", full(8, width), VMEM),
            ("g_vec", full(8, model), VMEM),
        ]
    scratch = [
        ("wq", low(*lead, 3 * each, width)),
        ("wg", low(*lead, each, ff)),
        ("wu", low(*lead, each, ff)),
        ("wd", low(*lead, each_ff, model)),
        ("gd", low(*lead, each_ff, model)),
        ("wo5", low(*lead, pad_out, model)),
        ("sm", low(*lead, 16, 128 if routes else model)),
        ("wo", low(width, model)),
        ("vec", full(16, model)),
        ("n1", full(rows, model)),
        ("ctx", low(rows, width)),
        ("lse", full(count * pairs, 8, seq)),
        ("vt", low(128, seq)),
        ("dvec", full(8, model)),
    ]
    scratch += [(n, low(rows, model)) for n in ("io", "s1", "q1", "s2", "q2")]
    scratch += [(n, low(tiles // 2, 2, TM, ff)) for n in ("hv", "av", "bv")]
    sems = [("io_sem", dma((tiles,))), ("out_sem", dma((tiles,))), ("dx_sem", dma((tiles,)))]
    sems += [("xs", dma((4, tiles))), ("xr", dma((4, tiles))), ("misc", dma((12,)))]
    sems += [("ready", pltpu.SemaphoreType.REGULAR((3,)))]
    if routes:
        scratch += [
            ("qkv_src", low(3 * each, width)),
            ("gate_src", low(each, ff)),
            ("up_src", low(each, ff)),
            ("down_src", low(each_ff, model)),
            ("out_src", low(pad_out, model)),
            ("small_src", low(16, 128)),
            ("spot", full(16, 128)),
            ("gsm", full(*lead, 8, 128)),
        ]
        for name, shape in (("ro", low(pad_out, model)), ("rq", low(3 * each, width)), ("rs", full(8, 128))):
            for j, front in enumerate(((4, 2), (4,), (3,))):
                scratch.append((name + str(j + 1), (front + shape[0], shape[1])))
        sems += [("gs", dma((20, 5))), ("gr", dma((20, 5))), ("gl", dma((20,)))]
        sems += [("ss", dma((24, 5))), ("sr", dma((24, 5)))]
    names = [n for group in (ins, outs, scratch, sems) for n, *_ in group]
    got = pl.pallas_call(
        functools.partial(layer_kernel, names, seq, pairs, routes, lead),
        out_shape=[jax.ShapeDtypeStruct(*s) for _, s, _ in outs],
        in_specs=[space for _, _, space in ins],
        out_specs=[space for _, _, space in outs],
        scratch_shapes=[pltpu.VMEM(*s) for _, s in scratch] + [s for _, s in sems],
        compiler_params=pltpu.CompilerParams(
            vmem_limit_bytes=64 << 20, collective_id=0, has_side_effects=True
        ),
        name="layer",
    )(*[a for _, a, _ in ins])
    return types.SimpleNamespace(**{n: a for (n, *_), a in zip(outs, got)})


def adam_update(weight_old, first_old, second_old, gradient, step_rate):
    first_new = beta_first * first_old + (1.0 - beta_first) * gradient
    second_new = beta_second * second_old + (1.0 - beta_second) * gradient * gradient
    first_hat = first_new / (1.0 - beta_first**STEP)
    second_hat = second_new / (1.0 - beta_second**STEP)
    weight_new = weight_old - step_rate * (
        first_hat / (jnp.sqrt(second_hat) + adam_epsilon) + decay_rate * weight_old
    )
    return (second_new, weight_new)


def update_kernel(*refs):
    out_in, dx_in, qkv, out, gate, up, down, small = refs[:8]
    olds = [refs[8 + 3 * j : 11 + 3 * j] for j in range(6)]
    out_ref, dx_ref = refs[26:28]
    news = [refs[28 + 3 * j : 31 + 3 * j] for j in range(6)]
    hold, sem = refs[46:]
    ends = ((out_in, out_ref), (dx_in, dx_ref))
    come = [pltpu.make_async_copy(a, hold.at[j], sem.at[0, j]) for j, (a, _) in enumerate(ends)]
    leave = [pltpu.make_async_copy(hold.at[j], b, sem.at[1, j]) for j, (_, b) in enumerate(ends)]
    for cp in come:
        cp.start()

    def write(j, at, grad):
        weight, first, second = (r[at] for r in olds[j])
        rate = matrix_rate if j < 4 else vector_rate
        second_new, weight_new = adam_update(weight, first, second, grad, rate)
        for ref, val in zip(news[j], (grad, second_new, weight_new)):
            ref[at] = val

    for cp, onward in zip(come, leave):
        cp.wait()
        onward.start()
    rows = olds[0][0].shape[1]
    for j in range(3):
        write(0, j, qkv[j * rows : (j + 1) * rows, :])
    whole = (slice(None), slice(None))
    write(1, whole, out[: olds[1][0].shape[0], :])
    write(2, 0, gate[...])
    write(2, 1, up[...])
    write(3, whole, down[...])
    write(4, whole, small[6:8, : olds[4][0].shape[1]])
    write(5, whole, small[0:6, : olds[5][0].shape[1]])
    for cp in leave:
        cp.wait()


def update(layer_out, input_grad, sums, olds):
    flat = [a for group in olds for a in group]
    shape = lambda a: jax.ShapeDtypeStruct(a.shape, a.dtype)
    return pl.pallas_call(
        update_kernel,
        out_shape=[shape(layer_out), shape(input_grad)] + [shape(a) for a in flat],
        in_specs=[ANY] * 2 + [VMEM] * (len(sums) + len(flat)),
        out_specs=[ANY] * 2 + [VMEM] * len(flat),
        scratch_shapes=[
            pltpu.VMEM((2,) + layer_out.shape, layer_out.dtype),
            pltpu.SemaphoreType.DMA((2, 2)),
        ],
        compiler_params=pltpu.CompilerParams(vmem_limit_bytes=64 << 20),
        name="update",
    )(layer_out, input_grad, *sums, *flat)


def shards(
    inputs,
    segments,
    cotangent,
    weight_qkv,
    first_qkv,
    second_qkv,
    weight_out,
    first_out,
    second_out,
    weight_gate_up,
    first_gate_up,
    second_gate_up,
    weight_down,
    first_down,
    second_down,
    head_bias,
    first_head_bias,
    second_head_bias,
    norm_vectors,
    first_norm_vectors,
    second_norm_vectors,
):
    slopes = jnp.asarray(alibi_slopes(HEADS) * np.float32(LOG2E))
    model, width = weight_out.shape[1], weight_qkv.shape[2]
    space = types.SimpleNamespace
    olds = [
        (weight_qkv, first_qkv, second_qkv),
        (weight_out, first_out, second_out),
        (weight_gate_up, first_gate_up, second_gate_up),
        (weight_down, first_down, second_down),
        (head_bias, first_head_bias, second_head_bias),
        (norm_vectors, first_norm_vectors, second_norm_vectors),
    ]
    if routed():
        shares = space(
            qkv=weight_qkv, gate_up=weight_gate_up, down=weight_down, out=weight_out,
            heads=head_bias, vectors=norm_vectors,
        )
        got = layer(inputs, cotangent, segments, slopes, shares)
        sums = [got.g_qkv, got.g_out, got.g_gate, got.g_up, got.g_down, got.g_small]
    else:
        whole = lambda v, axis: lax.all_gather(v.astype(bf16), "dp", axis=axis, tiled=True)
        small = jnp.zeros((16, model), bf16)
        small = small.at[:6].set(whole(norm_vectors, 1)).at[6:8, :width].set(whole(head_bias, 1))
        shares = space(
            qkv=whole(weight_qkv, 1), gate_up=whole(weight_gate_up, 1), down=whole(weight_down, 0),
            out=whole(weight_out, 0), small=small,
        )
        got = layer(inputs, cotangent, segments, slopes, shares)
        owned = lambda v, axis: lax.psum_scatter(
            v.astype(f32), "dp", scatter_dimension=axis, tiled=True
        )
        heads, vectors = owned(got.g_heads[6:8], 1), owned(got.g_vec[:6], 1)
        small = jnp.zeros((8, 128), f32)
        small = lax.dynamic_update_slice(small, vectors, (0, 0))
        small = lax.dynamic_update_slice(small, heads, (6, 0))
        sums = [
            owned(got.g_qkv.reshape(3, model, width), 1).reshape(-1, width),
            owned(got.g_out, 0),
            owned(got.g_gate, 0),
            owned(got.g_up, 0),
            owned(got.g_down, 0),
            small,
        ]
    return tuple(update(got.out, got.dx, sums, olds))


def solution(mesh):
    rows, both, cols = P("dp", None), P(("tensor", "dp"), None), P(None, "dp", "tensor")
    heads, vectors = P(None, ("tensor", "dp")), P(None, "dp")
    params = [s for s in (cols, both, cols, both, heads, vectors) for _ in range(3)]
    return jax.shard_map(
        shards,
        mesh=mesh,
        in_specs=(rows, rows, rows, *params),
        out_specs=(rows, rows, *params),
        check_vma=False,
    )
```

```python
import functools
import math
import types

import jax
import jax.numpy as jnp
import numpy as np
from jax import lax
from jax.experimental import pallas as pl
from jax.experimental.pallas import tpu as pltpu
from jax.sharding import PartitionSpec as P

HEADS = 12
HEAD_DIM = 64
SEQ = 1024
STEP = 10

norm_epsilon = 1e-12
beta_first = 0.9
beta_second = 0.999
adam_epsilon = 1e-08
decay_rate = 0.1
matrix_rate = 0.05
vector_rate = 0.5

MESH = pl.DeviceIdType.MESH
TORUS = (4, 2, 2)
f32, bf16 = jnp.float32, jnp.bfloat16
LOG2E = 1.4426950408889634
FAR = 3e12
REACH = 512
BQ = 256
TM = 256
HC = 512
VMEM = pl.BlockSpec(memory_space=pltpu.VMEM)
SMEM = pl.BlockSpec(memory_space=pltpu.SMEM)
ANY = pl.BlockSpec(memory_space=pl.ANY)


def alibi_slopes(head_total):
    power_two = 2 ** int(math.floor(math.log2(head_total)))
    leading = [2.0 ** (-8.0 * (h + 1) / power_two) for h in range(power_two)]
    trailing = [
        2.0 ** (-8.0 * (2 * h + 1) / (2 * power_two)) for h in range(head_total - power_two)
    ]
    return np.array(leading + trailing, dtype=np.float32)


def place():
    me = lax.axis_index("dp")
    return lax.div(me, 4), lax.rem(lax.div(me, 2), 2), lax.rem(me, 2)


def chip(z, y, x):
    return z * 4 + y * 2 + x


def remote(src, dst, ssem, rsem, dp):
    return pltpu.make_async_remote_copy(
        src_ref=src,
        dst_ref=dst,
        send_sem=ssem,
        recv_sem=rsem,
        device_id={"dp": dp},
        device_id_type=MESH,
    )


def swap(src, dst, ssem, rsem):
    return pltpu.make_async_remote_copy(
        src_ref=src,
        dst_ref=dst,
        send_sem=ssem,
        recv_sem=rsem,
        device_id={"tensor": 1 - lax.axis_index("tensor")},
        device_id_type=MESH,
    )


def greet(chips, core):
    barrier = pltpu.get_barrier_semaphore()
    count = 0
    if chips:
        z, y, x = place()
        peers = [chip(lax.rem(z + d, 4), y, x) for d in (1, 2, 3)]
        for dp in peers + [chip(z, 1 - y, x), chip(z, y, 1 - x)]:
            pl.semaphore_signal(barrier, inc=1, device_id={"dp": dp}, device_id_type=MESH)
            count += 1
    if core:
        other = {"tensor": 1 - lax.axis_index("tensor")}
        pl.semaphore_signal(barrier, inc=1, device_id=other, device_id_type=MESH)
        count += 1
    pl.semaphore_wait(barrier, count)


class Gather:
    def __init__(self, src, dst, first, ssem, rsem, lsem):
        self.src, self.dst, self.first = src, dst, first
        self.ssem, self.rsem, self.lsem = ssem, rsem, lsem
        self.z, self.y, self.x = place()

    def own(self):
        return pltpu.make_async_copy(self.src, self.dst(self.z, self.y, self.x), self.lsem)

    def along_z(self, d, arriving):
        z, y, x = self.z, self.y, self.x
        other = lax.rem(z + (4 - d if arriving else d), 4)
        slot = self.dst(other if arriving else z, y, x)
        return remote(self.src, slot, self.ssem.at[d - 1], self.rsem.at[d - 1], chip(other, y, x))

    def plane(self, k, arriving):
        z, y, x = self.z, self.y, self.x
        whole = slice(None)
        on_x = (self.first == "x") == (k == 0)
        dp = chip(z, y, 1 - x) if on_x else chip(z, 1 - y, x)
        yy, xx = y, x
        if arriving:
            yy, xx = (y, 1 - x) if on_x else (1 - y, x)
        if k == 1:
            yy, xx = (whole, xx) if on_x else (yy, whole)
        part = self.dst(whole, yy, xx)
        return remote(part, part, self.ssem.at[3 + k], self.rsem.at[3 + k], dp)

    def s0(self):
        self.own().start()
        for d in (1, 3, 2):
            self.along_z(d, False).start()

    def s1(self):
        self.own().wait()
        for d in (1, 3, 2):
            self.along_z(d, False).wait_send()
            self.along_z(d, True).wait_recv()
        self.plane(0, False).start()

    def s2(self):
        self.plane(0, False).wait_send()
        self.plane(0, True).wait_recv()
        self.plane(1, False).start()

    def s3(self):
        self.plane(1, False).wait_send()
        self.plane(1, True).wait_recv()


class GatherLate(Gather):
    def hop(self, k, arriving):
        z, y, x = self.z, self.y, self.x
        whole = slice(None)
        on_x = (self.first == "x") == (k == 0)
        dp = chip(z, y, 1 - x) if on_x else chip(z, 1 - y, x)
        yy, xx = y, x
        if arriving:
            yy, xx = (y, 1 - x) if on_x else (1 - y, x)
        if k == 1:
            yy, xx = (whole, xx) if on_x else (yy, whole)
        part = self.dst(z, yy, xx)
        src = self.src if k == 0 and not arriving else part
        return remote(src, part, self.ssem.at[3 + k], self.rsem.at[3 + k], dp)

    def along_z(self, d, arriving):
        whole = slice(None)
        other = lax.rem(self.z + (4 - d if arriving else d), 4)
        part = self.dst(other if arriving else self.z, whole, whole)
        dp = chip(other, self.y, self.x)
        return remote(part, part, self.ssem.at[d - 1], self.rsem.at[d - 1], dp)

    def s0(self):
        self.own().start()
        self.hop(0, False).start()

    def s1(self):
        self.own().wait()
        self.hop(0, False).wait_send()
        self.hop(0, True).wait_recv()
        self.hop(1, False).start()

    def s2(self):
        self.hop(1, False).wait_send()
        self.hop(1, True).wait_recv()
        for d in (1, 3, 2):
            self.along_z(d, False).start()

    def s3(self):
        for d in (1, 3, 2):
            self.along_z(d, False).wait_send()
            self.along_z(d, True).wait_recv()


class Scatter:
    def __init__(self, g, r1, r2, r3, out, first, ssem, rsem):
        self.r1, self.r2, self.r3, self.out, self.ssem, self.rsem = r1, r2, r3, out, ssem, rsem
        z, y, x = self.z, self.y, self.x = place()
        on_y, on_x = chip(z, 1 - y, x), chip(z, y, 1 - x)
        if first == "y":
            self.block = lambda zz, a, b: g(zz, a, b)
            self.a, self.b, self.to1, self.to2 = y, x, on_y, on_x
        else:
            self.block = lambda zz, a, b: g(zz, b, a)
            self.a, self.b, self.to1, self.to2 = x, y, on_x, on_y

    def c1(self):
        whole = slice(None)
        src = self.block(whole, 1 - self.a, whole)
        return remote(src, self.r1, self.ssem.at[0], self.rsem.at[0], self.to1)

    def c2(self):
        src = self.r1.at[:, 1 - self.b]
        return remote(src, self.r2, self.ssem.at[1], self.rsem.at[1], self.to2)

    def c3(self, d):
        to = lax.rem(self.z + d, 4)
        dp = chip(to, self.y, self.x)
        return remote(
            self.r2.at[to], self.r3.at[d - 1], self.ssem.at[1 + d], self.rsem.at[1 + d], dp
        )

    def s0(self):
        self.c1().start()

    def s1(self):
        self.c1().wait()
        o = 1 - self.b

        def add(zz, carry):
            t = self.r1.at[zz, o]
            t[...] = (t[...].astype(f32) + self.block(zz, self.a, o)[...].astype(f32)).astype(t.dtype)
            return carry

        lax.fori_loop(0, 4, add, 0)
        self.c2().start()

    def s2(self):
        self.c2().wait()

        def add(d, carry):
            zz = lax.rem(self.z + d, 4)
            t = self.r2.at[zz]
            here = self.r1[zz, self.b].astype(f32) + self.block(zz, self.a, self.b)[...].astype(f32)
            t[...] = (t[...].astype(f32) + here).astype(t.dtype)
            return carry

        lax.fori_loop(1, 4, add, 0)
        for d in (2, 1, 3):
            self.c3(d).start()

    def s3(self):
        for d in (2, 1, 3):
            self.c3(d).wait()
        z = self.z
        total = self.block(z, self.a, self.b)[...].astype(f32) + self.r1[z, self.b].astype(f32)
        total = total + self.r2[z].astype(f32)
        for d in range(3):
            total = total + self.r3[d].astype(f32)
        self.out[...] = total


def run(flows, stage):
    for flow in flows:
        getattr(flow, f"s{stage}")()


def routed():
    return lax.axis_size("dp") == TORUS[0] * TORUS[1] * TORUS[2]


def nt(a, b):
    return lax.dot_general(a, b, (((1,), (1,)), ((), ())), preferred_element_type=f32)


def tn(a, b):
    return lax.dot_general(a, b, (((0,), (0,)), ((), ())), preferred_element_type=f32)


def nn(a, b):
    return jnp.dot(a, b, preferred_element_type=f32)


def span(b, seq):
    lo = max(0, (b * BQ - REACH + 1) // BQ * BQ)
    hi = min(seq, -(-(b * BQ + BQ - 1 + REACH) // BQ) * BQ)
    return lo, hi


def half(value, which):
    lane = lax.broadcasted_iota(jnp.int32, value.shape, 1)
    keep = (lane < 64) if which == 0 else (lane >= 64)
    return jnp.where(keep, value, jnp.zeros_like(value))


def stats(h):
    c = h - jnp.mean(h, axis=-1, keepdims=True)
    return c, spread(c)


def spread(c):
    return lax.rsqrt(jnp.mean(c * c, axis=-1, keepdims=True) + norm_epsilon)


def norm_back(e, n, r):
    return r * (e - jnp.mean(e, axis=-1, keepdims=True) - n * jnp.mean(e * n, axis=-1, keepdims=True))


class Rows:
    def __init__(self, ref, lane, lanes):
        self.ref, self.lane, self.lanes = ref, lane, lanes

    def cols(self, pair):
        return pl.ds(pl.multiple_of(self.lane + pair * 384, 128), 128)

    def tile(self, i):
        return self.ref.at[lax.div(i, 2), lax.rem(i, 2), :, self.lane : self.lane + self.lanes]

    def block(self, s, b, pair):
        return self.ref.at[2 * s + b // 2, b % 2, :, self.cols(pair)]

    def span(self, s, lo, hi, pair):
        parts = [self.block(s, b, pair)[...] for b in range(lo // TM, hi // TM)]
        return jnp.concatenate(parts, axis=0)

    def all(self):
        v = self.ref[:, :, :, self.lane : self.lane + self.lanes]
        return v.reshape(-1, self.lanes)


class Far:
    def __init__(self, ref, seq):
        self.ref, self.seq = ref, seq
        self.across = ref.shape[1] // BQ

    def at(self, lo, hi, b):
        row, col = b // self.across * self.seq, b % self.across * BQ
        return self.ref.at[row + lo : row + hi, col : col + BQ]

    def fill(self, seg_ref, s):
        seq = self.seq
        segs = seg_ref[pl.ds(s, 1), :].astype(f32)
        for c in range(seq // 128):
            mine = jnp.broadcast_to(segs[:, c * 128 : (c + 1) * 128], (128, 128)).T
            for b in range(seq // BQ):
                r = lax.broadcasted_iota(jnp.int32, (128, BQ), 0) + c * 128
                k = lax.broadcasted_iota(jnp.int32, (128, BQ), 1) + b * BQ
                d = jnp.abs(r - k).astype(f32)
                same = jnp.concatenate([mine] * (BQ // 128), axis=1) == segs[:, b * BQ : (b + 1) * BQ]
                self.at(c * 128, (c + 1) * 128, b)[...] = jnp.where(same, d, FAR)


def attend(s, pair, q, k, v, vt_ref, far, slopes, ctx_ref, lse_ref, seq, pairs):
    cols = pl.ds(pl.multiple_of(pair * 128, 128), 128)
    vt_ref[...] = v.span(s, 0, seq, pair).T
    for b in range(seq // BQ):
        lo, hi = span(b, seq)
        qb = q.block(s, b, pair)[...] * jnp.asarray(HEAD_DIM**-0.5, bf16)
        kb = k.span(s, lo, hi, pair)
        score = [nt(kb, half(qb, h)) * LOG2E - slopes[h] * far.at(lo, hi, b)[...] for h in range(2)]
        top = [jnp.max(t, axis=0, keepdims=True) for t in score]
        weight = [jnp.exp2(t - m) for t, m in zip(score, top)]
        total = [jnp.sum(e, axis=0, keepdims=True) for e in weight]
        out = [
            nn(vt_ref[64 * h : 64 * h + 64, lo:hi], weight[h].astype(bf16)) * (1.0 / total[h])
            for h in range(2)
        ]
        for h in range(2):
            lse_ref[s * pairs + pair, h : h + 1, b * BQ : (b + 1) * BQ] = top[h] + jnp.log2(total[h])
        at = pl.ds(pl.multiple_of(s * seq + b * BQ, BQ), BQ)
        ctx_ref[at, cols] = jnp.concatenate(out, axis=0).T.astype(bf16)


def attend_back(
    s, pair, q, k, v, ctx_ref, dctx_ref, lse_ref, far, slopes, kt_ref, dk_acc, dv_acc, dq, dk, dv, seq, pairs
):
    cols = pl.ds(pl.multiple_of(pair * 128, 128), 128)
    kt_ref[...] = k.span(s, 0, seq, pair).T
    dk_acc[...] = jnp.zeros(dk_acc.shape, f32)
    dv_acc[...] = jnp.zeros(dv_acc.shape, f32)
    for b in range(seq // BQ):
        lo, hi = span(b, seq)
        at = pl.ds(pl.multiple_of(s * seq + b * BQ, BQ), BQ)
        qb = q.block(s, b, pair)[...] * jnp.asarray(HEAD_DIM**-0.5, bf16)
        kb, vb = k.span(s, lo, hi, pair), v.span(s, lo, hi, pair)
        db = dctx_ref[at, cols]
        prod = (db.astype(f32) * ctx_ref[at, cols].astype(f32)).T
        out = []
        for h in range(2):
            qh, dh = half(qb, h), half(db, h)
            delta = jnp.sum(prod[64 * h : 64 * h + 64], axis=0, keepdims=True)
            lse = lse_ref[s * pairs + pair, h : h + 1, b * BQ : (b + 1) * BQ]
            p = jnp.exp2(nt(kb, qh) * LOG2E - slopes[h] * far.at(lo, hi, b)[...] - lse)
            ds = (p * (nt(vb, dh) - delta)).astype(bf16)
            dv_acc[lo:hi, :] += nn(p.astype(bf16), dh)
            dk_acc[lo:hi, :] += nn(ds, qh)
            out.append(nn(kt_ref[64 * h : 64 * h + 64, lo:hi], ds))
        dq_val = jnp.concatenate(out, axis=0).T * HEAD_DIM**-0.5
        dq.block(s, b, pair)[...] = dq_val.astype(bf16)
    for b in range(seq // BQ):
        dk.block(s, b, pair)[...] = dk_acc[b * BQ : (b + 1) * BQ, :].astype(bf16)
        dv.block(s, b, pair)[...] = dv_acc[b * BQ : (b + 1) * BQ, :].astype(bf16)


AG = (
    (10, 0, 11, 20, 80, 1, 21, 30, 2, 12, 40, 3, 22, 31),
    (81, 50),
    (32, 41),
    (13, 60),
    (51, 42),
    (82, 23),
    (61, 70),
    (52, 62),
    (),
    (33,),
    (53, 83, 71, 43, 63),
    (72,),
    (),
    (73,),
)
RS = (
    (),
    (),
    (1, 11),
    (2, 20),
    (),
    (12,),
    (30,),
    (21, 31),
    (32,),
    (50, 40, 22),
    (51,),
    (41, 52),
    (60, 33),
    (42,),
    (61, 3, 23, 13, 62),
    (63, 43, 53),
)


def layer_kernel(names, seq, pairs, routes, lead, *refs):
    R = types.SimpleNamespace(**dict(zip(names, refs)))
    seg_ref, slope_ref, x_hbm, cot_hbm = R.seg, R.slope, R.x, R.cot
    out_hbm, dx_hbm, keep_hbm = R.out, R.dx, R.keep
    wq, wg, wu, wd, wo5 = R.wq, R.wg, R.wu, R.wd, R.wo5
    wo, sm, vec, dvec, gd = R.wo, R.sm, R.vec, R.dvec, R.gd
    io, s1, q1, s2, q2, n1 = R.io, R.s1, R.q1, R.s2, R.q2, R.n1
    hv, av, bv, ctx, lse, vt = R.hv, R.av, R.bv, R.ctx, R.lse, R.vt
    io_sem, out_sem, dx_sem = R.io_sem, R.out_sem, R.dx_sem
    xs, xr, misc = R.xs, R.xr, R.misc
    rows, model = io.shape
    width, ff = ctx.shape[1], av.shape[3]
    tiles, nb = rows // TM, lead[0] * lead[1] * lead[2]
    each, each_out, each_ff = model // nb, width // nb, ff // nb
    pad_out = wo5.shape[3]
    count = seg_ref.shape[0]
    HC = ff // 2
    at = lambda i: pl.ds(pl.multiple_of(i * TM, TM), TM)
    tile = lambda ref, i: ref.at[lax.div(i, 2), lax.rem(i, 2)]
    load = lambda hbm, i: pltpu.make_async_copy(hbm.at[at(i)], io.at[at(i)], io_sem.at[i])
    emit = lambda i: pltpu.make_async_copy(io.at[at(i)], out_hbm.at[at(i)], out_sem.at[i])
    exch = lambda k, i: swap((s1, s2, s1, s1)[k].at[at(i)], (q1, q2, q1, q1)[k].at[at(i)], xs.at[k, i], xr.at[k, i])
    me = lax.axis_index("dp")
    core = lax.axis_index("tensor")
    head0 = core * (2 * pairs)
    slopes_of = lambda pair: [slope_ref[head0 + 2 * pair + h] for h in range(2)]
    gate_w = lambda ref, c: ref[:, :, :, :, c : c + HC].reshape(model, HC)
    lh = lead[0] // 2

    def down_w(c):
        if routes:
            return wd[c // HC * lh : (c // HC + 1) * lh].reshape(HC, model)
        return wd[0, 0, 0, c : c + HC, :]

    def each_tile(f, lo, hi):
        def body(i, carry):
            f(i)
            return carry

        lax.fori_loop(lo, hi, body, 0)

    each_tile(lambda i: load(x_hbm, i).start(), 0, tiles)

    if routes:
        lanes = n1.shape[1]
        place_of, moves, row = {}, [], 0

        def stage_in(name, src):
            nonlocal row
            r, c = src.shape
            place_of[name] = []
            for a in range(0, c, lanes):
                w = min(lanes, c - a)
                spot_in = n1.at[row : row + r, 0:w]
                cp = pltpu.make_async_copy(src.at[:, a : a + w], spot_in, misc.at[len(moves)])
                cp.start()
                moves.append(cp)
                place_of[name].append(spot_in)
                row += -(-r // 8) * 8

        for j in range(3):
            stage_in(j, R.weight_qkv.at[j])
        for j in range(2):
            stage_in(3 + j, R.weight_gate_up.at[j])
        stage_in(5, R.weight_down)
        stage_in(6, R.weight_out)
        for cp in moves:
            cp.wait()
        fetch = lambda name: jnp.concatenate([p[...] for p in place_of[name]], axis=1)
        for j in range(3):
            mine = fetch(j).astype(bf16)
            for p in range(pairs):
                R.qkv_src[p * each : (p + 1) * each, j * 128 : (j + 1) * 128] = mine[:, p * 128 : (p + 1) * 128]
        R.gate_src[...] = fetch(3).astype(bf16)
        R.up_src[...] = fetch(4).astype(bf16)
        R.down_src[...] = fetch(5).astype(bf16)
        pad = R.out_src.shape[0] - each_out
        R.out_src[...] = jnp.concatenate(
            [fetch(6), jnp.zeros((pad, model), f32)], axis=0
        ).astype(bf16)
        spot = R.spot
        spot[...] = jnp.zeros(spot.shape, f32)
        spot[0:6, 0:each] = R.norm_vectors[...]
        spot[6:8, 0:each_out] = R.head_bias[...]
        R.small_src[...] = spot[...].astype(bf16)
        gs, gr, gl = R.gs, R.gr, R.gl
        flows = []

        def flow(src, dst, cuts, kind=Gather):
            made = []
            for a, b, first in cuts:
                j = len(flows)
                slot = lambda z, y, x, a=a, b=b: dst.at[z, y, x, a:b]
                made.append(kind(src.at[a:b], slot, first, gs.at[j], gr.at[j], gl.at[j]))
                flows.append(made[-1])
            return made

        both = lambda a, m, b: ((a, m, "x"), (m, b, "y"))
        gate_up = lambda a, b: flow(R.gate_src, wg, ((a, b, "x"),)) + flow(R.up_src, wu, ((a, b, "y"),))
        qkv_src, down_src = R.qkv_src, R.down_src
        cut = each // 3
        pieces = [
            flow(qkv_src, wq, both(0, 16, each)) + flow(R.small_src, sm, ((0, 16, "x"),)),
            flow(qkv_src, wq, both(each, 80, 2 * each)),
            flow(qkv_src, wq, both(2 * each, 112, 3 * each)),
            flow(R.out_src, wo5, both(0, 16, pad_out)),
            gate_up(0, cut),
            gate_up(cut, 2 * cut),
            gate_up(2 * cut, each),
            flow(down_src, wd, both(0, 32, 64)),
            flow(down_src, wd, both(64, 80, each_ff), GatherLate),
        ]

        def bring(*steps):
            for step in steps:
                run(pieces[step // 10], step % 10)

        greet(True, True)
        bring(*AG[0])
    else:
        pairs_in = [
            (R.weight_qkv, wq), (R.weight_gate, wg), (R.weight_up, wu),
            (R.weight_down, wd), (R.weight_out, wo5), (R.small, sm),
        ]
        copies = [pltpu.make_async_copy(a, b.at[0, 0, 0], misc.at[2 + j]) for j, (a, b) in enumerate(pairs_in)]
        for cp in copies:
            cp.start()
        greet(False, True)
        for cp in copies:
            cp.wait()
    if routes:
        wide_zero = jnp.zeros((8, model - 128), f32)
        lane = lax.broadcasted_iota(jnp.int32, (8, 128), 1)
        row = lax.broadcasted_iota(jnp.int32, (8, 128), 0)
        width_of = jnp.where(row < 6, each, each_out)
        upper, lower = 0.0, 0.0
        for b in range(nb):
            piece = sm[b // 4, (b // 2) % 2, b % 2].astype(f32)[0:8]
            piece = jnp.concatenate([jnp.where(lane < width_of, piece, 0.0), wide_zero], axis=1)
            upper = upper + pltpu.roll(piece, b * each, 1)
            lower = lower + pltpu.roll(piece, b * each_out, 1)
        vec[0:8, :], vec[8:16, :] = upper, lower
    else:
        vec[0:8, :] = sm[0, 0, 0, 0:16, :].astype(f32)[0:8]
        vec[8:16, :] = vec[0:8, :]
    bo, bd, g1, c1, g2, c2 = (vec[k : k + 1, :] for k in range(6))

    pair_w = lambda p: wq[:, :, :, p * each : (p + 1) * each, :].reshape(model, 3 * 128)
    qkv = [Rows(bv, j * 128, 128) for j in range(3)]
    keep = lambda out: pltpu.make_async_copy(
        *((bv.at[:, :, :, 0 : 3 * width], keep_hbm) if out else (keep_hbm, bv.at[:, :, :, 0 : 3 * width])),
        misc.at[0],
    )
    each_tile(lambda i: load(x_hbm, i).wait(), 0, tiles)
    far = Far(n1, seq)

    def project(p):
        here = slice(p * 128, (p + 1) * 128)
        bias = jnp.concatenate([vec[14:15, here], jnp.zeros((1, 128), f32), vec[15:16, here]], axis=1)

        def tile_of(i):
            Rows(bv, p * 384, 384).tile(i)[...] = (nn(io[at(i), :], pair_w(p)) + bias).astype(bf16)

        each_tile(tile_of, 0, tiles)
        if routes:
            bring(*AG[1 + 3 * p])

    def forward(it):
        pair, turn = lax.div(it, count), lax.rem(it, count)
        far.fill(seg_ref, turn)
        attend(turn, pair, *qkv, vt, far, slopes_of(pair), ctx, lse, seq, pairs)
        for p in range(pairs):

            @pl.when(it == p * count + count - 2)
            def _(p=p):
                if routes:
                    bring(*AG[2 + 3 * p])

            @pl.when(it == p * count + count - 1)
            def _(p=p):
                if routes:
                    bring(*AG[3 + 3 * p])
                if p + 1 < pairs:
                    project(p + 1)

    project(0)
    each_tile(forward, 0, count * pairs)
    keep(True).start()
    wo[...] = wo5[:, :, :, :each_out, :].astype(f32).reshape(width, model).astype(bf16)

    def phase_a(i):
        s1[at(i), :] = nn(ctx[at(i), :], wo[...]).astype(bf16)
        exch(0, i).start()

    each_tile(phase_a, 0, tiles)
    keep(True).wait()

    if routes:
        lo_hi = (slice(0, lh), slice(lh, lead[0]))
        stage = [gd.at[part, :, :, 0 : TM * 2 // nb, :] for part in lo_hi]
    else:
        stage = [gd.at[:, :, :, j * TM : (j + 1) * TM, :] for j in range(2)]

    def meet_one(i):
        exch(0, i).wait()

    def norm_one(i, parity):
        attn = s1[at(i), :].astype(f32) + q1[at(i), :].astype(f32) + bo
        c, r = stats(io[at(i), :].astype(f32) + attn)
        n1[at(i), :] = c
        stage[parity][...] = (c * r * g1 + c1).astype(bf16).reshape(stage[parity].shape)

    def geglu(i, parity):
        xb = stage[parity][...].reshape(TM, model)
        for c in range(0, ff, HC):
            gate, up = nn(xb, gate_w(wg, c)), nn(xb, gate_w(wu, c))
            cdf = 0.5 * (1.0 + lax.erf(gate * 0.7071067811865476))
            gel = gate * cdf
            slope = cdf + gate * (jnp.exp(gate * gate * -0.5) * 0.3989422804014327)
            tile(hv, i)[:, c : c + HC] = (gel * up).astype(bf16)
            tile(av, i)[:, c : c + HC] = (up * slope).astype(bf16)
            tile(bv, i)[:, c : c + HC] = gel.astype(bf16)

    def phase_b(j):
        meet_one(2 * j + 1)
        meet_one(2 * j + 2)
        norm_one(2 * j + 1, 1)
        geglu(2 * j, 0)
        norm_one(2 * j + 2, 0)
        geglu(2 * j + 1, 1)
        for i in (2 * j + 1, 2 * j + 2):
            load(cot_hbm, i).start()

    meet_one(0)
    norm_one(0, 0)
    load(cot_hbm, 0).start()
    if routes:
        bring(*AG[10])
    each_tile(phase_b, 0, 1)
    if routes:
        bring(*AG[11])
    each_tile(phase_b, 1, 2)
    if routes:
        bring(*AG[12])
    each_tile(phase_b, 2, tiles // 2 - 1)
    meet_one(tiles - 1)
    norm_one(tiles - 1, 1)
    load(cot_hbm, tiles - 1).start()
    geglu(tiles - 2, 0)
    geglu(tiles - 1, 1)
    if routes:
        bring(*AG[13])

    dvec[...] = jnp.zeros(dvec.shape, f32)

    def meet_two(i):
        exch(1, i).wait()
        load(cot_hbm, i).wait()

    def norm_two(i):
        c = n1[at(i), :]
        x1 = c * spread(c) * g1 + c1
        ffn = s2[at(i), :].astype(f32) + q2[at(i), :].astype(f32) + bd
        h, r2 = stats(x1 + ffn)
        n2 = h * r2
        dy = io[at(i), :].astype(f32)
        io[at(i), :] = (n2 * g2 + c2).astype(bf16)
        dvec[4:5, :] += jnp.sum(dy * n2, axis=0, keepdims=True)
        dvec[5:6, :] += jnp.sum(dy, axis=0, keepdims=True)
        dh2 = norm_back(dy * g2, n2, r2)
        dvec[1:2, :] += jnp.sum(dh2, axis=0, keepdims=True)
        s2[at(i), :] = dh2.astype(bf16)
        q2[at(i), :] = x1.astype(bf16)

    def down(i):
        s2[at(i), :] = nn(tile(hv, i)[...], wd[...].reshape(ff, model)).astype(bf16)

    def phase_down(i):
        down(i)
        exch(1, i).start()

    def phase_norm(i):
        meet_two(i)
        norm_two(i)
        emit(i).start()

    lag = 3

    def phase_c(i):
        meet_two(i - lag)
        norm_two(i - lag)
        down(i)
        emit(i - lag).start()
        exch(1, i).start()

    each_tile(phase_down, 0, lag)
    each_tile(phase_c, lag, tiles)
    each_tile(phase_norm, tiles - lag, tiles)

    quarter = ff // 4

    def grad_down(c):
        cols = pl.ds(pl.multiple_of(c * quarter, 128), quarter)
        val = tn(hv[:, :, :, cols].reshape(rows, quarter), s2[...]).astype(bf16)
        if routes:
            gd[c] = val.reshape(gd.shape[1:])
        else:
            gd[0, 0, 0, pl.ds(pl.multiple_of(c * quarter, 128), quarter), :] = val

    each_tile(grad_down, 0, 4)
    if routes:
        z, y, x = place()
        peers = [chip(lax.rem(z + d, 4), y, x) for d in (1, 2, 3)]
        peers += [chip(z, 1 - y, x), chip(z, y, 1 - x)]
        other = {"tensor": 1 - core}

        def ready(sem, devices):
            for dev in devices:
                pl.semaphore_signal(sem, inc=1, device_id=dev, device_id_type=MESH)
            pl.semaphore_wait(sem, len(devices))

        ss, sr = R.ss, R.sr
        sent = []

        def back_flow(g, r1, r2, r3, out, cuts, lo=0, lanes=None, shift=(0, 0)):
            made = []
            hi = lo + (lanes or out.shape[1])
            down, along = shift
            for a, b, first in cuts:
                j = len(sent)
                made.append(
                    Scatter(
                        lambda z, y, x, a=a, b=b: g.at[z, y, x, a - down : b - down, lo + along : hi + along],
                        r1(a, b), r2(a, b), r3(a, b), out.at[a:b, lo:hi], first, ss.at[j], sr.at[j],
                    )
                )
                sent.append(made[-1])
            return made

        def spare(top, deep, left, right):
            return (
                lambda a, b: hv.at[:, :, top + a : top + b, left[0] : left[1]],
                lambda a, b: hv.at[:, 0, deep + a : deep + b, right[0] : right[1]],
                lambda a, b: hv.at[0:3, 1, deep + a : deep + b, right[0] : right[1]],
            )

        own = lambda r1, r2, r3: (
            lambda a, b: r1.at[:, :, a:b],
            lambda a, b: r2.at[:, a:b],
            lambda a, b: r3.at[:, a:b],
        )
        eff = wd.shape[3]
        downs = back_flow(
            gd,
            lambda a, b: hv.at[:, :, a:b, 0:model],
            lambda a, b: hv.at[:, 0, eff + a : eff + b, 0:model],
            lambda a, b: hv.at[0:3, 1, eff + a : eff + b, 0:model],
            R.g_down,
            both(0, 48, eff),
        )
        def wide(g, j, out, first, lo, top, end):
            lanes = slice(lo, lo + HC)
            return back_flow(
                g,
                lambda a, b: av.at[:, :, j * each + a : j * each + b, lanes],
                lambda a, b: av.at[:, j, 2 * each + a : 2 * each + b, lanes],
                lambda a, b: av.at[0:3, j, 3 * each + a : 3 * each + b, lanes],
                out,
                ((top, end, first),),
                lo,
                HC,
            )

        gates = [
            wide(wg, 0, R.g_gate, "x", lo, 0, each) + wide(wu, 1, R.g_up, "y", lo, 0, each)
            for lo in (0, HC)
        ]
        outs_flow = back_flow(wo5, *spare(2 * eff, 2 * eff + pad_out, (0, model), (0, model)), R.g_out, both(0, 16, pad_out))
        heads_flow = [
            back_flow(
                wd,
                *spare(0, 0, (model, model + width), (model + width, model + 2 * width)),
                R.g_qkv,
                both(p * each, p * each + (32 if p == 1 else 16), (p + 1) * each),
                shift=((p - p % 2) * each, p // 2 * width),
            )
            for p in range(pairs)
        ]
        heads_flow[-1] += back_flow(R.gsm, *own(R.rs1, R.rs2, R.rs3), R.g_small, ((0, 8, "x"),))
        parts = [downs, gates[0], gates[1], outs_flow, *heads_flow]

        def push(*steps):
            for step in steps:
                run(parts[step // 10], step % 10)

        chips = [{"dp": p} for p in peers]

    def ffn_back(c, i):
        df = s2[at(i), :]
        dh = nt(df, down_w(c))
        a, b = tile(av, i), tile(bv, i)
        dg = (dh * a[:, c : c + HC].astype(f32)).astype(bf16)
        du = (dh * b[:, c : c + HC].astype(f32)).astype(bf16)
        a[:, c : c + HC] = dg
        b[:, c : c + HC] = du
        part = nt(dg, gate_w(wg, c)) + nt(du, gate_w(wu, c))
        if c > 0:
            part = part + s1[at(i), :].astype(f32)
        s1[at(i), :] = part.astype(bf16)
        if c + HC == ff:
            exch(2, i).start()

    def meet_back(i):
        exch(2, i).wait()
        emit(i).wait()

    def norm_one_back(i):
        c = n1[at(i), :]
        r = spread(c)
        n = c * r
        dx1 = s2[at(i), :].astype(f32) + (s1[at(i), :].astype(f32) + q1[at(i), :].astype(f32))
        dvec[2:3, :] += jnp.sum(dx1 * n, axis=0, keepdims=True)
        dvec[3:4, :] += jnp.sum(dx1, axis=0, keepdims=True)
        dh1 = norm_back(dx1 * g1, n, r)
        dvec[0:1, :] += jnp.sum(dh1, axis=0, keepdims=True)
        da = dh1.astype(bf16)
        io[at(i), :] = da
        s2[at(i), 0:width] = nt(da, wo[...]).astype(bf16)

    def grad_wide(c):
        cols = pl.ds(pl.multiple_of(c * 256, 256), 256)
        for src, dst in ((av, wg), (bv, wu)):
            val = tn(q2[...], src[:, :, :, cols].reshape(rows, 256)).astype(bf16)
            dst[:, :, :, :, cols] = val.reshape(dst.shape[:4] + (256,))

    per = HC // 256
    if routes:
        ready(R.ready.at[0], chips)
        push(0)
    mid = tiles // 2
    each_tile(lambda i: ffn_back(0, i), 0, tiles)
    if routes:
        push(*RS[0])
    each_tile(grad_wide, 0, per)
    if routes:
        ready(R.ready.at[1], chips)
        push(10, *RS[1])
    each_tile(lambda i: ffn_back(HC, i), 0, tiles)
    if routes:
        push(*RS[2])

    def phase_e(j):
        meet_back(2 * j)
        meet_back(2 * j + 1)
        norm_one_back(2 * j)
        norm_one_back(2 * j + 1)
        grad_wide(per + j)

    each_tile(phase_e, 0, per)

    def phase_last(i):
        meet_back(i)
        norm_one_back(i)

    each_tile(phase_last, 2 * per, tiles)
    keep(False).start()
    reload = pltpu.make_async_copy(x_hbm, q2, misc.at[1])
    reload.start()
    dwo = tn(ctx[...], io[...])
    wo5[:, :, :, :each_out, :] = dwo.reshape(lead + (each_out, model)).astype(bf16)
    if routes:
        ready(R.ready.at[2], chips + [other])
        push(*RS[3])
    else:
        pl.semaphore_signal(R.ready.at[2], inc=1, device_id={"tensor": 1 - core}, device_id_type=MESH)
        pl.semaphore_wait(R.ready.at[2], 1)
        grads_out = [(wg, R.g_gate), (wu, R.g_up), (gd, R.g_down), (wo5, R.g_out)]
        copies = [pltpu.make_async_copy(a.at[0, 0, 0], b, misc.at[2 + j]) for j, (a, b) in enumerate(grads_out)]
        for cp in copies:
            cp.start()
    keep(False).wait()

    d_pairs = [Rows(bv, p * 384, 384) for p in range(pairs)]
    dk_acc, dv_acc = (n1.at[seq : 2 * seq, j : j + 128] for j in (BQ, BQ + 128))
    reload.wait()

    def at_pair(pair, tables, first):
        for p in range(pairs):

            @pl.when(pair == p)
            def _(p=p):
                push(*tables[first + 3 * p])

    def backward(pair):
        def one(turn):
            far.fill(seg_ref, turn)
            attend_back(
                turn, pair, *qkv, ctx, s2, lse, far, slopes_of(pair), vt, dk_acc, dv_acc, *qkv, seq, pairs
            )

        each_tile(one, 0, count - 1)
        if routes:
            at_pair(pair, RS, 4)
        each_tile(one, count - 1, count)
        if routes:
            at_pair(pair, RS, 5)
        cols = pl.ds(pl.multiple_of(pair * 384, 128), 384)
        val = tn(q2[...], bv[:, :, :, cols].reshape(rows, 384)).astype(bf16).reshape(lead + (each, 384))
        for p in range(pairs):

            @pl.when(pair == p)
            def _(p=p):
                wd[:, :, :, p % 2 * each : (p % 2 + 1) * each, p // 2 * width : (p // 2 + 1) * width] = val
                if routes and p < pairs - 1:
                    push(*RS[6 + 3 * p])

    each_tile(backward, 0, pairs)

    def add_tile(d, i, total):
        return total + jnp.sum(d.tile(i)[...].astype(f32), axis=0, keepdims=True)

    totals = [
        lax.fori_loop(0, tiles, functools.partial(add_tile, d), jnp.zeros((1, 384), f32)) for d in d_pairs
    ]
    rows_of = [jnp.concatenate([t[:, j : j + 128] for t in totals], axis=1) for j in (0, 256)]
    heads = jnp.concatenate([jnp.zeros((6, width), f32)] + rows_of, axis=0)
    if routes:
        row = lax.broadcasted_iota(jnp.int32, (8, 128), 0)
        for b in range(nb):
            upper = pltpu.roll(dvec[...], (model - b * each) % model, 1)[:, :128]
            lower = pltpu.roll(heads, (width - b * each_out) % width, 1)[:, :128]
            R.gsm[b // 4, (b // 2) % 2, b % 2] = jnp.where(row < 6, upper, lower)
        push(*RS[12])
    else:
        R.g_heads[...] = heads
        R.g_vec[...] = dvec[...]
        for j in range(3):
            src = wd.at[0, 0, 0, j % 2 * each : (j % 2 + 1) * each, j // 2 * width : (j // 2 + 1) * width]
            copies.append(pltpu.make_async_copy(src, R.g_qkv.at[j * each : (j + 1) * each], misc.at[6 + j]))
            copies[-1].start()

    def input_part(i):
        val = sum(nt(d.tile(i)[...], pair_w(p)) for p, d in enumerate(d_pairs))
        s1[at(i), :] = val.astype(bf16)
        exch(3, i).start()

    each_tile(input_part, 0, mid)
    if routes:
        push(*RS[13])
    each_tile(input_part, mid, tiles)
    if routes:
        push(*RS[14])

    def finish(i):
        exch(3, i).wait()
        val = io[at(i), :].astype(f32) + (s1[at(i), :].astype(f32) + q1[at(i), :].astype(f32))
        s1[at(i), :] = val.astype(bf16)
        pltpu.make_async_copy(s1.at[at(i)], dx_hbm.at[at(i)], dx_sem.at[i]).start()

    each_tile(finish, 0, tiles)
    if routes:
        push(*RS[15])
    else:
        for cp in copies:
            cp.wait()
    each_tile(lambda i: pltpu.make_async_copy(s1.at[at(i)], dx_hbm.at[at(i)], dx_sem.at[i]).wait(), 0, tiles)


def layer(x, cot, segments, slopes, weights):
    routes = routed()
    lead = TORUS if routes else (1, 1, 1)
    rows, model = x.shape
    count, seq = segments.shape
    width, ff = weights.qkv.shape[-1], weights.gate_up.shape[-1]
    pairs, tiles = width // 128, rows // TM
    nb = lead[0] * lead[1] * lead[2]
    each, each_out, each_ff = model // nb, width // nb, ff // nb
    pad_out = -(-each_out // 32) * 32
    dma = pltpu.SemaphoreType.DMA
    low = lambda *s: (s, bf16)
    full = lambda *s: (s, f32)
    ins = [("seg", segments, VMEM), ("slope", slopes, SMEM), ("x", x, ANY), ("cot", cot, ANY)]
    outs = [("out", low(rows, model), ANY), ("dx", low(rows, model), ANY)]
    outs += [("keep", low(tiles // 2, 2, TM, 3 * width), ANY)]
    if routes:
        ins += [("weight_qkv", weights.qkv, ANY), ("weight_gate_up", weights.gate_up, ANY)]
        ins += [("weight_down", weights.down, ANY), ("weight_out", weights.out, ANY)]
        ins += [("head_bias", weights.heads, VMEM), ("norm_vectors", weights.vectors, VMEM)]
        outs += [
            ("g_qkv", full(3 * each, width), VMEM),
            ("g_gate", full(each, ff), VMEM),
            ("g_up", full(each, ff), VMEM),
            ("g_down", full(each_ff, model), VMEM),
            ("g_out", full(pad_out, model), VMEM),
            ("g_small", full(8, 128), VMEM),
        ]
    else:
        ins += [("weight_qkv", weights.qkv, ANY)]
        ins += [("weight_gate", weights.gate_up[0], ANY)]
        ins += [("weight_up", weights.gate_up[1], ANY)]
        ins += [("weight_down", weights.down, ANY), ("weight_out", weights.out, ANY)]
        ins += [("small", weights.small, ANY)]
        outs += [
            ("g_qkv", low(3 * model, width), ANY),
            ("g_gate", low(model, ff), ANY),
            ("g_up", low(model, ff), ANY),
            ("g_down", low(ff, model), ANY),
            ("g_out", low(width, model), ANY),
            ("g_heads", full(8, width), VMEM),
            ("g_vec", full(8, model), VMEM),
        ]
    scratch = [
        ("wq", low(*lead, 3 * each, width)),
        ("wg", low(*lead, each, ff)),
        ("wu", low(*lead, each, ff)),
        ("wd", low(*lead, each_ff, model)),
        ("gd", low(*lead, each_ff, model)),
        ("wo5", low(*lead, pad_out, model)),
        ("sm", low(*lead, 16, 128 if routes else model)),
        ("wo", low(width, model)),
        ("vec", full(16, model)),
        ("n1", full(rows, model)),
        ("ctx", low(rows, width)),
        ("lse", full(count * pairs, 8, seq)),
        ("vt", low(128, seq)),
        ("dvec", full(8, model)),
    ]
    scratch += [(n, low(rows, model)) for n in ("io", "s1", "q1", "s2", "q2")]
    scratch += [(n, low(tiles // 2, 2, TM, ff)) for n in ("hv", "av", "bv")]
    sems = [("io_sem", dma((tiles,))), ("out_sem", dma((tiles,))), ("dx_sem", dma((tiles,)))]
    sems += [("xs", dma((4, tiles))), ("xr", dma((4, tiles))), ("misc", dma((12,)))]
    sems += [("ready", pltpu.SemaphoreType.REGULAR((3,)))]
    if routes:
        scratch += [
            ("qkv_src", low(3 * each, width)),
            ("gate_src", low(each, ff)),
            ("up_src", low(each, ff)),
            ("down_src", low(each_ff, model)),
            ("out_src", low(pad_out, model)),
            ("small_src", low(16, 128)),
            ("spot", full(16, 128)),
            ("gsm", full(*lead, 8, 128)),
        ]
        for name, shape in (("rs", full(8, 128)),):
            for j, front in enumerate(((4, 2), (4,), (3,))):
                scratch.append((name + str(j + 1), (front + shape[0], shape[1])))
        sems += [("gs", dma((20, 5))), ("gr", dma((20, 5))), ("gl", dma((20,)))]
        sems += [("ss", dma((24, 5))), ("sr", dma((24, 5)))]
    names = [n for group in (ins, outs, scratch, sems) for n, *_ in group]
    got = pl.pallas_call(
        functools.partial(layer_kernel, names, seq, pairs, routes, lead),
        out_shape=[jax.ShapeDtypeStruct(*s) for _, s, _ in outs],
        in_specs=[space for _, _, space in ins],
        out_specs=[space for _, _, space in outs],
        scratch_shapes=[pltpu.VMEM(*s) for _, s in scratch] + [s for _, s in sems],
        compiler_params=pltpu.CompilerParams(
            vmem_limit_bytes=64 << 20, collective_id=0, has_side_effects=True
        ),
        name="layer",
    )(*[a for _, a, _ in ins])
    return types.SimpleNamespace(**{n: a for (n, *_), a in zip(outs, got)})


def adam_update(weight_old, first_old, second_old, gradient, step_rate):
    first_new = beta_first * first_old + (1.0 - beta_first) * gradient
    second_new = beta_second * second_old + (1.0 - beta_second) * gradient * gradient
    first_hat = first_new / (1.0 - beta_first**STEP)
    second_hat = second_new / (1.0 - beta_second**STEP)
    weight_new = weight_old - step_rate * (
        first_hat / (jnp.sqrt(second_hat) + adam_epsilon) + decay_rate * weight_old
    )
    return (second_new, weight_new)


def update_kernel(*refs):
    out_in, dx_in, qkv, out, gate, up, down, small = refs[:8]
    olds = [refs[8 + 3 * j : 11 + 3 * j] for j in range(6)]
    out_ref, dx_ref = refs[26:28]
    news = [refs[28 + 3 * j : 31 + 3 * j] for j in range(6)]
    hold, sem = refs[46:]
    ends = ((out_in, out_ref), (dx_in, dx_ref))
    come = [pltpu.make_async_copy(a, hold.at[j], sem.at[0, j]) for j, (a, _) in enumerate(ends)]
    leave = [pltpu.make_async_copy(hold.at[j], b, sem.at[1, j]) for j, (_, b) in enumerate(ends)]
    for cp in come:
        cp.start()

    def write(j, at, grad):
        weight, first, second = (r[at] for r in olds[j])
        rate = matrix_rate if j < 4 else vector_rate
        second_new, weight_new = adam_update(weight, first, second, grad, rate)
        for ref, val in zip(news[j], (grad, second_new, weight_new)):
            ref[at] = val

    for cp, onward in zip(come, leave):
        cp.wait()
        onward.start()
    rows = olds[0][0].shape[1]
    for j in range(3):
        cols = slice(j * 128, (j + 1) * 128)
        mine = [qkv[p * rows : (p + 1) * rows, cols] for p in range(qkv.shape[0] // rows)]
        write(0, j, jnp.concatenate(mine, axis=1))
    whole = (slice(None), slice(None))
    write(1, whole, out[: olds[1][0].shape[0], :])
    write(2, 0, gate[...])
    write(2, 1, up[...])
    write(3, whole, down[...])
    write(4, whole, small[6:8, : olds[4][0].shape[1]])
    write(5, whole, small[0:6, : olds[5][0].shape[1]])
    for cp in leave:
        cp.wait()


def update(layer_out, input_grad, sums, olds):
    flat = [a for group in olds for a in group]
    shape = lambda a: jax.ShapeDtypeStruct(a.shape, a.dtype)
    return pl.pallas_call(
        update_kernel,
        out_shape=[shape(layer_out), shape(input_grad)] + [shape(a) for a in flat],
        in_specs=[ANY] * 2 + [VMEM] * (len(sums) + len(flat)),
        out_specs=[ANY] * 2 + [VMEM] * len(flat),
        scratch_shapes=[
            pltpu.VMEM((2,) + layer_out.shape, layer_out.dtype),
            pltpu.SemaphoreType.DMA((2, 2)),
        ],
        compiler_params=pltpu.CompilerParams(vmem_limit_bytes=64 << 20),
        name="update",
    )(layer_out, input_grad, *sums, *flat)


def shards(
    inputs,
    segments,
    cotangent,
    weight_qkv,
    first_qkv,
    second_qkv,
    weight_out,
    first_out,
    second_out,
    weight_gate_up,
    first_gate_up,
    second_gate_up,
    weight_down,
    first_down,
    second_down,
    head_bias,
    first_head_bias,
    second_head_bias,
    norm_vectors,
    first_norm_vectors,
    second_norm_vectors,
):
    slopes = jnp.asarray(alibi_slopes(HEADS) * np.float32(LOG2E))
    model, width = weight_out.shape[1], weight_qkv.shape[2]
    space = types.SimpleNamespace
    olds = [
        (weight_qkv, first_qkv, second_qkv),
        (weight_out, first_out, second_out),
        (weight_gate_up, first_gate_up, second_gate_up),
        (weight_down, first_down, second_down),
        (head_bias, first_head_bias, second_head_bias),
        (norm_vectors, first_norm_vectors, second_norm_vectors),
    ]
    if routed():
        shares = space(
            qkv=weight_qkv, gate_up=weight_gate_up, down=weight_down, out=weight_out,
            heads=head_bias, vectors=norm_vectors,
        )
        got = layer(inputs, cotangent, segments, slopes, shares)
        sums = [got.g_qkv, got.g_out, got.g_gate, got.g_up, got.g_down, got.g_small]
    else:
        whole = lambda v, axis: lax.all_gather(v.astype(bf16), "dp", axis=axis, tiled=True)
        small = jnp.zeros((16, model), bf16)
        small = small.at[:6].set(whole(norm_vectors, 1)).at[6:8, :width].set(whole(head_bias, 1))
        packed = whole(weight_qkv, 1).reshape(3, model, -1, 128).transpose(2, 1, 0, 3).reshape(-1, width)
        shares = space(
            qkv=packed, gate_up=whole(weight_gate_up, 1), down=whole(weight_down, 0),
            out=whole(weight_out, 0), small=small,
        )
        got = layer(inputs, cotangent, segments, slopes, shares)
        owned = lambda v, axis: lax.psum_scatter(
            v.astype(f32), "dp", scatter_dimension=axis, tiled=True
        )
        heads, vectors = owned(got.g_heads[6:8], 1), owned(got.g_vec[:6], 1)
        small = jnp.zeros((8, 128), f32)
        small = lax.dynamic_update_slice(small, vectors, (0, 0))
        small = lax.dynamic_update_slice(small, heads, (6, 0))
        sums = [
            owned(got.g_qkv.reshape(-1, model, width), 1).reshape(-1, width),
            owned(got.g_out, 0),
            owned(got.g_gate, 0),
            owned(got.g_up, 0),
            owned(got.g_down, 0),
            small,
        ]
    return tuple(update(got.out, got.dx, sums, olds))


def solution(mesh):
    rows, both, cols = P("dp", None), P(("tensor", "dp"), None), P(None, "dp", "tensor")
    heads, vectors = P(None, ("tensor", "dp")), P(None, "dp")
    params = [s for s in (cols, both, cols, both, heads, vectors) for _ in range(3)]
    return jax.shard_map(
        shards,
        mesh=mesh,
        in_specs=(rows, rows, rows, *params),
        out_specs=(rows, rows, *params),
        check_vma=False,
    )
```

```python
import functools
import math
import types

import jax
import jax.numpy as jnp
import numpy as np
from jax import lax
from jax.experimental import pallas as pl
from jax.experimental.pallas import tpu as pltpu
from jax.sharding import PartitionSpec as P

HEADS = 12
HEAD_DIM = 64
SEQ = 1024
STEP = 10

norm_epsilon = 1e-12
beta_first = 0.9
beta_second = 0.999
adam_epsilon = 1e-08
decay_rate = 0.1
matrix_rate = 0.05
vector_rate = 0.5

MESH = pl.DeviceIdType.MESH
TORUS = (4, 2, 2)
f32, bf16 = jnp.float32, jnp.bfloat16
LOG2E = 1.4426950408889634
FAR = 3e12
REACH = 512
BQ = 256
TM = 256
HC = 512
VMEM = pl.BlockSpec(memory_space=pltpu.VMEM)
SMEM = pl.BlockSpec(memory_space=pltpu.SMEM)
ANY = pl.BlockSpec(memory_space=pl.ANY)


def alibi_slopes(head_total):
    power_two = 2 ** int(math.floor(math.log2(head_total)))
    leading = [2.0 ** (-8.0 * (h + 1) / power_two) for h in range(power_two)]
    trailing = [
        2.0 ** (-8.0 * (2 * h + 1) / (2 * power_two)) for h in range(head_total - power_two)
    ]
    return np.array(leading + trailing, dtype=np.float32)


def place():
    me = lax.axis_index("dp")
    return lax.div(me, 4), lax.rem(lax.div(me, 2), 2), lax.rem(me, 2)


def chip(z, y, x):
    return z * 4 + y * 2 + x


def remote(src, dst, ssem, rsem, dp):
    return pltpu.make_async_remote_copy(
        src_ref=src,
        dst_ref=dst,
        send_sem=ssem,
        recv_sem=rsem,
        device_id={"dp": dp},
        device_id_type=MESH,
    )


def swap(src, dst, ssem, rsem):
    return pltpu.make_async_remote_copy(
        src_ref=src,
        dst_ref=dst,
        send_sem=ssem,
        recv_sem=rsem,
        device_id={"tensor": 1 - lax.axis_index("tensor")},
        device_id_type=MESH,
    )


def greet(chips, core):
    barrier = pltpu.get_barrier_semaphore()
    count = 0
    if chips:
        z, y, x = place()
        peers = [chip(lax.rem(z + d, 4), y, x) for d in (1, 2, 3)]
        for dp in peers + [chip(z, 1 - y, x), chip(z, y, 1 - x)]:
            pl.semaphore_signal(barrier, inc=1, device_id={"dp": dp}, device_id_type=MESH)
            count += 1
    if core:
        other = {"tensor": 1 - lax.axis_index("tensor")}
        pl.semaphore_signal(barrier, inc=1, device_id=other, device_id_type=MESH)
        count += 1
    pl.semaphore_wait(barrier, count)


class Gather:
    def __init__(self, src, dst, first, ssem, rsem, lsem):
        self.src, self.dst, self.first = src, dst, first
        self.ssem, self.rsem, self.lsem = ssem, rsem, lsem
        self.z, self.y, self.x = place()

    def own(self):
        return pltpu.make_async_copy(self.src, self.dst(self.z, self.y, self.x), self.lsem)

    def along_z(self, d, arriving):
        z, y, x = self.z, self.y, self.x
        other = lax.rem(z + (4 - d if arriving else d), 4)
        slot = self.dst(other if arriving else z, y, x)
        return remote(self.src, slot, self.ssem.at[d - 1], self.rsem.at[d - 1], chip(other, y, x))

    def plane(self, k, arriving):
        z, y, x = self.z, self.y, self.x
        whole = slice(None)
        on_x = (self.first == "x") == (k == 0)
        dp = chip(z, y, 1 - x) if on_x else chip(z, 1 - y, x)
        yy, xx = y, x
        if arriving:
            yy, xx = (y, 1 - x) if on_x else (1 - y, x)
        if k == 1:
            yy, xx = (whole, xx) if on_x else (yy, whole)
        part = self.dst(whole, yy, xx)
        return remote(part, part, self.ssem.at[3 + k], self.rsem.at[3 + k], dp)

    def s0(self):
        self.own().start()
        for d in (1, 3, 2):
            self.along_z(d, False).start()

    def s1(self):
        self.own().wait()
        for d in (1, 3, 2):
            self.along_z(d, False).wait_send()
            self.along_z(d, True).wait_recv()
        self.plane(0, False).start()

    def s2(self):
        self.plane(0, False).wait_send()
        self.plane(0, True).wait_recv()
        self.plane(1, False).start()

    def s3(self):
        self.plane(1, False).wait_send()
        self.plane(1, True).wait_recv()


class GatherLate(Gather):
    def hop(self, k, arriving):
        z, y, x = self.z, self.y, self.x
        whole = slice(None)
        on_x = (self.first == "x") == (k == 0)
        dp = chip(z, y, 1 - x) if on_x else chip(z, 1 - y, x)
        yy, xx = y, x
        if arriving:
            yy, xx = (y, 1 - x) if on_x else (1 - y, x)
        if k == 1:
            yy, xx = (whole, xx) if on_x else (yy, whole)
        part = self.dst(z, yy, xx)
        src = self.src if k == 0 and not arriving else part
        return remote(src, part, self.ssem.at[3 + k], self.rsem.at[3 + k], dp)

    def along_z(self, d, arriving):
        whole = slice(None)
        other = lax.rem(self.z + (4 - d if arriving else d), 4)
        part = self.dst(other if arriving else self.z, whole, whole)
        dp = chip(other, self.y, self.x)
        return remote(part, part, self.ssem.at[d - 1], self.rsem.at[d - 1], dp)

    def s0(self):
        self.own().start()
        self.hop(0, False).start()

    def s1(self):
        self.own().wait()
        self.hop(0, False).wait_send()
        self.hop(0, True).wait_recv()
        self.hop(1, False).start()

    def s2(self):
        self.hop(1, False).wait_send()
        self.hop(1, True).wait_recv()
        for d in (1, 3, 2):
            self.along_z(d, False).start()

    def s3(self):
        for d in (1, 3, 2):
            self.along_z(d, False).wait_send()
            self.along_z(d, True).wait_recv()


class Scatter:
    def __init__(self, g, r1, r2, r3, out, first, ssem, rsem):
        self.r1, self.r2, self.r3, self.out, self.ssem, self.rsem = r1, r2, r3, out, ssem, rsem
        z, y, x = self.z, self.y, self.x = place()
        on_y, on_x = chip(z, 1 - y, x), chip(z, y, 1 - x)
        if first == "y":
            self.block = lambda zz, a, b: g(zz, a, b)
            self.a, self.b, self.to1, self.to2 = y, x, on_y, on_x
        else:
            self.block = lambda zz, a, b: g(zz, b, a)
            self.a, self.b, self.to1, self.to2 = x, y, on_x, on_y

    def c1(self):
        whole = slice(None)
        src = self.block(whole, 1 - self.a, whole)
        return remote(src, self.r1, self.ssem.at[0], self.rsem.at[0], self.to1)

    def c2(self):
        src = self.r1.at[:, 1 - self.b]
        return remote(src, self.r2, self.ssem.at[1], self.rsem.at[1], self.to2)

    def c3(self, d):
        to = lax.rem(self.z + d, 4)
        dp = chip(to, self.y, self.x)
        return remote(
            self.r2.at[to], self.r3.at[d - 1], self.ssem.at[1 + d], self.rsem.at[1 + d], dp
        )

    def s0(self):
        self.c1().start()

    def s1(self):
        self.c1().wait()
        o = 1 - self.b

        def add(zz, carry):
            t = self.r1.at[zz, o]
            t[...] = (t[...].astype(f32) + self.block(zz, self.a, o)[...].astype(f32)).astype(t.dtype)
            return carry

        lax.fori_loop(0, 4, add, 0)
        self.c2().start()

    def s2(self):
        self.c2().wait()

        def add(d, carry):
            zz = lax.rem(self.z + d, 4)
            t = self.r2.at[zz]
            here = self.r1[zz, self.b].astype(f32) + self.block(zz, self.a, self.b)[...].astype(f32)
            t[...] = (t[...].astype(f32) + here).astype(t.dtype)
            return carry

        lax.fori_loop(1, 4, add, 0)
        for d in (2, 1, 3):
            self.c3(d).start()

    def s3(self):
        for d in (2, 1, 3):
            self.c3(d).wait()
        z = self.z
        total = self.block(z, self.a, self.b)[...].astype(f32) + self.r1[z, self.b].astype(f32)
        total = total + self.r2[z].astype(f32)
        for d in range(3):
            total = total + self.r3[d].astype(f32)
        self.out[...] = total


def run(flows, stage):
    for flow in flows:
        getattr(flow, f"s{stage}")()


def routed():
    return lax.axis_size("dp") == TORUS[0] * TORUS[1] * TORUS[2]


def nt(a, b):
    return lax.dot_general(a, b, (((1,), (1,)), ((), ())), preferred_element_type=f32)


def tn(a, b):
    return lax.dot_general(a, b, (((0,), (0,)), ((), ())), preferred_element_type=f32)


def nn(a, b):
    return jnp.dot(a, b, preferred_element_type=f32)


def span(b, seq):
    lo = max(0, (b * BQ - REACH + 1) // BQ * BQ)
    hi = min(seq, -(-(b * BQ + BQ - 1 + REACH) // BQ) * BQ)
    return lo, hi


def half(value, which):
    lane = lax.broadcasted_iota(jnp.int32, value.shape, 1)
    keep = (lane < 64) if which == 0 else (lane >= 64)
    return jnp.where(keep, value, jnp.zeros_like(value))


def stats(h):
    c = h - jnp.mean(h, axis=-1, keepdims=True)
    return c, spread(c)


def spread(c):
    return lax.rsqrt(jnp.mean(c * c, axis=-1, keepdims=True) + norm_epsilon)


def norm_back(e, n, r):
    return r * (e - jnp.mean(e, axis=-1, keepdims=True) - n * jnp.mean(e * n, axis=-1, keepdims=True))


class Rows:
    def __init__(self, ref, lane, lanes):
        self.ref, self.lane, self.lanes = ref, lane, lanes

    def cols(self, pair):
        return pl.ds(pl.multiple_of(self.lane + pair * 384, 128), 128)

    def tile(self, i):
        return self.ref.at[lax.div(i, 2), lax.rem(i, 2), :, self.lane : self.lane + self.lanes]

    def block(self, s, b, pair):
        return self.ref.at[2 * s + b // 2, b % 2, :, self.cols(pair)]

    def span(self, s, lo, hi, pair):
        parts = [self.block(s, b, pair)[...] for b in range(lo // TM, hi // TM)]
        return jnp.concatenate(parts, axis=0)

    def all(self):
        v = self.ref[:, :, :, self.lane : self.lane + self.lanes]
        return v.reshape(-1, self.lanes)


class Far:
    def __init__(self, ref, seq):
        self.ref, self.seq = ref, seq
        self.across = ref.shape[1] // BQ

    def at(self, lo, hi, b):
        row, col = b // self.across * self.seq, b % self.across * BQ
        return self.ref.at[row + lo : row + hi, col : col + BQ]

    def fill(self, seg_ref, s):
        seq = self.seq
        segs = seg_ref[pl.ds(s, 1), :].astype(f32)
        for c in range(seq // 128):
            mine = jnp.broadcast_to(segs[:, c * 128 : (c + 1) * 128], (128, 128)).T
            for b in range(seq // BQ):
                r = lax.broadcasted_iota(jnp.int32, (128, BQ), 0) + c * 128
                k = lax.broadcasted_iota(jnp.int32, (128, BQ), 1) + b * BQ
                d = jnp.abs(r - k).astype(f32)
                same = jnp.concatenate([mine] * (BQ // 128), axis=1) == segs[:, b * BQ : (b + 1) * BQ]
                self.at(c * 128, (c + 1) * 128, b)[...] = jnp.where(same, d, FAR)


def attend(s, pair, q, k, v, vt_ref, far, slopes, ctx_ref, lse_ref, seq, pairs):
    cols = pl.ds(pl.multiple_of(pair * 128, 128), 128)
    vt_ref[...] = v.span(s, 0, seq, pair).T
    for b in range(seq // BQ):
        lo, hi = span(b, seq)
        qb = q.block(s, b, pair)[...] * jnp.asarray(HEAD_DIM**-0.5, bf16)
        kb = k.span(s, lo, hi, pair)
        score = [nt(kb, half(qb, h)) * LOG2E - slopes[h] * far.at(lo, hi, b)[...] for h in range(2)]
        top = [jnp.max(t, axis=0, keepdims=True) for t in score]
        weight = [jnp.exp2(t - m) for t, m in zip(score, top)]
        total = [jnp.sum(e, axis=0, keepdims=True) for e in weight]
        out = [
            nn(vt_ref[64 * h : 64 * h + 64, lo:hi], weight[h].astype(bf16)) * (1.0 / total[h])
            for h in range(2)
        ]
        for h in range(2):
            lse_ref[s * pairs + pair, h : h + 1, b * BQ : (b + 1) * BQ] = top[h] + jnp.log2(total[h])
        at = pl.ds(pl.multiple_of(s * seq + b * BQ, BQ), BQ)
        ctx_ref[at, cols] = jnp.concatenate(out, axis=0).T.astype(bf16)


def attend_back(
    s, pair, q, k, v, ctx_ref, dctx_ref, lse_ref, far, slopes, kt_ref, dk_acc, dv_acc, dq, dk, dv, seq, pairs
):
    cols = pl.ds(pl.multiple_of(pair * 128, 128), 128)
    kt_ref[...] = k.span(s, 0, seq, pair).T
    dk_acc[...] = jnp.zeros(dk_acc.shape, f32)
    dv_acc[...] = jnp.zeros(dv_acc.shape, f32)
    for b in range(seq // BQ):
        lo, hi = span(b, seq)
        at = pl.ds(pl.multiple_of(s * seq + b * BQ, BQ), BQ)
        qb = q.block(s, b, pair)[...] * jnp.asarray(HEAD_DIM**-0.5, bf16)
        kb, vb = k.span(s, lo, hi, pair), v.span(s, lo, hi, pair)
        db = dctx_ref[at, cols]
        prod = (db.astype(f32) * ctx_ref[at, cols].astype(f32)).T
        out = []
        for h in range(2):
            qh, dh = half(qb, h), half(db, h)
            delta = jnp.sum(prod[64 * h : 64 * h + 64], axis=0, keepdims=True)
            lse = lse_ref[s * pairs + pair, h : h + 1, b * BQ : (b + 1) * BQ]
            p = jnp.exp2(nt(kb, qh) * LOG2E - slopes[h] * far.at(lo, hi, b)[...] - lse)
            ds = (p * (nt(vb, dh) - delta)).astype(bf16)
            dv_acc[lo:hi, :] += nn(p.astype(bf16), dh)
            dk_acc[lo:hi, :] += nn(ds, qh)
            out.append(nn(kt_ref[64 * h : 64 * h + 64, lo:hi], ds))
        dq_val = jnp.concatenate(out, axis=0).T * HEAD_DIM**-0.5
        dq.block(s, b, pair)[...] = dq_val.astype(bf16)
    for b in range(seq // BQ):
        dk.block(s, b, pair)[...] = dk_acc[b * BQ : (b + 1) * BQ, :].astype(bf16)
        dv.block(s, b, pair)[...] = dv_acc[b * BQ : (b + 1) * BQ, :].astype(bf16)


AG = (
    (10, 0, 11, 20, 80, 1, 21, 30, 2, 12, 40, 3, 22, 31),
    (81, 50),
    (32, 41),
    (13, 60),
    (51, 42),
    (82, 23),
    (61, 70),
    (52, 62),
    (),
    (33,),
    (53, 83, 71, 43, 63),
    (72,),
    (),
    (73,),
)
RS = (
    (),
    (),
    (1, 11),
    (2, 20),
    (),
    (12,),
    (30,),
    (21, 31),
    (32,),
    (50, 40, 22),
    (51,),
    (41, 52),
    (60, 33),
    (42,),
    (61, 3, 23, 13, 62),
    (63, 43, 53),
)


def layer_kernel(names, seq, pairs, routes, lead, *refs):
    R = types.SimpleNamespace(**dict(zip(names, refs)))
    seg_ref, slope_ref, x_hbm, cot_hbm = R.seg, R.slope, R.x, R.cot
    out_hbm, dx_hbm, keep_hbm = R.out, R.dx, R.keep
    wq, wg, wu, wd, wo5 = R.wq, R.wg, R.wu, R.wd, R.wo5
    wo, sm, vec, dvec, gd = R.wo, R.sm, R.vec, R.dvec, R.gd
    io, s1, q1, s2, q2, n1 = R.io, R.s1, R.q1, R.s2, R.q2, R.n1
    hv, av, bv, ctx, lse, vt = R.hv, R.av, R.bv, R.ctx, R.lse, R.vt
    io_sem, out_sem, dx_sem = R.io_sem, R.out_sem, R.dx_sem
    xs, xr, misc = R.xs, R.xr, R.misc
    rows, model = io.shape
    width, ff = ctx.shape[1], av.shape[3]
    tiles, nb = rows // TM, lead[0] * lead[1] * lead[2]
    each, each_out, each_ff = model // nb, width // nb, ff // nb
    pad_out = wo5.shape[3]
    count = seg_ref.shape[0]
    HC = ff // 2
    at = lambda i: pl.ds(pl.multiple_of(i * TM, TM), TM)
    tile = lambda ref, i: ref.at[lax.div(i, 2), lax.rem(i, 2)]
    load = lambda hbm, i: pltpu.make_async_copy(hbm.at[at(i)], io.at[at(i)], io_sem.at[i])
    emit = lambda i: pltpu.make_async_copy(io.at[at(i)], out_hbm.at[at(i)], out_sem.at[i])
    exch = lambda k, i: swap((s1, s2, s1, s1)[k].at[at(i)], (q1, q2, q1, q1)[k].at[at(i)], xs.at[k, i], xr.at[k, i])
    me = lax.axis_index("dp")
    core = lax.axis_index("tensor")
    head0 = core * (2 * pairs)
    slopes_of = lambda pair: [slope_ref[head0 + 2 * pair + h] for h in range(2)]
    gate_w = lambda ref, c: ref[:, :, :, :, c : c + HC].reshape(model, HC)
    lh = lead[0] // 2

    def down_w(c):
        if routes:
            return wd[c // HC * lh : (c // HC + 1) * lh].reshape(HC, model)
        return wd[0, 0, 0, c : c + HC, :]

    def each_tile(f, lo, hi):
        def body(i, carry):
            f(i)
            return carry

        lax.fori_loop(lo, hi, body, 0)

    each_tile(lambda i: load(x_hbm, i).start(), 0, tiles)

    if routes:
        lanes = n1.shape[1]
        place_of, moves, row = {}, [], 0

        def stage_in(name, src):
            nonlocal row
            r, c = src.shape
            place_of[name] = []
            for a in range(0, c, lanes):
                w = min(lanes, c - a)
                spot_in = n1.at[row : row + r, 0:w]
                cp = pltpu.make_async_copy(src.at[:, a : a + w], spot_in, misc.at[len(moves)])
                cp.start()
                moves.append(cp)
                place_of[name].append(spot_in)
                row += -(-r // 8) * 8

        for j in range(3):
            stage_in(j, R.weight_qkv.at[j])
        for j in range(2):
            stage_in(3 + j, R.weight_gate_up.at[j])
        stage_in(5, R.weight_down)
        stage_in(6, R.weight_out)
        for cp in moves:
            cp.wait()
        fetch = lambda name: jnp.concatenate([p[...] for p in place_of[name]], axis=1)
        for j in range(3):
            mine = fetch(j).astype(bf16)
            for p in range(pairs):
                R.qkv_src[p * each : (p + 1) * each, j * 128 : (j + 1) * 128] = mine[:, p * 128 : (p + 1) * 128]
        R.gate_src[...] = fetch(3).astype(bf16)
        R.up_src[...] = fetch(4).astype(bf16)
        R.down_src[...] = fetch(5).astype(bf16)
        pad = R.out_src.shape[0] - each_out
        R.out_src[...] = jnp.concatenate(
            [fetch(6), jnp.zeros((pad, model), f32)], axis=0
        ).astype(bf16)
        spot = R.spot
        spot[...] = jnp.zeros(spot.shape, f32)
        spot[0:6, 0:each] = R.norm_vectors[...]
        spot[6:8, 0:each_out] = R.head_bias[...]
        R.small_src[...] = spot[...].astype(bf16)
        gs, gr, gl = R.gs, R.gr, R.gl
        flows = []

        def flow(src, dst, cuts, kind=Gather):
            made = []
            for a, b, first in cuts:
                j = len(flows)
                slot = lambda z, y, x, a=a, b=b: dst.at[z, y, x, a:b]
                made.append(kind(src.at[a:b], slot, first, gs.at[j], gr.at[j], gl.at[j]))
                flows.append(made[-1])
            return made

        both = lambda a, m, b: ((a, m, "x"), (m, b, "y"))
        gate_up = lambda a, b: flow(R.gate_src, wg, ((a, b, "x"),)) + flow(R.up_src, wu, ((a, b, "y"),))
        qkv_src, down_src = R.qkv_src, R.down_src
        cut = each // 3
        pieces = [
            flow(qkv_src, wq, both(0, 16, each)) + flow(R.small_src, sm, ((0, 16, "x"),)),
            flow(qkv_src, wq, both(each, 80, 2 * each)),
            flow(qkv_src, wq, both(2 * each, 112, 3 * each)),
            flow(R.out_src, wo5, both(0, 16, pad_out)),
            gate_up(0, cut),
            gate_up(cut, 2 * cut),
            gate_up(2 * cut, each),
            flow(down_src, wd, both(0, 32, 64)),
            flow(down_src, wd, both(64, 80, each_ff), GatherLate),
        ]

        def bring(*steps):
            for step in steps:
                run(pieces[step // 10], step % 10)

        greet(True, True)
        bring(*AG[0])
    else:
        pairs_in = [
            (R.weight_qkv, wq), (R.weight_gate, wg), (R.weight_up, wu),
            (R.weight_down, wd), (R.weight_out, wo5), (R.small, sm),
        ]
        copies = [pltpu.make_async_copy(a, b.at[0, 0, 0], misc.at[2 + j]) for j, (a, b) in enumerate(pairs_in)]
        for cp in copies:
            cp.start()
        greet(False, True)
        for cp in copies:
            cp.wait()
    if routes:
        wide_zero = jnp.zeros((8, model - 128), f32)
        lane = lax.broadcasted_iota(jnp.int32, (8, 128), 1)
        row = lax.broadcasted_iota(jnp.int32, (8, 128), 0)
        width_of = jnp.where(row < 6, each, each_out)
        upper, lower = 0.0, 0.0
        for b in range(nb):
            piece = sm[b // 4, (b // 2) % 2, b % 2].astype(f32)[0:8]
            piece = jnp.concatenate([jnp.where(lane < width_of, piece, 0.0), wide_zero], axis=1)
            upper = upper + pltpu.roll(piece, b * each, 1)
            lower = lower + pltpu.roll(piece, b * each_out, 1)
        vec[0:8, :], vec[8:16, :] = upper, lower
    else:
        vec[0:8, :] = sm[0, 0, 0, 0:16, :].astype(f32)[0:8]
        vec[8:16, :] = vec[0:8, :]
    bo, bd, g1, c1, g2, c2 = (vec[k : k + 1, :] for k in range(6))

    pair_w = lambda p: wq[:, :, :, p * each : (p + 1) * each, :].reshape(model, 3 * 128)
    qkv = [Rows(bv, j * 128, 128) for j in range(3)]
    keep = lambda out: pltpu.make_async_copy(
        *((bv.at[:, :, :, 0 : 3 * width], keep_hbm) if out else (keep_hbm, bv.at[:, :, :, 0 : 3 * width])),
        misc.at[0],
    )
    each_tile(lambda i: load(x_hbm, i).wait(), 0, tiles)
    far = Far(n1, seq)

    def project(p):
        here = slice(p * 128, (p + 1) * 128)
        bias = jnp.concatenate([vec[14:15, here], jnp.zeros((1, 128), f32), vec[15:16, here]], axis=1)

        def tile_of(i):
            Rows(bv, p * 384, 384).tile(i)[...] = (nn(io[at(i), :], pair_w(p)) + bias).astype(bf16)

        each_tile(tile_of, 0, tiles)
        if routes:
            bring(*AG[1 + 3 * p])

    def forward(it):
        pair, turn = lax.div(it, count), lax.rem(it, count)
        s = turn + lax.rem(pair, 2) * (count - 1 - 2 * turn)

        @pl.when((turn > 0) | (pair == 0))
        def _():
            far.fill(seg_ref, s)

        attend(s, pair, *qkv, vt, far, slopes_of(pair), ctx, lse, seq, pairs)
        for p in range(pairs):

            @pl.when(it == p * count + count - 2)
            def _(p=p):
                if routes:
                    bring(*AG[2 + 3 * p])

            @pl.when(it == p * count + count - 1)
            def _(p=p):
                if routes:
                    bring(*AG[3 + 3 * p])
                if p + 1 < pairs:
                    project(p + 1)

    project(0)
    each_tile(forward, 0, count * pairs)
    keep(True).start()
    wo[...] = wo5[:, :, :, :each_out, :].astype(f32).reshape(width, model).astype(bf16)

    def phase_a(i):
        s1[at(i), :] = nn(ctx[at(i), :], wo[...]).astype(bf16)
        exch(0, i).start()

    each_tile(phase_a, 0, tiles)
    keep(True).wait()

    if routes:
        lo_hi = (slice(0, lh), slice(lh, lead[0]))
        stage = [gd.at[part, :, :, 0 : TM * 2 // nb, :] for part in lo_hi]
    else:
        stage = [gd.at[:, :, :, j * TM : (j + 1) * TM, :] for j in range(2)]

    def meet_one(i):
        exch(0, i).wait()

    def norm_one(i, parity):
        attn = s1[at(i), :].astype(f32) + q1[at(i), :].astype(f32) + bo
        c, r = stats(io[at(i), :].astype(f32) + attn)
        n1[at(i), :] = c
        stage[parity][...] = (c * r * g1 + c1).astype(bf16).reshape(stage[parity].shape)

    def geglu(i, parity):
        xb = stage[parity][...].reshape(TM, model)
        for c in range(0, ff, HC):
            gate, up = nn(xb, gate_w(wg, c)), nn(xb, gate_w(wu, c))
            cdf = 0.5 * (1.0 + lax.erf(gate * 0.7071067811865476))
            gel = gate * cdf
            slope = cdf + gate * (jnp.exp(gate * gate * -0.5) * 0.3989422804014327)
            tile(hv, i)[:, c : c + HC] = (gel * up).astype(bf16)
            tile(av, i)[:, c : c + HC] = (up * slope).astype(bf16)
            tile(bv, i)[:, c : c + HC] = gel.astype(bf16)

    def phase_b(j):
        meet_one(2 * j + 1)
        meet_one(2 * j + 2)
        norm_one(2 * j + 1, 1)
        geglu(2 * j, 0)
        norm_one(2 * j + 2, 0)
        geglu(2 * j + 1, 1)
        for i in (2 * j + 1, 2 * j + 2):
            load(cot_hbm, i).start()

    meet_one(0)
    norm_one(0, 0)
    load(cot_hbm, 0).start()
    if routes:
        bring(*AG[10])
    each_tile(phase_b, 0, 1)
    if routes:
        bring(*AG[11])
    each_tile(phase_b, 1, 2)
    if routes:
        bring(*AG[12])
    each_tile(phase_b, 2, tiles // 2 - 1)
    meet_one(tiles - 1)
    norm_one(tiles - 1, 1)
    load(cot_hbm, tiles - 1).start()
    geglu(tiles - 2, 0)
    geglu(tiles - 1, 1)
    if routes:
        bring(*AG[13])

    dvec[...] = jnp.zeros(dvec.shape, f32)

    def meet_two(i):
        exch(1, i).wait()
        load(cot_hbm, i).wait()

    def norm_two(i):
        c = n1[at(i), :]
        x1 = c * spread(c) * g1 + c1
        ffn = s2[at(i), :].astype(f32) + q2[at(i), :].astype(f32) + bd
        h, r2 = stats(x1 + ffn)
        n2 = h * r2
        dy = io[at(i), :].astype(f32)
        io[at(i), :] = (n2 * g2 + c2).astype(bf16)
        dvec[4:5, :] += jnp.sum(dy * n2, axis=0, keepdims=True)
        dvec[5:6, :] += jnp.sum(dy, axis=0, keepdims=True)
        dh2 = norm_back(dy * g2, n2, r2)
        dvec[1:2, :] += jnp.sum(dh2, axis=0, keepdims=True)
        s2[at(i), :] = dh2.astype(bf16)
        q2[at(i), :] = x1.astype(bf16)

    def down(i):
        s2[at(i), :] = nn(tile(hv, i)[...], wd[...].reshape(ff, model)).astype(bf16)

    def phase_down(i):
        down(i)
        exch(1, i).start()

    def phase_norm(i):
        meet_two(i)
        norm_two(i)
        emit(i).start()

    lag = 3

    def phase_c(i):
        meet_two(i - lag)
        norm_two(i - lag)
        down(i)
        emit(i - lag).start()
        exch(1, i).start()

    each_tile(phase_down, 0, lag)
    each_tile(phase_c, lag, tiles)
    each_tile(phase_norm, tiles - lag, tiles)

    quarter = ff // 4

    def grad_down(c):
        cols = pl.ds(pl.multiple_of(c * quarter, 128), quarter)
        val = tn(hv[:, :, :, cols].reshape(rows, quarter), s2[...]).astype(bf16)
        if routes:
            gd[c] = val.reshape(gd.shape[1:])
        else:
            gd[0, 0, 0, pl.ds(pl.multiple_of(c * quarter, 128), quarter), :] = val

    each_tile(grad_down, 0, 4)
    if routes:
        z, y, x = place()
        peers = [chip(lax.rem(z + d, 4), y, x) for d in (1, 2, 3)]
        peers += [chip(z, 1 - y, x), chip(z, y, 1 - x)]
        other = {"tensor": 1 - core}

        def ready(sem, devices):
            for dev in devices:
                pl.semaphore_signal(sem, inc=1, device_id=dev, device_id_type=MESH)
            pl.semaphore_wait(sem, len(devices))

        ss, sr = R.ss, R.sr
        sent = []

        def back_flow(g, r1, r2, r3, out, cuts, lo=0, lanes=None, shift=(0, 0)):
            made = []
            hi = lo + (lanes or out.shape[1])
            down, along = shift
            for a, b, first in cuts:
                j = len(sent)
                made.append(
                    Scatter(
                        lambda z, y, x, a=a, b=b: g.at[z, y, x, a - down : b - down, lo + along : hi + along],
                        r1(a, b), r2(a, b), r3(a, b), out.at[a:b, lo:hi], first, ss.at[j], sr.at[j],
                    )
                )
                sent.append(made[-1])
            return made

        def spare(top, deep, left, right):
            return (
                lambda a, b: hv.at[:, :, top + a : top + b, left[0] : left[1]],
                lambda a, b: hv.at[:, 0, deep + a : deep + b, right[0] : right[1]],
                lambda a, b: hv.at[0:3, 1, deep + a : deep + b, right[0] : right[1]],
            )

        own = lambda r1, r2, r3: (
            lambda a, b: r1.at[:, :, a:b],
            lambda a, b: r2.at[:, a:b],
            lambda a, b: r3.at[:, a:b],
        )
        eff = wd.shape[3]
        downs = back_flow(
            gd,
            lambda a, b: hv.at[:, :, a:b, 0:model],
            lambda a, b: hv.at[:, 0, eff + a : eff + b, 0:model],
            lambda a, b: hv.at[0:3, 1, eff + a : eff + b, 0:model],
            R.g_down,
            both(0, 48, eff),
        )
        def wide(g, j, out, first, lo, top, end):
            lanes = slice(lo, lo + HC)
            return back_flow(
                g,
                lambda a, b: av.at[:, :, j * each + a : j * each + b, lanes],
                lambda a, b: av.at[:, j, 2 * each + a : 2 * each + b, lanes],
                lambda a, b: av.at[0:3, j, 3 * each + a : 3 * each + b, lanes],
                out,
                ((top, end, first),),
                lo,
                HC,
            )

        gates = [
            wide(wg, 0, R.g_gate, "x", lo, 0, each) + wide(wu, 1, R.g_up, "y", lo, 0, each)
            for lo in (0, HC)
        ]
        outs_flow = back_flow(wo5, *spare(2 * eff, 2 * eff + pad_out, (0, model), (0, model)), R.g_out, both(0, 16, pad_out))
        heads_flow = [
            back_flow(
                wd,
                *spare(0, 0, (model, model + width), (model + width, model + 2 * width)),
                R.g_qkv,
                both(p * each, p * each + (32 if p == 1 else 16), (p + 1) * each),
                shift=((p - p % 2) * each, p // 2 * width),
            )
            for p in range(pairs)
        ]
        heads_flow[-1] += back_flow(R.gsm, *own(R.rs1, R.rs2, R.rs3), R.g_small, ((0, 8, "x"),))
        parts = [downs, gates[0], gates[1], outs_flow, *heads_flow]

        def push(*steps):
            for step in steps:
                run(parts[step // 10], step % 10)

        chips = [{"dp": p} for p in peers]

    def ffn_back(c, i):
        df = s2[at(i), :]
        dh = nt(df, down_w(c))
        a, b = tile(av, i), tile(bv, i)
        dg = (dh * a[:, c : c + HC].astype(f32)).astype(bf16)
        du = (dh * b[:, c : c + HC].astype(f32)).astype(bf16)
        a[:, c : c + HC] = dg
        b[:, c : c + HC] = du
        part = nt(dg, gate_w(wg, c)) + nt(du, gate_w(wu, c))
        if c > 0:
            part = part + s1[at(i), :].astype(f32)
        s1[at(i), :] = part.astype(bf16)
        if c + HC == ff:
            exch(2, i).start()

    def meet_back(i):
        exch(2, i).wait()
        emit(i).wait()

    def norm_one_back(i):
        c = n1[at(i), :]
        r = spread(c)
        n = c * r
        dx1 = s2[at(i), :].astype(f32) + (s1[at(i), :].astype(f32) + q1[at(i), :].astype(f32))
        dvec[2:3, :] += jnp.sum(dx1 * n, axis=0, keepdims=True)
        dvec[3:4, :] += jnp.sum(dx1, axis=0, keepdims=True)
        dh1 = norm_back(dx1 * g1, n, r)
        dvec[0:1, :] += jnp.sum(dh1, axis=0, keepdims=True)
        da = dh1.astype(bf16)
        io[at(i), :] = da
        s2[at(i), 0:width] = nt(da, wo[...]).astype(bf16)

    def grad_wide(c):
        cols = pl.ds(pl.multiple_of(c * 256, 256), 256)
        for src, dst in ((av, wg), (bv, wu)):
            val = tn(q2[...], src[:, :, :, cols].reshape(rows, 256)).astype(bf16)
            dst[:, :, :, :, cols] = val.reshape(dst.shape[:4] + (256,))

    per = HC // 256
    if routes:
        ready(R.ready.at[0], chips)
        push(0)
    mid = tiles // 2
    each_tile(lambda i: ffn_back(0, i), 0, tiles)
    if routes:
        push(*RS[0])
    each_tile(grad_wide, 0, per)
    if routes:
        ready(R.ready.at[1], chips)
        push(10, *RS[1])
    each_tile(lambda i: ffn_back(HC, i), 0, tiles)
    if routes:
        push(*RS[2])

    def phase_e(j):
        meet_back(2 * j)
        meet_back(2 * j + 1)
        norm_one_back(2 * j)
        norm_one_back(2 * j + 1)
        grad_wide(per + j)

    each_tile(phase_e, 0, per)

    def phase_last(i):
        meet_back(i)
        norm_one_back(i)

    each_tile(phase_last, 2 * per, tiles)
    keep(False).start()
    reload = pltpu.make_async_copy(x_hbm, q2, misc.at[1])
    reload.start()
    dwo = tn(ctx[...], io[...])
    wo5[:, :, :, :each_out, :] = dwo.reshape(lead + (each_out, model)).astype(bf16)
    if routes:
        ready(R.ready.at[2], chips + [other])
        push(*RS[3])
    else:
        pl.semaphore_signal(R.ready.at[2], inc=1, device_id={"tensor": 1 - core}, device_id_type=MESH)
        pl.semaphore_wait(R.ready.at[2], 1)
        grads_out = [(wg, R.g_gate), (wu, R.g_up), (gd, R.g_down), (wo5, R.g_out)]
        copies = [pltpu.make_async_copy(a.at[0, 0, 0], b, misc.at[2 + j]) for j, (a, b) in enumerate(grads_out)]
        for cp in copies:
            cp.start()
    keep(False).wait()

    d_pairs = [Rows(bv, p * 384, 384) for p in range(pairs)]
    dk_acc, dv_acc = (n1.at[seq : 2 * seq, j : j + 128] for j in (BQ, BQ + 128))
    reload.wait()

    def at_pair(pair, tables, first):
        for p in range(pairs):

            @pl.when(pair == p)
            def _(p=p):
                push(*tables[first + 3 * p])

    def backward(pair):
        def one(turn):
            s = turn + lax.rem(pair, 2) * (count - 1 - 2 * turn)

            @pl.when((turn > 0) | (pair == 0))
            def _():
                far.fill(seg_ref, s)

            attend_back(
                s, pair, *qkv, ctx, s2, lse, far, slopes_of(pair), vt, dk_acc, dv_acc, *qkv, seq, pairs
            )

        each_tile(one, 0, count - 1)
        if routes:
            at_pair(pair, RS, 4)
        each_tile(one, count - 1, count)
        if routes:
            at_pair(pair, RS, 5)
        cols = pl.ds(pl.multiple_of(pair * 384, 128), 384)
        val = tn(q2[...], bv[:, :, :, cols].reshape(rows, 384)).astype(bf16).reshape(lead + (each, 384))
        for p in range(pairs):

            @pl.when(pair == p)
            def _(p=p):
                wd[:, :, :, p % 2 * each : (p % 2 + 1) * each, p // 2 * width : (p // 2 + 1) * width] = val
                if routes and p < pairs - 1:
                    push(*RS[6 + 3 * p])

    each_tile(backward, 0, pairs)

    def add_tile(d, i, total):
        return total + jnp.sum(d.tile(i)[...].astype(f32), axis=0, keepdims=True)

    totals = [
        lax.fori_loop(0, tiles, functools.partial(add_tile, d), jnp.zeros((1, 384), f32)) for d in d_pairs
    ]
    rows_of = [jnp.concatenate([t[:, j : j + 128] for t in totals], axis=1) for j in (0, 256)]
    heads = jnp.concatenate([jnp.zeros((6, width), f32)] + rows_of, axis=0)
    if routes:
        row = lax.broadcasted_iota(jnp.int32, (8, 128), 0)
        for b in range(nb):
            upper = pltpu.roll(dvec[...], (model - b * each) % model, 1)[:, :128]
            lower = pltpu.roll(heads, (width - b * each_out) % width, 1)[:, :128]
            R.gsm[b // 4, (b // 2) % 2, b % 2] = jnp.where(row < 6, upper, lower)
        push(*RS[12])
    else:
        R.g_heads[...] = heads
        R.g_vec[...] = dvec[...]
        for j in range(3):
            src = wd.at[0, 0, 0, j % 2 * each : (j % 2 + 1) * each, j // 2 * width : (j // 2 + 1) * width]
            copies.append(pltpu.make_async_copy(src, R.g_qkv.at[j * each : (j + 1) * each], misc.at[6 + j]))
            copies[-1].start()

    def input_part(i):
        val = sum(nt(d.tile(i)[...], pair_w(p)) for p, d in enumerate(d_pairs))
        s1[at(i), :] = val.astype(bf16)
        exch(3, i).start()

    each_tile(input_part, 0, mid)
    if routes:
        push(*RS[13])
    each_tile(input_part, mid, tiles)
    if routes:
        push(*RS[14])

    def finish(i):
        exch(3, i).wait()
        val = io[at(i), :].astype(f32) + (s1[at(i), :].astype(f32) + q1[at(i), :].astype(f32))
        s1[at(i), :] = val.astype(bf16)
        pltpu.make_async_copy(s1.at[at(i)], dx_hbm.at[at(i)], dx_sem.at[i]).start()

    each_tile(finish, 0, tiles)
    if routes:
        push(*RS[15])
    else:
        for cp in copies:
            cp.wait()
    each_tile(lambda i: pltpu.make_async_copy(s1.at[at(i)], dx_hbm.at[at(i)], dx_sem.at[i]).wait(), 0, tiles)


def layer(x, cot, segments, slopes, weights):
    routes = routed()
    lead = TORUS if routes else (1, 1, 1)
    rows, model = x.shape
    count, seq = segments.shape
    width, ff = weights.qkv.shape[-1], weights.gate_up.shape[-1]
    pairs, tiles = width // 128, rows // TM
    nb = lead[0] * lead[1] * lead[2]
    each, each_out, each_ff = model // nb, width // nb, ff // nb
    pad_out = -(-each_out // 32) * 32
    dma = pltpu.SemaphoreType.DMA
    low = lambda *s: (s, bf16)
    full = lambda *s: (s, f32)
    ins = [("seg", segments, VMEM), ("slope", slopes, SMEM), ("x", x, ANY), ("cot", cot, ANY)]
    outs = [("out", low(rows, model), ANY), ("dx", low(rows, model), ANY)]
    outs += [("keep", low(tiles // 2, 2, TM, 3 * width), ANY)]
    if routes:
        ins += [("weight_qkv", weights.qkv, ANY), ("weight_gate_up", weights.gate_up, ANY)]
        ins += [("weight_down", weights.down, ANY), ("weight_out", weights.out, ANY)]
        ins += [("head_bias", weights.heads, VMEM), ("norm_vectors", weights.vectors, VMEM)]
        outs += [
            ("g_qkv", full(3 * each, width), VMEM),
            ("g_gate", full(each, ff), VMEM),
            ("g_up", full(each, ff), VMEM),
            ("g_down", full(each_ff, model), VMEM),
            ("g_out", full(pad_out, model), VMEM),
            ("g_small", full(8, 128), VMEM),
        ]
    else:
        ins += [("weight_qkv", weights.qkv, ANY)]
        ins += [("weight_gate", weights.gate_up[0], ANY)]
        ins += [("weight_up", weights.gate_up[1], ANY)]
        ins += [("weight_down", weights.down, ANY), ("weight_out", weights.out, ANY)]
        ins += [("small", weights.small, ANY)]
        outs += [
            ("g_qkv", low(3 * model, width), ANY),
            ("g_gate", low(model, ff), ANY),
            ("g_up", low(model, ff), ANY),
            ("g_down", low(ff, model), ANY),
            ("g_out", low(width, model), ANY),
            ("g_heads", full(8, width), VMEM),
            ("g_vec", full(8, model), VMEM),
        ]
    scratch = [
        ("wq", low(*lead, 3 * each, width)),
        ("wg", low(*lead, each, ff)),
        ("wu", low(*lead, each, ff)),
        ("wd", low(*lead, each_ff, model)),
        ("gd", low(*lead, each_ff, model)),
        ("wo5", low(*lead, pad_out, model)),
        ("sm", low(*lead, 16, 128 if routes else model)),
        ("wo", low(width, model)),
        ("vec", full(16, model)),
        ("n1", full(rows, model)),
        ("ctx", low(rows, width)),
        ("lse", full(count * pairs, 8, seq)),
        ("vt", low(128, seq)),
        ("dvec", full(8, model)),
    ]
    scratch += [(n, low(rows, model)) for n in ("io", "s1", "q1", "s2", "q2")]
    scratch += [(n, low(tiles // 2, 2, TM, ff)) for n in ("hv", "av", "bv")]
    sems = [("io_sem", dma((tiles,))), ("out_sem", dma((tiles,))), ("dx_sem", dma((tiles,)))]
    sems += [("xs", dma((4, tiles))), ("xr", dma((4, tiles))), ("misc", dma((12,)))]
    sems += [("ready", pltpu.SemaphoreType.REGULAR((3,)))]
    if routes:
        scratch += [
            ("qkv_src", low(3 * each, width)),
            ("gate_src", low(each, ff)),
            ("up_src", low(each, ff)),
            ("down_src", low(each_ff, model)),
            ("out_src", low(pad_out, model)),
            ("small_src", low(16, 128)),
            ("spot", full(16, 128)),
            ("gsm", full(*lead, 8, 128)),
        ]
        for name, shape in (("rs", full(8, 128)),):
            for j, front in enumerate(((4, 2), (4,), (3,))):
                scratch.append((name + str(j + 1), (front + shape[0], shape[1])))
        sems += [("gs", dma((20, 5))), ("gr", dma((20, 5))), ("gl", dma((20,)))]
        sems += [("ss", dma((24, 5))), ("sr", dma((24, 5)))]
    names = [n for group in (ins, outs, scratch, sems) for n, *_ in group]
    got = pl.pallas_call(
        functools.partial(layer_kernel, names, seq, pairs, routes, lead),
        out_shape=[jax.ShapeDtypeStruct(*s) for _, s, _ in outs],
        in_specs=[space for _, _, space in ins],
        out_specs=[space for _, _, space in outs],
        scratch_shapes=[pltpu.VMEM(*s) for _, s in scratch] + [s for _, s in sems],
        compiler_params=pltpu.CompilerParams(
            vmem_limit_bytes=64 << 20, collective_id=0, has_side_effects=True
        ),
        name="layer",
    )(*[a for _, a, _ in ins])
    return types.SimpleNamespace(**{n: a for (n, *_), a in zip(outs, got)})


def adam_update(weight_old, first_old, second_old, gradient, step_rate):
    first_new = beta_first * first_old + (1.0 - beta_first) * gradient
    second_new = beta_second * second_old + (1.0 - beta_second) * gradient * gradient
    first_hat = first_new / (1.0 - beta_first**STEP)
    second_hat = second_new / (1.0 - beta_second**STEP)
    weight_new = weight_old - step_rate * (
        first_hat / (jnp.sqrt(second_hat) + adam_epsilon) + decay_rate * weight_old
    )
    return (second_new, weight_new)


def update_kernel(*refs):
    out_in, dx_in, qkv, out, gate, up, down, small = refs[:8]
    olds = [refs[8 + 3 * j : 11 + 3 * j] for j in range(6)]
    out_ref, dx_ref = refs[26:28]
    news = [refs[28 + 3 * j : 31 + 3 * j] for j in range(6)]
    hold, sem = refs[46:]
    ends = ((out_in, out_ref), (dx_in, dx_ref))
    come = [pltpu.make_async_copy(a, hold.at[j], sem.at[0, j]) for j, (a, _) in enumerate(ends)]
    leave = [pltpu.make_async_copy(hold.at[j], b, sem.at[1, j]) for j, (_, b) in enumerate(ends)]
    for cp in come:
        cp.start()

    def write(j, at, grad):
        weight, first, second = (r[at] for r in olds[j])
        rate = matrix_rate if j < 4 else vector_rate
        second_new, weight_new = adam_update(weight, first, second, grad, rate)
        for ref, val in zip(news[j], (grad, second_new, weight_new)):
            ref[at] = val

    for cp, onward in zip(come, leave):
        cp.wait()
        onward.start()
    rows = olds[0][0].shape[1]
    for j in range(3):
        cols = slice(j * 128, (j + 1) * 128)
        mine = [qkv[p * rows : (p + 1) * rows, cols] for p in range(qkv.shape[0] // rows)]
        write(0, j, jnp.concatenate(mine, axis=1))
    whole = (slice(None), slice(None))
    write(1, whole, out[: olds[1][0].shape[0], :])
    write(2, 0, gate[...])
    write(2, 1, up[...])
    write(3, whole, down[...])
    write(4, whole, small[6:8, : olds[4][0].shape[1]])
    write(5, whole, small[0:6, : olds[5][0].shape[1]])
    for cp in leave:
        cp.wait()


def update(layer_out, input_grad, sums, olds):
    flat = [a for group in olds for a in group]
    shape = lambda a: jax.ShapeDtypeStruct(a.shape, a.dtype)
    return pl.pallas_call(
        update_kernel,
        out_shape=[shape(layer_out), shape(input_grad)] + [shape(a) for a in flat],
        in_specs=[ANY] * 2 + [VMEM] * (len(sums) + len(flat)),
        out_specs=[ANY] * 2 + [VMEM] * len(flat),
        scratch_shapes=[
            pltpu.VMEM((2,) + layer_out.shape, layer_out.dtype),
            pltpu.SemaphoreType.DMA((2, 2)),
        ],
        compiler_params=pltpu.CompilerParams(vmem_limit_bytes=64 << 20),
        name="update",
    )(layer_out, input_grad, *sums, *flat)


def shards(
    inputs,
    segments,
    cotangent,
    weight_qkv,
    first_qkv,
    second_qkv,
    weight_out,
    first_out,
    second_out,
    weight_gate_up,
    first_gate_up,
    second_gate_up,
    weight_down,
    first_down,
    second_down,
    head_bias,
    first_head_bias,
    second_head_bias,
    norm_vectors,
    first_norm_vectors,
    second_norm_vectors,
):
    slopes = jnp.asarray(alibi_slopes(HEADS) * np.float32(LOG2E))
    model, width = weight_out.shape[1], weight_qkv.shape[2]
    space = types.SimpleNamespace
    olds = [
        (weight_qkv, first_qkv, second_qkv),
        (weight_out, first_out, second_out),
        (weight_gate_up, first_gate_up, second_gate_up),
        (weight_down, first_down, second_down),
        (head_bias, first_head_bias, second_head_bias),
        (norm_vectors, first_norm_vectors, second_norm_vectors),
    ]
    if routed():
        shares = space(
            qkv=weight_qkv, gate_up=weight_gate_up, down=weight_down, out=weight_out,
            heads=head_bias, vectors=norm_vectors,
        )
        got = layer(inputs, cotangent, segments, slopes, shares)
        sums = [got.g_qkv, got.g_out, got.g_gate, got.g_up, got.g_down, got.g_small]
    else:
        whole = lambda v, axis: lax.all_gather(v.astype(bf16), "dp", axis=axis, tiled=True)
        small = jnp.zeros((16, model), bf16)
        small = small.at[:6].set(whole(norm_vectors, 1)).at[6:8, :width].set(whole(head_bias, 1))
        packed = whole(weight_qkv, 1).reshape(3, model, -1, 128).transpose(2, 1, 0, 3).reshape(-1, width)
        shares = space(
            qkv=packed, gate_up=whole(weight_gate_up, 1), down=whole(weight_down, 0),
            out=whole(weight_out, 0), small=small,
        )
        got = layer(inputs, cotangent, segments, slopes, shares)
        owned = lambda v, axis: lax.psum_scatter(
            v.astype(f32), "dp", scatter_dimension=axis, tiled=True
        )
        heads, vectors = owned(got.g_heads[6:8], 1), owned(got.g_vec[:6], 1)
        small = jnp.zeros((8, 128), f32)
        small = lax.dynamic_update_slice(small, vectors, (0, 0))
        small = lax.dynamic_update_slice(small, heads, (6, 0))
        sums = [
            owned(got.g_qkv.reshape(-1, model, width), 1).reshape(-1, width),
            owned(got.g_out, 0),
            owned(got.g_gate, 0),
            owned(got.g_up, 0),
            owned(got.g_down, 0),
            small,
        ]
    return tuple(update(got.out, got.dx, sums, olds))


def solution(mesh):
    rows, both, cols = P("dp", None), P(("tensor", "dp"), None), P(None, "dp", "tensor")
    heads, vectors = P(None, ("tensor", "dp")), P(None, "dp")
    params = [s for s in (cols, both, cols, both, heads, vectors) for _ in range(3)]
    return jax.shard_map(
        shards,
        mesh=mesh,
        in_specs=(rows, rows, rows, *params),
        out_specs=(rows, rows, *params),
        check_vma=False,
    )
```
